128 devices in a mesh: fib: 16 (over y, x), row: 4 (over z), slab: 2 (over core).
Axes of the slice: x: 4, y: 4, z: 4, core: 2. Of those that a mesh axis runs over, the one named last changes fastest.
Arguments:
- tensor: float32 [512, 128, 64, 128], P('fib', 'row', 'slab'), may hold values from -300 to 300
- factor_one: float32 [512, 64], replicated, may hold values from -0.25 to 0.25
- factor_two: float32 [128, 64], P('row'), may hold values from -50 to 50
- factor_three: float32 [64, 64], P('slab'), may hold values from -50 to 50
- factor_four: float32 [128, 64], replicated, may hold values from -0.5 to 0.5
Outputs:
- updated_factor: float32 [512, 64], replicated
- core_tensor: float32 [64, 64, 64, 64], P(None, ('row', 'slab'), 'fib')
The draws below stay inside these ranges and needn't reach their ends.
All inputs are finite; a program needn't handle non-finite values.
Results may differ from the reference program's by a relative error of at most 0.00015.
Values sent between devices are 32-bit elements; how exact they have to be, the bound alone decides.
A program may use at most 256 MiB of HBM per device.

```python
import math
import jax
import jax.numpy as jnp
from jax import lax

R = 64
B1 = 32
I4 = 128
I1 = 512
I2 = 128
I3 = 64
N_FIB = 16


def rising_factor(key, length, columns, steep):
    noise = jnp.clip(jax.random.normal(key, (length, columns), jnp.float32), -4.0, 4.0)
    position = jnp.arange(columns, dtype=jnp.float32) / (columns - 1)
    wobble = jnp.exp(jax.random.uniform(jax.random.fold_in(key, 1), (columns,), jnp.float32, -0.3, 0.3))
    return noise * (steep ** position * wobble)[None, :] / math.sqrt(length)


def draw_factor_two(key, part):
    key = jax.random.fold_in(key, 2)
    steep = 3.0
    return rising_factor(key, I2, R, steep)


def draw_factor_three(key, part):
    key = jax.random.fold_in(key, 3)
    steep = 3.0
    return rising_factor(key, I3, R, steep)


def draw_tensor(key, part):
    key = jax.random.fold_in(key, 5)
    keys = jax.random.split(key, 4)
    shape = (I1, I2, I3, I4)
    rough = jnp.clip(jax.random.normal(keys[0], shape, jnp.float32), -4.0, 4.0)
    mixing = 0.3
    widest = 3.0
    common = jnp.clip(jax.random.normal(keys[1], (3, I2, I3, I4), jnp.float32), -4.0, 4.0)
    loadings = jax.random.uniform(keys[2], (I1, 3), jnp.float32, -1.0, 1.0)
    scales = jnp.exp(jax.random.uniform(keys[3], (I1,), jnp.float32, 0.0, math.log(widest)))
    shared = loadings[:, 0, None, None, None] * common[0][None]
    shared = shared + loadings[:, 1, None, None, None] * common[1][None]
    shared = shared + loadings[:, 2, None, None, None] * common[2][None]
    return scales[:, None, None, None] * (rough + mixing * shared)


def bell_draw(own_key, extent, width, bound, kind=jnp.bfloat16):
    values = width * jax.random.normal(own_key, extent, jnp.float32)
    return jnp.clip(values, min=-bound, max=bound).astype(kind)


def setup_inputs(seed: int = 0) -> dict:
    splits = jax.random.split(jax.random.key(seed), 6)
    tensor = draw_tensor(jax.random.fold_in(splits[5], 71), 0)
    factor_one = bell_draw(splits[1], (I1, R), I1 ** -0.5, 0.25, jnp.float32)
    factor_two = draw_factor_two(jax.random.fold_in(splits[5], 71), 0)
    factor_three = draw_factor_three(jax.random.fold_in(splits[5], 71), 0)
    factor_four = bell_draw(splits[4], (I4, R), I4 ** -0.5, 0.5, jnp.float32)
    return {"tensor": tensor, "factor_one": factor_one, "factor_two": factor_two, "factor_three": factor_three, "factor_four": factor_four}


def contract_block(block, factor_two, factor_three, factor_four):
    highest = lax.Precision.HIGHEST
    partial_four = jnp.einsum('ijkl,lr->ijkr', block, factor_four, precision=highest)
    partial_two = jnp.einsum('ijkr,jq->iqkr', partial_four, factor_two, precision=highest)
    return jnp.einsum('iqkr,kp->iqpr', partial_two, factor_three, precision=highest)

def orthonormal(target):
    highest = lax.Precision.HIGHEST
    result = target
    for repeat in range(2):
        crossed = jnp.dot(result.T, result, precision=highest)
        cholesky_factor = jnp.linalg.cholesky(crossed)
        result = jax.scipy.linalg.solve_triangular(cholesky_factor, result.T, lower=True).T
    return result

def reference(tensor, factor_one, factor_two, factor_three, factor_four):
    highest = lax.Precision.HIGHEST
    blocks = tensor.reshape(N_FIB, B1, I2, I3, I4)
    projected = lax.map(lambda piece: contract_block(piece, factor_two, factor_three, factor_four), blocks)
    unfolded = projected.reshape(I1, R * R * R)
    gram = jnp.dot(unfolded, unfolded.T, precision=highest)
    target = jnp.dot(gram, factor_one, precision=highest)
    updated = orthonormal(target)
    core = jnp.dot(updated.T, unfolded, precision=highest).reshape(R, R, R, R)
    return (updated, core)
```

```python
import jax
import jax.numpy as jnp
from jax import lax
from jax.sharding import PartitionSpec as P

HIGH = lax.Precision.HIGH
HIGHEST = lax.Precision.HIGHEST


def orthonormal(target):
    result = target
    for repeat in range(2):
        crossed = jnp.dot(result.T, result, precision=HIGHEST)
        cholesky_factor = jnp.linalg.cholesky(crossed)
        result = jax.scipy.linalg.solve_triangular(cholesky_factor, result.T, lower=True).T
    return result


def body(tensor, factor_one, factor_two, factor_three, factor_four):
    two = lax.all_gather(factor_two, "row")
    three = lax.all_gather(factor_three, "slab")
    reduced = jnp.einsum("ijkl,lr->rijk", tensor, factor_four, precision=HIGH)
    exchanged = lax.all_to_all(reduced, ("row", "slab"), split_axis=0, concat_axis=0, tiled=True)
    exchanged = exchanged.reshape(4, 2, 8, 32, 32, 32)
    halfway = jnp.einsum("abrijk,ajq->brikq", exchanged, two, precision=HIGH)
    projected = jnp.einsum("brikq,bkp->priq", halfway, three, precision=HIGH)
    fibers = lax.all_to_all(projected, "fib", split_axis=0, concat_axis=0, tiled=True)
    fibers = fibers.reshape(16, 4, 8, 32, 64)
    one = factor_one.reshape(16, 32, 64)
    crossed = jnp.einsum("fpriq,fia->apqr", fibers, one, precision=HIGH)
    partial = jnp.einsum("fpriq,apqr->fia", fibers, crossed, precision=HIGH)
    target = lax.psum(partial.reshape(512, 64), ("fib", "row", "slab"))
    updated = orthonormal(target)
    core = jnp.einsum("fpriq,fia->aqpr", fibers, updated.reshape(16, 32, 64), precision=HIGH)
    core = lax.all_to_all(core, ("row", "slab"), split_axis=1, concat_axis=3, tiled=True)
    return (updated, core)


def solution(mesh):
    in_specs = (P("fib", "row", "slab", None), P(), P("row", None), P("slab", None), P())
    out_specs = (P(), P(None, ("row", "slab"), "fib", None))
    return jax.shard_map(body, mesh=mesh, in_specs=in_specs, out_specs=out_specs, check_vma=False)
```

```python
import jax
import jax.numpy as jnp
from jax import lax
from jax.experimental import pallas as pl
from jax.experimental.pallas import tpu as pltpu
from jax.sharding import PartitionSpec as P

HIGHEST = lax.Precision.HIGHEST
MESH = pl.DeviceIdType.MESH
F32 = jnp.float32
BF16 = jnp.bfloat16
CHUNKS = 8
LAG = 2


def split(x):
    high = x.astype(BF16)
    return high, (x - high.astype(F32)).astype(BF16)


def dot(a, b):
    return jnp.dot(a, b, preferred_element_type=F32)


def dot_nt(a, b):
    return lax.dot_general(a, b, (((1,), (1,)), ((), ())), preferred_element_type=F32)


def place():
    return lax.axis_index("fib"), lax.axis_index("row"), lax.axis_index("slab")


def plane_peer(d):
    fib, row, slab = place()
    row, slab = lax.rem(row + d // 2, 4), lax.rem(slab + d % 2, 2)
    return (fib, row, slab), row * 2 + slab


def fib_peer(d):
    fib, row, slab = place()
    fib = lax.rem(fib // 4 + d // 4, 4) * 4 + lax.rem(fib % 4 + d % 4, 4)
    return (fib, row, slab), fib


def each(lower, upper, step):
    def run(index, carry):
        step(index)
        return carry

    lax.fori_loop(lower, upper, run, 0)


def remote(src, dst, send, recv, device):
    return pltpu.make_async_remote_copy(
        src_ref=src, dst_ref=dst, send_sem=send, recv_sem=recv, device_id=device, device_id_type=MESH
    )


def greet(plane, fibers):
    barrier = pltpu.get_barrier_semaphore()
    count = 0
    if plane:
        count += 7
        each(1, 8, lambda d: pl.semaphore_signal(barrier, inc=1, device_id=plane_peer(d)[0], device_id_type=MESH))
    if fibers:
        count += 15
        each(1, 16, lambda d: pl.semaphore_signal(barrier, inc=1, device_id=fib_peer(d)[0], device_id_type=MESH))
    pl.semaphore_wait(barrier, count)


def stack(x):
    high, low = split(x)
    return jnp.concatenate([jnp.concatenate([high, high], 1), jnp.concatenate([low, low], 1)], 0)


def left_half(shape):
    return lax.broadcasted_iota(jnp.int32, shape, 1) < 64


def rows_of(fibers, column):
    return jnp.concatenate([fibers[half, pl.ds(column, 128, stride=32), :] for half in range(2)], axis=1)


def fold(out):
    left = left_half((64, 128))
    folded = jnp.where(left, out[0:64, 0:128], out[64:128, 0:128])
    folded = folded + jnp.where(left, out[128:192, 128:256], out[192:256, 128:256])
    return folded + pltpu.roll(folded, 64, 1)


def project_kernel(
    tensor, four, three, two, one, target, fibers_out, four_stack, one_stack,
    staged, outgoing, incoming, halfway, contracted, fibers, two_all, three_all, wide_high, wide_low,
    crossed, partial, scattered, shared, reduced,
    load_sem, own_sem, z_send, z_recv, fib_own_sem, f_send, f_recv,
    two_send, two_recv, three_send, three_recv, small_own, rs_send, rs_recv, ar_send, ar_recv, ag_send, ag_recv, out_sem,
):
    fib, row, slab = place()
    me = row * 2 + slab

    def load(chunk):
        return pltpu.make_async_copy(tensor.at[chunk], staged.at[chunk % 3], load_sem.at[chunk % 3])

    load(0).start()
    load(1).start()
    four_stack[...] = stack(four[...])
    one_stack[...] = stack(one[...])
    greet(True, True)

    def two_copy(step, block):
        peer = lax.rem(row + step, 4)
        return remote(two, two_all.at[block], two_send.at[step], two_recv.at[block], (fib, peer, slab))

    def three_copy():
        return remote(three, three_all.at[slab], three_send, three_recv, (fib, row, 1 - slab))

    two_own = pltpu.make_async_copy(two, two_all.at[row], small_own.at[0])
    three_own = pltpu.make_async_copy(three, three_all.at[slab], small_own.at[1])
    each(1, 4, lambda s: two_copy(s, row).start())
    three_copy().start()
    two_own.start()
    three_own.start()

    def z_copy(chunk, d):
        device, peer = plane_peer(d)
        return remote(
            outgoing.at[chunk, pl.ds(peer * 256, 256), :],
            incoming.at[chunk, pl.ds(me * 256, 256), :],
            z_send.at[chunk, d], z_recv.at[chunk, me], device,
        )

    def z_arrived(chunk, d):
        device, peer = plane_peer(d)
        block = incoming.at[chunk, pl.ds(peer * 256, 256), :]
        remote(block, block, z_send.at[chunk, d], z_recv.at[chunk, peer], device).wait_recv()

    def z_own(chunk):
        rows = pl.ds(me * 256, 256)
        return pltpu.make_async_copy(outgoing.at[chunk, rows, :], incoming.at[chunk, rows, :], own_sem.at[chunk])

    def f_copy(chunk, d):
        device, peer = fib_peer(d)
        return remote(
            contracted.at[chunk, :, pl.ds(peer * 32, 32), :],
            fibers.at[:, pl.ds((fib * CHUNKS + chunk) * 32, 32), :],
            f_send.at[chunk, d], f_recv.at[chunk, fib], device,
        )

    def f_arrived(chunk, d):
        device, peer = fib_peer(d)
        block = fibers.at[:, pl.ds((peer * CHUNKS + chunk) * 32, 32), :]
        remote(block, block, f_send.at[chunk, d], f_recv.at[chunk, peer], device).wait_recv()

    def f_own(chunk):
        return pltpu.make_async_copy(
            contracted.at[chunk, :, pl.ds(fib * 32, 32), :],
            fibers.at[:, pl.ds((fib * CHUNKS + chunk) * 32, 32), :],
            fib_own_sem.at[chunk],
        )

    def mode_four(chunk):
        slot = chunk % 3

        def two_steps(pair):
            first = staged[slot, pl.ds(2 * pair, 128, stride=32), :]
            second = staged[slot, pl.ds(2 * pair + 1, 128, stride=32), :]
            high, low = split(jnp.concatenate([first, second], axis=0))
            out = dot_nt(four_stack[...], jnp.concatenate([high, low], axis=1))
            out = out[:64] + out[64:]
            outgoing[chunk, pl.ds(2 * pair, 64, stride=32), :] = out[:, :128]
            outgoing[chunk, pl.ds(2 * pair + 1, 64, stride=32), :] = out[:, 128:]

        each(0, 16, two_steps)

    def modes_three_two(chunk):
        whole = three_all[0] + three_all[1]
        high, low = split(whole)
        lanes = lax.broadcasted_iota(jnp.int32, (64, 256), 1)
        factor = jnp.where(lanes < 128, high.astype(F32), low.astype(F32)).astype(BF16)

        def rank(r):
            parts = []
            for z in range(4):
                pieces = [incoming[chunk, pl.ds((2 * z + c) * 256 + r * 32, 32), :] for c in range(2)]
                high, low = split(jnp.concatenate(pieces, axis=0))
                parts.append(jnp.concatenate([high, low, high, low], axis=0))
            out = dot(factor, jnp.concatenate(parts, axis=1))
            for z in range(4):
                halfway[z, pl.ds(r, 64, stride=8), :] = out[:, z * 128 : (z + 1) * 128]

        each(0, 8, rank)

        def rows(block):
            at = pl.ds(pl.multiple_of(block * 128, 128), 128)
            total = jnp.zeros((128, 256), F32)
            for z in range(4):
                high, low = split(halfway[z, at, :])
                both = dot(jnp.concatenate([high, low], axis=0), wide_high[z])
                total = total + both[:128] + both[128:] + dot(high, wide_low[z])
            contracted[chunk, 0, at, :] = total[:, :128]
            contracted[chunk, 1, at, :] = total[:, 128:]

        each(0, 4, rows)

    def widen():
        two_own.wait()
        three_own.wait()
        each(1, 4, lambda s: two_copy(s, lax.rem(row + 4 - s, 4)).wait_recv())
        remote(three, three_all.at[1 - slab], three_send, three_recv, (fib, row, 1 - slab)).wait_recv()
        left = left_half((32, 128))
        nothing = jnp.zeros((32, 128), F32)
        for z in range(4):
            block = two_all[z]
            sides = (jnp.where(left, block, 0.0), jnp.where(left, 0.0, block))
            pieces = []
            for i in range(4):
                tiles = [nothing, nothing]
                tiles[i // 2] = sides[i % 2]
                pieces.append(jnp.concatenate(tiles, axis=1))
            high, low = split(jnp.concatenate(pieces, axis=0))
            wide_high[z] = high
            wide_low[z] = low

    def advance(turn):
        @pl.when(turn < CHUNKS)
        def _():
            load(turn).wait()

            @pl.when(turn + 2 < CHUNKS)
            def _():
                load(turn + 2).start()

            mode_four(turn)

            @pl.when(turn >= 2)
            def _():
                each(1, 8, lambda d: z_copy(turn - 2, d).wait_send())

            each(1, 8, lambda d: z_copy(turn, d).start())
            z_own(turn).start()

        @pl.when(turn == 0)
        def _():
            widen()

        @pl.when(turn >= LAG)
        def _():
            chunk = turn - LAG
            z_own(chunk).wait()
            each(1, 8, lambda d: z_arrived(chunk, d))
            modes_three_two(chunk)
            each(1, 16, lambda d: f_copy(chunk, d).start())
            f_own(chunk).start()

    each(0, CHUNKS + LAG, advance)
    each(CHUNKS - 2, CHUNKS, lambda chunk: each(1, 8, lambda d: z_copy(chunk, d).wait_send()))

    def gathered(chunk):
        f_own(chunk).wait()
        each(1, 16, lambda d: f_arrived(chunk, d))

    each(0, CHUNKS, gathered)
    out_copy = pltpu.make_async_copy(fibers, fibers_out, out_sem)
    out_copy.start()

    def cross(column):
        high, low = split(rows_of(fibers, column))
        out = dot(one_stack[...], jnp.concatenate([high, low], axis=0))
        crossed[column] = fold(out[:256] + out[256:])

    each(0, 32, cross)

    partial[...] = jnp.zeros_like(partial)

    def back(column):
        high, low = split(rows_of(fibers, column))
        left = left_half((64, 128))
        block = crossed[column]
        nothing = jnp.zeros((64, 128), F32)
        sides = (jnp.where(left, block, 0.0), jnp.where(left, 0.0, block))
        wide = jnp.concatenate(
            [
                jnp.concatenate([sides[0], nothing], axis=1),
                jnp.concatenate([sides[1], nothing], axis=1),
                jnp.concatenate([nothing, sides[0]], axis=1),
                jnp.concatenate([nothing, sides[1]], axis=1),
            ],
            axis=0,
        )
        wide_h, wide_l = split(wide)
        both = dot_nt(jnp.concatenate([high, low], axis=0), wide_h)
        partial[...] += both[:128] + both[128:] + dot_nt(high, wide_l)

    each(0, 32, back)

    def rs_copy(d):
        device, peer = plane_peer(d)
        return remote(partial.at[pl.ds(peer * 16, 16), :], scattered.at[me], rs_send.at[d], rs_recv.at[me], device)

    def rs_arrived(d):
        device, peer = plane_peer(d)
        remote(scattered.at[peer], scattered.at[peer], rs_send.at[d], rs_recv.at[peer], device).wait_recv()

    def ar_copy(d):
        device, peer = fib_peer(d)
        return remote(shared.at[fib], shared.at[fib], ar_send.at[d], ar_recv.at[fib], device)

    def ar_arrived(d):
        device, peer = fib_peer(d)
        remote(shared.at[peer], shared.at[peer], ar_send.at[d], ar_recv.at[peer], device).wait_recv()

    def ag_copy(d):
        device, peer = plane_peer(d)
        mine = reduced.at[pl.ds(me * 16, 16), :]
        return remote(mine, mine, ag_send.at[d], ag_recv.at[me], device)

    def ag_arrived(d):
        device, peer = plane_peer(d)
        block = reduced.at[pl.ds(peer * 16, 16), :]
        remote(block, block, ag_send.at[d], ag_recv.at[peer], device).wait_recv()

    each(1, 8, lambda d: rs_copy(d).start())
    scattered[me] = partial[pl.ds(pl.multiple_of(me * 16, 16), 16), :]
    each(1, 8, rs_arrived)
    shared[fib] = jnp.sum(scattered[...], axis=0)
    each(1, 16, lambda d: ar_copy(d).start())
    each(1, 16, ar_arrived)
    reduced[pl.ds(pl.multiple_of(me * 16, 16), 16), :] = jnp.sum(shared[...], axis=0)
    each(1, 8, lambda d: ag_copy(d).start())
    each(1, 8, ag_arrived)
    target[...] = reduced[...]

    each(1, 8, lambda d: rs_copy(d).wait_send())
    each(1, 16, lambda d: ar_copy(d).wait_send())
    each(1, 8, lambda d: ag_copy(d).wait_send())
    each(1, 4, lambda s: two_copy(s, row).wait_send())
    three_copy().wait_send()
    each(0, CHUNKS, lambda chunk: each(1, 16, lambda d: f_copy(chunk, d).wait_send()))
    out_copy.wait()


def core_kernel(updated, fibers, gathered, stacked, outgoing, incoming, send, recv):
    fib, row, slab = place()
    me = row * 2 + slab
    stacked[...] = stack(updated[...])
    greet(True, False)

    def project(group):
        folded = []
        for s in range(4):
            high, low = split(rows_of(fibers, group * 4 + s))
            out = dot(stacked[...], jnp.concatenate([high, low], axis=0))
            folded.append(fold(out[:256] + out[256:]))
        left = left_half((64, 128))
        square = jnp.concatenate(
            [jnp.where(left, folded[0], folded[1]), jnp.where(left, folded[2], folded[3])], axis=0
        )
        turned = square.T
        for half in range(2):
            for peer in range(8):
                start = half * 64 + peer * 8
                at = pl.ds(pl.multiple_of(group * 16 + half * 8, 8), 8)
                outgoing[peer, at, :] = turned[start : start + 8, :]

    each(0, 8, project)

    def copy(d):
        device, peer = plane_peer(d)
        return remote(outgoing.at[peer], incoming.at[me], send.at[d], recv.at[me], device)

    def arrived(d):
        device, peer = plane_peer(d)
        remote(incoming.at[peer], incoming.at[peer], send.at[d], recv.at[peer], device).wait_recv()

    each(1, 8, lambda d: copy(d).start())
    incoming[me] = outgoing[me]
    each(1, 8, arrived)
    gathered[...] = incoming[...]
    each(1, 8, lambda d: copy(d).wait_send())


def turned(matrix):
    return matrix.reshape(128, 4, 64).transpose(1, 2, 0).reshape(256, 128)


def orthonormal(target):
    result = target
    for repeat in range(2):
        crossed = jnp.dot(result.T, result, precision=HIGHEST)
        cholesky_factor = jnp.linalg.cholesky(crossed)
        result = jax.scipy.linalg.solve_triangular(cholesky_factor, result.T, lower=True).T
    return result


def body(tensor, factor_one, factor_two, factor_three, factor_four):
    slab = lax.axis_index("slab")
    across = factor_three.T
    nothing = jnp.zeros_like(across)
    three = jnp.where(slab == 0, jnp.concatenate([across, nothing], 1), jnp.concatenate([nothing, across], 1))
    three = jnp.concatenate([three] * 4, 1)
    two = jnp.concatenate([factor_two, factor_two], 1)
    vmem = pl.BlockSpec(memory_space=pltpu.VMEM)
    hbm = pl.BlockSpec(memory_space=pl.ANY)
    dma = pltpu.SemaphoreType.DMA
    target, fibers = pl.pallas_call(
        project_kernel,
        out_shape=(jax.ShapeDtypeStruct((128, 256), F32), jax.ShapeDtypeStruct((2, 4096, 128), F32)),
        in_specs=[hbm, vmem, vmem, vmem, vmem],
        out_specs=(vmem, hbm),
        scratch_shapes=[
            pltpu.VMEM((128, 256), BF16),
            pltpu.VMEM((512, 256), BF16),
            pltpu.VMEM((3, 4096, 128), F32),
            pltpu.VMEM((CHUNKS, 2048, 128), F32),
            pltpu.VMEM((CHUNKS, 2048, 128), F32),
            pltpu.VMEM((4, 512, 128), F32),
            pltpu.VMEM((CHUNKS, 2, 512, 128), F32),
            pltpu.VMEM((2, 4096, 128), F32),
            pltpu.VMEM((4, 32, 128), F32),
            pltpu.VMEM((2, 64, 256), F32),
            pltpu.VMEM((4, 128, 256), BF16),
            pltpu.VMEM((4, 128, 256), BF16),
            pltpu.VMEM((32, 64, 128), F32),
            pltpu.VMEM((128, 256), F32),
            pltpu.VMEM((8, 16, 256), F32),
            pltpu.VMEM((16, 16, 256), F32),
            pltpu.VMEM((128, 256), F32),
            dma((3,)), dma((CHUNKS,)), dma((CHUNKS, 8)), dma((CHUNKS, 8)), dma((CHUNKS,)), dma((CHUNKS, 16)), dma((CHUNKS, 16)),
            dma((4,)), dma((4,)), dma(()), dma(()), dma((2,)), dma((8,)), dma((8,)), dma((16,)), dma((16,)), dma((8,)), dma((8,)), dma(()),
        ],
        compiler_params=pltpu.CompilerParams(collective_id=0, has_side_effects=True, vmem_limit_bytes=52 * 2**20),
        name="project",
    )(tensor.reshape(8, 4096, 128), factor_four.T, three, two, turned(factor_one))
    updated = orthonormal(target.reshape(512, 64))
    core = pl.pallas_call(
        core_kernel,
        out_shape=jax.ShapeDtypeStruct((8, 128, 128), F32),
        in_specs=[vmem, vmem],
        out_specs=vmem,
        scratch_shapes=[pltpu.VMEM((512, 256), BF16), pltpu.VMEM((8, 128, 128), F32), pltpu.VMEM((8, 128, 128), F32), dma((8,)), dma((8,))],
        compiler_params=pltpu.CompilerParams(collective_id=1, has_side_effects=True, vmem_limit_bytes=32 * 2**20),
        name="core",
    )(turned(updated), fibers)
    core = core.reshape(8, 4, 2, 2, 8, 2, 64).transpose(6, 4, 1, 0, 2, 5, 3).reshape(64, 8, 4, 64)
    return (updated, core)


def solution(mesh):
    in_specs = (P("fib", "row", "slab", None), P(), P("row", None), P("slab", None), P())
    out_specs = (P(), P(None, ("row", "slab"), "fib", None))
    return jax.shard_map(body, mesh=mesh, in_specs=in_specs, out_specs=out_specs, check_vma=False)
```

```python
import jax
import jax.numpy as jnp
from jax import lax
from jax.experimental import pallas as pl
from jax.experimental.pallas import tpu as pltpu
from jax.sharding import PartitionSpec as P

HIGHEST = lax.Precision.HIGHEST
MESH = pl.DeviceIdType.MESH
F32 = jnp.float32
BF16 = jnp.bfloat16
CHUNKS = 8
LAG = 2


def split(x):
    high = x.astype(BF16)
    return high, (x - high.astype(F32)).astype(BF16)


def dot(a, b):
    return jnp.dot(a, b, preferred_element_type=F32)


def dot_nt(a, b):
    return lax.dot_general(a, b, (((1,), (1,)), ((), ())), preferred_element_type=F32)


def place():
    return lax.axis_index("fib"), lax.axis_index("row"), lax.axis_index("slab")


def plane_peer(d):
    fib, row, slab = place()
    row, slab = lax.rem(row + d // 2, 4), lax.rem(slab + d % 2, 2)
    return (fib, row, slab), row * 2 + slab


def fib_peer(d):
    fib, row, slab = place()
    fib = lax.rem(fib // 4 + d // 4, 4) * 4 + lax.rem(fib % 4 + d % 4, 4)
    return (fib, row, slab), fib


def each(lower, upper, step):
    def run(index, carry):
        step(index)
        return carry

    lax.fori_loop(lower, upper, run, 0)


def remote(src, dst, send, recv, device):
    return pltpu.make_async_remote_copy(
        src_ref=src, dst_ref=dst, send_sem=send, recv_sem=recv, device_id=device, device_id_type=MESH
    )


def greet(plane, fibers):
    barrier = pltpu.get_barrier_semaphore()
    count = 0
    if plane:
        count += 7
        each(1, 8, lambda d: pl.semaphore_signal(barrier, inc=1, device_id=plane_peer(d)[0], device_id_type=MESH))
    if fibers:
        count += 15
        each(1, 16, lambda d: pl.semaphore_signal(barrier, inc=1, device_id=fib_peer(d)[0], device_id_type=MESH))
    pl.semaphore_wait(barrier, count)


def stack(x):
    high, low = split(x)
    return jnp.concatenate([jnp.concatenate([high, high], 1), jnp.concatenate([low, low], 1)], 0)


def left_half(shape):
    return lax.broadcasted_iota(jnp.int32, shape, 1) < 64


def halves(x):
    return jnp.concatenate(split(x), axis=0)


def eliminate(crossed):
    lane = lax.broadcasted_iota(jnp.int32, (8, 64), 1)
    row = lax.broadcasted_iota(jnp.int32, (8, 64), 0)
    below = lax.broadcasted_iota(jnp.int32, (8, 128), 0)
    blocks = [
        jnp.concatenate([crossed[8 * b : 8 * b + 8], jnp.where(lane == row + 8 * b, 1.0, 0.0)], axis=1) for b in range(8)
    ]
    for j in range(64):
        b, k = j // 8, j % 8
        scale = lax.rsqrt(blocks[b][k : k + 1, j : j + 1])
        pivot = blocks[b][k : k + 1, :] * scale
        updated = blocks[b] - blocks[b][:, j : j + 1] * scale * pivot
        for other in range(b + 1, 8):
            blocks[other] = blocks[other] - blocks[other][:, j : j + 1] * scale * pivot
        blocks[b] = jnp.where(below > k, updated, jnp.where(below == k, pivot, blocks[b]))
    return jnp.concatenate(blocks, axis=0)[:, 64:]


def kernel(
    tensor, four, three, two, one, updated, collected, four_stack, one_stack,
    staged, outgoing, incoming, halfway, contracted, fibers, two_all, three_all, wide_high, wide_low,
    fibers_high, fibers_low, partial, scattered, shared, reduced, core_out, core_in,
    load_sem, own_sem, z_send, z_recv, fib_own_sem, f_send, f_recv,
    two_send, two_recv, three_send, three_recv, small_own, rs_send, rs_recv, ar_send, ar_recv, ag_send, ag_recv, core_send, core_recv,
):
    fib, row, slab = place()
    me = row * 2 + slab

    def load(chunk):
        return pltpu.make_async_copy(tensor.at[chunk], staged.at[chunk % 3], load_sem.at[chunk % 3])

    load(0).start()
    load(1).start()
    four_stack[...] = stack(four[...])
    one_stack[...] = halves(one[...])
    greet(True, True)

    def two_copy(step, block):
        peer = lax.rem(row + step, 4)
        return remote(two, two_all.at[block], two_send.at[step], two_recv.at[block], (fib, peer, slab))

    def three_copy():
        return remote(three, three_all.at[slab], three_send, three_recv, (fib, row, 1 - slab))

    two_own = pltpu.make_async_copy(two, two_all.at[row], small_own.at[0])
    three_own = pltpu.make_async_copy(three, three_all.at[slab], small_own.at[1])
    each(1, 4, lambda s: two_copy(s, row).start())
    three_copy().start()
    two_own.start()
    three_own.start()

    def z_copy(chunk, d):
        device, peer = plane_peer(d)
        return remote(
            outgoing.at[chunk, pl.ds(peer * 256, 256), :],
            incoming.at[chunk, pl.ds(me * 256, 256), :],
            z_send.at[chunk, d], z_recv.at[chunk, me], device,
        )

    def z_arrived(chunk, d):
        device, peer = plane_peer(d)
        block = incoming.at[chunk, pl.ds(peer * 256, 256), :]
        remote(block, block, z_send.at[chunk, d], z_recv.at[chunk, peer], device).wait_recv()

    def z_own(chunk):
        rows = pl.ds(me * 256, 256)
        return pltpu.make_async_copy(outgoing.at[chunk, rows, :], incoming.at[chunk, rows, :], own_sem.at[chunk])

    def f_copy(chunk, d):
        device, peer = fib_peer(d)
        return remote(
            contracted.at[chunk, pl.ds(peer * 64, 64), :],
            fibers.at[pl.ds((fib * CHUNKS + chunk) * 64, 64), :],
            f_send.at[chunk, d], f_recv.at[chunk, fib], device,
        )

    def f_arrived(chunk, d):
        device, peer = fib_peer(d)
        block = fibers.at[pl.ds((peer * CHUNKS + chunk) * 64, 64), :]
        remote(block, block, f_send.at[chunk, d], f_recv.at[chunk, peer], device).wait_recv()

    def f_own(chunk):
        return pltpu.make_async_copy(
            contracted.at[chunk, pl.ds(fib * 64, 64), :],
            fibers.at[pl.ds((fib * CHUNKS + chunk) * 64, 64), :],
            fib_own_sem.at[chunk],
        )

    def mode_four(chunk):
        slot = chunk % 3

        def two_steps(pair):
            first = staged[slot, pl.ds(2 * pair, 128, stride=32), :]
            second = staged[slot, pl.ds(2 * pair + 1, 128, stride=32), :]
            high, low = split(jnp.concatenate([first, second], axis=0))
            out = dot_nt(four_stack[...], jnp.concatenate([high, low], axis=1))
            out = out[:64] + out[64:]
            outgoing[chunk, pl.ds(2 * pair, 64, stride=32), :] = out[:, :128]
            outgoing[chunk, pl.ds(2 * pair + 1, 64, stride=32), :] = out[:, 128:]

        each(0, 16, two_steps)

    def modes_three_two(chunk):
        whole = three_all[0] + three_all[1]
        high, low = split(whole)
        lanes = lax.broadcasted_iota(jnp.int32, (64, 256), 1)
        factor = jnp.where(lanes < 128, high.astype(F32), low.astype(F32)).astype(BF16)

        def rank(r):
            parts = []
            for z in range(4):
                pieces = [incoming[chunk, pl.ds((2 * z + c) * 256 + r * 32, 32), :] for c in range(2)]
                high, low = split(jnp.concatenate(pieces, axis=0))
                parts.append(jnp.concatenate([high, low, high, low], axis=0))
            out = dot(factor, jnp.concatenate(parts, axis=1))
            for z in range(4):
                halfway[z, pl.ds(r, 64, stride=8), :] = out[:, z * 128 : (z + 1) * 128]

        each(0, 8, rank)

        def rows(block):
            at = pl.ds(pl.multiple_of(block * 128, 128), 128)
            total = jnp.zeros((128, 256), F32)
            for z in range(4):
                high, low = split(halfway[z, at, :])
                both = dot(jnp.concatenate([high, low], axis=0), wide_high[z])
                total = total + both[:128] + both[128:] + dot(high, wide_low[z])
            left = left_half((16, 128))
            for f in range(4):
                for t in range(2):
                    lower = total[f * 32 : f * 32 + 16, t * 128 : t * 128 + 128]
                    upper = total[f * 32 + 16 : f * 32 + 32, t * 128 : t * 128 + 128]
                    even = jnp.where(left, lower, pltpu.roll(upper, 64, 1))
                    odd = jnp.where(left, pltpu.roll(lower, 64, 1), upper)
                    start = pl.multiple_of((block * 4 + f) * 64 + t * 32, 32)
                    contracted[chunk, pl.ds(start, 32), :] = jnp.concatenate([even, odd], axis=0)

        each(0, 4, rows)

    def widen():
        two_own.wait()
        three_own.wait()
        each(1, 4, lambda s: two_copy(s, lax.rem(row + 4 - s, 4)).wait_recv())
        remote(three, three_all.at[1 - slab], three_send, three_recv, (fib, row, 1 - slab)).wait_recv()
        left = left_half((32, 128))
        nothing = jnp.zeros((32, 128), F32)
        for z in range(4):
            block = two_all[z]
            sides = (jnp.where(left, block, 0.0), jnp.where(left, 0.0, block))
            pieces = []
            for i in range(4):
                tiles = [nothing, nothing]
                tiles[i // 2] = sides[i % 2]
                pieces.append(jnp.concatenate(tiles, axis=1))
            high, low = split(jnp.concatenate(pieces, axis=0))
            wide_high[z] = high
            wide_low[z] = low

    def advance(turn):
        @pl.when(turn < CHUNKS)
        def _():
            load(turn).wait()

            @pl.when(turn + 2 < CHUNKS)
            def _():
                load(turn + 2).start()

            mode_four(turn)

            @pl.when(turn >= 2)
            def _():
                each(1, 8, lambda d: z_copy(turn - 2, d).wait_send())

            each(1, 8, lambda d: z_copy(turn, d).start())
            z_own(turn).start()

        @pl.when(turn == 0)
        def _():
            widen()

        @pl.when(turn >= LAG)
        def _():
            chunk = turn - LAG
            z_own(chunk).wait()
            each(1, 8, lambda d: z_arrived(chunk, d))
            modes_three_two(chunk)
            each(1, 16, lambda d: f_copy(chunk, d).start())
            f_own(chunk).start()

    each(0, CHUNKS + LAG, advance)
    each(CHUNKS - 2, CHUNKS, lambda chunk: each(1, 8, lambda d: z_copy(chunk, d).wait_send()))

    def gathered(chunk):
        f_own(chunk).wait()
        each(1, 16, lambda d: f_arrived(chunk, d))

    each(0, CHUNKS, gathered)
    partial[...] = jnp.zeros_like(partial)

    def cross(step):
        block = jnp.concatenate([fibers[pl.ds(2 * step + n, 512, stride=16), :] for n in range(2)], axis=1)
        high, low = split(block)
        fibers_high[step] = high
        fibers_low[step] = low
        both = dot(one_stack[...], high)
        both_parts = halves(both[:64] + both[64:] + dot(one_stack[:64, :], low))
        back = dot_nt(both_parts, high)
        partial[...] += back[:64] + back[64:] + dot_nt(both_parts[:64], low)

    each(0, 8, cross)

    def rs_copy(d):
        device, peer = plane_peer(d)
        return remote(partial.at[pl.ds(peer * 8, 8), :], scattered.at[me], rs_send.at[d], rs_recv.at[me], device)

    def rs_arrived(d):
        device, peer = plane_peer(d)
        remote(scattered.at[peer], scattered.at[peer], rs_send.at[d], rs_recv.at[peer], device).wait_recv()

    def ar_copy(d):
        device, peer = fib_peer(d)
        return remote(shared.at[fib], shared.at[fib], ar_send.at[d], ar_recv.at[fib], device)

    def ar_arrived(d):
        device, peer = fib_peer(d)
        remote(shared.at[peer], shared.at[peer], ar_send.at[d], ar_recv.at[peer], device).wait_recv()

    def ag_copy(d):
        device, peer = plane_peer(d)
        mine = reduced.at[pl.ds(me * 8, 8), :]
        return remote(mine, mine, ag_send.at[d], ag_recv.at[me], device)

    def ag_arrived(d):
        device, peer = plane_peer(d)
        block = reduced.at[pl.ds(peer * 8, 8), :]
        remote(block, block, ag_send.at[d], ag_recv.at[peer], device).wait_recv()

    each(1, 8, lambda d: rs_copy(d).start())
    scattered[me] = partial[pl.ds(pl.multiple_of(me * 8, 8), 8), :]
    each(1, 8, rs_arrived)
    shared[fib] = jnp.sum(scattered[...], axis=0)
    each(1, 16, lambda d: ar_copy(d).start())
    each(1, 16, ar_arrived)
    reduced[pl.ds(pl.multiple_of(me * 8, 8), 8), :] = jnp.sum(shared[...], axis=0)
    each(1, 8, lambda d: ag_copy(d).start())
    each(1, 8, ag_arrived)

    updated[...] = reduced[...]

    def cholesky_qr(repeat):
        rows = updated[...]
        crossed = lax.dot_general(rows, rows, (((1,), (1,)), ((), ())), precision=HIGHEST, preferred_element_type=F32)
        updated[...] = jnp.dot(eliminate(crossed), rows, precision=HIGHEST, preferred_element_type=F32)

    each(0, 2, cholesky_qr)
    one_stack[...] = halves(updated[...])

    def core(step):
        both = dot(one_stack[...], fibers_high[step])
        out = both[:64] + both[64:] + dot(one_stack[:64, :], fibers_low[step])
        across = jnp.concatenate([out[:, :128], out[:, 128:]], axis=0).T
        for half in range(2):
            for peer in range(8):
                start = half * 64 + peer * 8
                core_out[peer, pl.ds(pl.multiple_of(step * 16 + half * 8, 8), 8), :] = across[start : start + 8, :]

    each(0, 8, core)

    def core_copy(d):
        device, peer = plane_peer(d)
        return remote(core_out.at[peer], core_in.at[me], core_send.at[d], core_recv.at[me], device)

    def core_arrived(d):
        device, peer = plane_peer(d)
        remote(core_in.at[peer], core_in.at[peer], core_send.at[d], core_recv.at[peer], device).wait_recv()

    each(1, 8, lambda d: core_copy(d).start())
    core_in[me] = core_out[me]
    each(1, 8, core_arrived)
    collected[...] = core_in[...]

    each(1, 8, lambda d: core_copy(d).wait_send())

    each(1, 8, lambda d: rs_copy(d).wait_send())
    each(1, 16, lambda d: ar_copy(d).wait_send())
    each(1, 8, lambda d: ag_copy(d).wait_send())
    each(1, 4, lambda s: two_copy(s, row).wait_send())
    three_copy().wait_send()
    each(0, CHUNKS, lambda chunk: each(1, 16, lambda d: f_copy(chunk, d).wait_send()))


def body(tensor, factor_one, factor_two, factor_three, factor_four):
    slab = lax.axis_index("slab")
    across = factor_three.T
    nothing = jnp.zeros_like(across)
    three = jnp.where(slab == 0, jnp.concatenate([across, nothing], 1), jnp.concatenate([nothing, across], 1))
    three = jnp.concatenate([three] * 4, 1)
    two = jnp.concatenate([factor_two, factor_two], 1)
    vmem = pl.BlockSpec(memory_space=pltpu.VMEM)
    hbm = pl.BlockSpec(memory_space=pl.ANY)
    dma = pltpu.SemaphoreType.DMA
    updated, core = pl.pallas_call(
        kernel,
        out_shape=(jax.ShapeDtypeStruct((64, 512), F32), jax.ShapeDtypeStruct((8, 128, 128), F32)),
        in_specs=[hbm, vmem, vmem, vmem, vmem],
        out_specs=(vmem, vmem),
        scratch_shapes=[
            pltpu.VMEM((128, 256), BF16),
            pltpu.VMEM((128, 512), BF16),
            pltpu.VMEM((3, 4096, 128), F32),
            pltpu.VMEM((CHUNKS, 2048, 128), F32),
            pltpu.VMEM((CHUNKS, 2048, 128), F32),
            pltpu.VMEM((4, 512, 128), F32),
            pltpu.VMEM((CHUNKS, 1024, 128), F32),
            pltpu.VMEM((8192, 128), F32),
            pltpu.VMEM((4, 32, 128), F32),
            pltpu.VMEM((2, 64, 256), F32),
            pltpu.VMEM((4, 128, 256), BF16),
            pltpu.VMEM((4, 128, 256), BF16),
            pltpu.VMEM((8, 512, 256), BF16),
            pltpu.VMEM((8, 512, 256), BF16),
            pltpu.VMEM((64, 512), F32),
            pltpu.VMEM((8, 8, 512), F32),
            pltpu.VMEM((16, 8, 512), F32),
            pltpu.VMEM((64, 512), F32),
            pltpu.VMEM((8, 128, 128), F32),
            pltpu.VMEM((8, 128, 128), F32),
            dma((3,)), dma((CHUNKS,)), dma((CHUNKS, 8)), dma((CHUNKS, 8)), dma((CHUNKS,)), dma((CHUNKS, 16)), dma((CHUNKS, 16)),
            dma((4,)), dma((4,)), dma(()), dma(()), dma((2,)), dma((8,)), dma((8,)), dma((16,)), dma((16,)), dma((8,)), dma((8,)), dma((8,)), dma((8,)),
        ],
        compiler_params=pltpu.CompilerParams(collective_id=0, has_side_effects=True, vmem_limit_bytes=56 * 2**20),
        name="hooi",
    )(tensor.reshape(8, 4096, 128), factor_four.T, three, two, factor_one.T)
    core = core.reshape(8, 2, 4, 2, 8, 2, 64).transpose(6, 4, 3, 1, 0, 2, 5).reshape(64, 8, 4, 64)
    return (updated.T, core)


def solution(mesh):
    in_specs = (P("fib", "row", "slab", None), P(), P("row", None), P("slab", None), P())
    out_specs = (P(), P(None, ("row", "slab"), "fib", None))
    return jax.shard_map(body, mesh=mesh, in_specs=in_specs, out_specs=out_specs, check_vma=False)
```

```python
import jax
import jax.numpy as jnp
from jax import lax
from jax.experimental import pallas as pl
from jax.experimental.pallas import tpu as pltpu
from jax.sharding import PartitionSpec as P

HIGHEST = lax.Precision.HIGHEST
MESH = pl.DeviceIdType.MESH
F32 = jnp.float32
BF16 = jnp.bfloat16
CHUNKS = 8
LAG = 2
PLANE = tuple(range(1, 8))
FIBERS = tuple(sorted(range(1, 16), key=lambda d: -(min(d // 4, 4 - d // 4) + min(d % 4, 4 - d % 4))))


def split(x):
    high = x.astype(BF16)
    return high, (x - high.astype(F32)).astype(BF16)


def dot(a, b):
    return jnp.dot(a, b, preferred_element_type=F32)


def dot_nt(a, b):
    return lax.dot_general(a, b, (((1,), (1,)), ((), ())), preferred_element_type=F32)


def place():
    return lax.axis_index("fib"), lax.axis_index("row"), lax.axis_index("slab")


def plane_peer(d):
    fib, row, slab = place()
    row, slab = lax.rem(row + d // 2, 4), lax.rem(slab + d % 2, 2)
    return (fib, row, slab), row * 2 + slab


def fib_peer(d):
    fib, row, slab = place()
    fib = lax.rem(fib // 4 + d // 4, 4) * 4 + lax.rem(fib % 4 + d % 4, 4)
    return (fib, row, slab), fib


def each(lower, upper, step, unroll=1):
    def run(index, carry):
        step(index)
        return carry

    lax.fori_loop(lower, upper, run, 0, unroll=unroll)


def remote(src, dst, send, recv, device):
    return pltpu.make_async_remote_copy(
        src_ref=src, dst_ref=dst, send_sem=send, recv_sem=recv, device_id=device, device_id_type=MESH
    )


def greet():
    barrier = pltpu.get_barrier_semaphore()
    for d in PLANE:
        pl.semaphore_signal(barrier, inc=1, device_id=plane_peer(d)[0], device_id_type=MESH)
    for d in FIBERS:
        pl.semaphore_signal(barrier, inc=1, device_id=fib_peer(d)[0], device_id_type=MESH)


def stack(x):
    high, low = split(x)
    return jnp.concatenate([jnp.concatenate([high, high], 1), jnp.concatenate([low, low], 1)], 0)


def left_half(shape):
    return lax.broadcasted_iota(jnp.int32, shape, 1) < 64


def halves(x):
    return jnp.concatenate(split(x), axis=0)


def eliminate(crossed, group=4):
    lane = lax.broadcasted_iota(jnp.int32, (8, 64), 1)
    row = lax.broadcasted_iota(jnp.int32, (8, 64), 0)
    below = lax.broadcasted_iota(jnp.int32, (8, 128), 0)
    blocks = [
        jnp.concatenate([crossed[8 * b : 8 * b + 8], jnp.where(lane == row + 8 * b, 1.0, 0.0)], axis=1) for b in range(8)
    ]

    def spread(x):
        return jnp.broadcast_to(x, (8, 128))

    for first in range(0, 64, group):
        b, k = first // 8, first % 8
        here = blocks[b]
        corner = [[spread(here[k + m : k + m + 1, first + n : first + n + 1]) for n in range(m + 1)] for m in range(group)]
        below_diagonal = [[None] * group for m in range(group)]
        scale = [None] * group
        for m in range(group):
            square = corner[m][m]
            for n in range(m):
                square = square - below_diagonal[m][n] * below_diagonal[m][n]
            scale[m] = lax.rsqrt(square)
            for other in range(m + 1, group):
                entry = corner[other][m]
                for n in range(m):
                    entry = entry - below_diagonal[other][n] * below_diagonal[m][n]
                below_diagonal[other][m] = entry * scale[m]

        def forward(parts):
            done = []
            for m in range(group):
                part = parts[m]
                for n in range(m):
                    part = part - done[n] * below_diagonal[m][n]
                done.append(part * scale[m])
            return done

        pivots = forward([spread(here[k + m : k + m + 1, :]) for m in range(group)])
        for at in range(b, 8):
            if at == b and k + group == 8:
                update = here
            else:
                columns = forward([spread(blocks[at][:, first + m : first + m + 1]) for m in range(group)])
                update = blocks[at]
                for m in range(group):
                    update = update - columns[m] * pivots[m]
            if at == b:
                update = jnp.where(below < k, here, update)
                for m in range(group):
                    update = jnp.where(below == k + m, pivots[m], update)
            blocks[at] = update
    return jnp.concatenate(blocks, axis=0)[:, 64:]


def kernel(
    tensor, four, three, two, one, updated, collected, four_stack, one_stack, three_own_block, two_own_block,
    staged, outgoing, incoming, halfway, contracted, fibers, two_all, three_all, three_stack, wide_high, wide_low,
    fibers_high, fibers_low, partial, scattered, shared, reduced, core_out, core_in,
    load_sem, own_sem, z_send, z_recv, fib_own_sem, f_send, f_recv,
    two_send, two_recv, three_send, three_recv, rs_send, rs_recv, ar_send, ar_recv, ag_send, ag_recv, core_send, core_recv,
):
    fib, row, slab = place()
    me = row * 2 + slab

    def load(chunk):
        return pltpu.make_async_copy(tensor.at[chunk], staged.at[chunk % 3], load_sem.at[chunk % 3])

    def mode_four(chunk):
        slot = chunk % 3

        def two_steps(pair):
            first = staged[slot, pl.ds(2 * pair, 128, stride=32), :]
            second = staged[slot, pl.ds(2 * pair + 1, 128, stride=32), :]
            high, low = split(jnp.concatenate([first, second], axis=0))
            out = dot_nt(four_stack[...], jnp.concatenate([high, low], axis=1))
            out = out[:64] + out[64:]
            outgoing[chunk, pl.ds(2 * pair, 64, stride=32), :] = out[:, :128]
            outgoing[chunk, pl.ds(2 * pair + 1, 64, stride=32), :] = out[:, 128:]

        each(0, 16, two_steps, unroll=2)

    load(0).start()
    load(1).start()
    greet()
    four_stack[...] = stack(four[...].T)
    load(0).wait()
    load(2).start()
    mode_four(0)
    pl.semaphore_wait(pltpu.get_barrier_semaphore(), len(PLANE) + len(FIBERS))

    def z_copy(chunk, half, d):
        device, peer = plane_peer(d)
        return remote(
            outgoing.at[chunk, pl.ds(peer * 256 + half * 128, 128), :],
            incoming.at[chunk, half, pl.ds(me * 128, 128), :],
            z_send.at[chunk, half], z_recv.at[chunk, half], device,
        )

    def z_all(chunk, half):
        block = incoming.at[chunk, half, pl.ds(0, 7 * 128), :]
        return remote(block, block, z_send.at[chunk, half], z_recv.at[chunk, half], plane_peer(1)[0])

    def z_own(chunk, half):
        return pltpu.make_async_copy(
            outgoing.at[chunk, pl.ds(me * 256 + half * 128, 128), :],
            incoming.at[chunk, half, pl.ds(me * 128, 128), :],
            own_sem.at[chunk, half],
        )

    def send_chunk(chunk):
        for half in range(2):
            for d in PLANE:
                z_copy(chunk, half, d).start()
            z_own(chunk, half).start()

    def sent_chunk(chunk):
        for half in range(2):
            z_all(chunk, half).wait_send()

    def f_rows(chunk, half, device):
        return fibers.at[pl.ds((device * CHUNKS + chunk) * 4, 4), half]

    def f_copy(chunk, half, d):
        device, peer = fib_peer(d)
        return remote(contracted.at[chunk, half, peer], f_rows(chunk, half, fib), f_send, f_recv, device)

    def f_all():
        block = fibers.at[pl.ds(0, 15 * CHUNKS * 4)]
        return remote(block, block, f_send, f_recv, fib_peer(1)[0])

    def f_own(chunk, half):
        return pltpu.make_async_copy(contracted.at[chunk, half, fib], f_rows(chunk, half, fib), fib_own_sem.at[chunk, half])

    def two_copy(step):
        return remote(two_own_block, two_all.at[row], two_send, two_recv, (fib, lax.rem(row + step, 4), slab))

    def two_arrived():
        block = two_all.at[pl.ds(0, 3)]
        return remote(block, block, two_send, two_recv, (fib, lax.rem(row + 1, 4), slab))

    def three_copy():
        return remote(three_own_block, three_all.at[slab], three_send, three_recv, (fib, row, 1 - slab))

    def exchange_factors():
        two_own_block[...] = jnp.concatenate([two[...], two[...]], axis=1)
        across = three[...].T
        nothing = jnp.zeros_like(across)
        mine = jnp.where(slab == 0, 1.0, 0.0)
        block = jnp.concatenate([across * mine, across * (1.0 - mine)], axis=1)
        three_own_block[...] = jnp.concatenate([block] * 4, axis=1)
        for step in range(1, 4):
            two_copy(step).start()
        three_copy().start()
        two_all[row] = two_own_block[...]
        three_all[slab] = three_own_block[...]

    def widen():
        two_arrived().wait_recv()
        three_copy().wait_recv()
        high, low = split(three_all[0] + three_all[1])
        lanes = lax.broadcasted_iota(jnp.int32, (64, 256), 1)
        three_stack[...] = jnp.where(lanes < 128, high.astype(F32), low.astype(F32)).astype(BF16)
        left = left_half((32, 128))
        nothing = jnp.zeros((32, 128), F32)
        for z in range(4):
            block = two_all[z]
            sides = (jnp.where(left, block, 0.0), jnp.where(left, 0.0, block))
            pieces = []
            for i in range(4):
                tiles = [nothing, nothing]
                tiles[i // 2] = sides[i % 2]
                pieces.append(jnp.concatenate(tiles, axis=1))
            high, low = split(jnp.concatenate(pieces, axis=0))
            wide_high[z] = high
            wide_low[z] = low
        one_stack[...] = halves(one[...].T)

    def modes_three_two(chunk, half):
        def rank(r):
            parts = []
            for z in range(4):
                pieces = [incoming[chunk, half, pl.ds((2 * z + c) * 128 + r * 32, 32), :] for c in range(2)]
                high, low = split(jnp.concatenate(pieces, axis=0))
                parts.append(jnp.concatenate([high, low, high, low], axis=0))
            out = dot(three_stack[...], jnp.concatenate(parts, axis=1))
            for z in range(4):
                halfway[z, pl.ds(r, 64, stride=4), :] = out[:, z * 128 : (z + 1) * 128]

        each(0, 4, rank, unroll=2)

        def rows(block):
            at = pl.ds(pl.multiple_of(block * 128, 128), 128)
            total = jnp.zeros((128, 256), F32)
            for z in range(4):
                high, low = split(halfway[z, at, :])
                both = dot(jnp.concatenate([high, low], axis=0), wide_high[z])
                total = total + both[:128] + both[128:] + dot(high, wide_low[z])
            left = left_half((8, 128))
            for f in range(8):
                for t in range(2):
                    lower = total[f * 16 : f * 16 + 8, t * 128 : t * 128 + 128]
                    upper = total[f * 16 + 8 : f * 16 + 16, t * 128 : t * 128 + 128]
                    contracted[chunk, half, block * 8 + f, 2 * t] = jnp.where(left, lower, pltpu.roll(upper, 64, 1))
                    contracted[chunk, half, block * 8 + f, 2 * t + 1] = jnp.where(left, pltpu.roll(lower, 64, 1), upper)

        each(0, 2, rows)

    def advance(turn):
        @pl.when(turn < CHUNKS)
        def _():
            @pl.when(turn >= 2)
            def _():
                sent_chunk(turn - 2)

            send_chunk(turn)

        @pl.when(turn == 0)
        def _():
            exchange_factors()

        @pl.when(turn + 1 < CHUNKS)
        def _():
            load(turn + 1).wait()

            @pl.when(turn + 3 < CHUNKS)
            def _():
                load(turn + 3).start()

            mode_four(turn + 1)

        @pl.when(turn == 0)
        def _():
            widen()

        @pl.when(turn >= LAG)
        def _():
            chunk = turn - LAG

            def one_half(half):
                z_own(chunk, half).wait()
                z_all(chunk, half).wait_recv()
                modes_three_two(chunk, half)
                for d in FIBERS:
                    f_copy(chunk, half, d).start()
                f_own(chunk, half).start()

            each(0, 2, one_half)

    each(0, CHUNKS + LAG, advance)
    each(CHUNKS - 2, CHUNKS, sent_chunk)
    partial[...] = jnp.zeros_like(partial)
    each(0, CHUNKS, lambda chunk: each(0, 2, lambda half: f_own(chunk, half).wait()))
    f_all().wait_recv()
    fiber_rows = fibers.reshape(8192, 128)

    def cross(step):
        block = jnp.concatenate([fiber_rows[pl.ds(2 * step + n, 512, stride=16), :] for n in range(2)], axis=1)
        high, low = split(block)
        fibers_high[step] = high
        fibers_low[step] = low
        both = dot(one_stack[...], high)
        both_parts = halves(both[:64] + both[64:] + dot(one_stack[:64, :], low))
        back = dot_nt(both_parts, high)
        partial[...] += back[:64] + back[64:] + dot_nt(both_parts[:64], low)

    each(0, 8, cross, unroll=2)

    def rs_copy(d):
        device, peer = plane_peer(d)
        return remote(partial.at[pl.ds(peer * 8, 8), :], scattered.at[me], rs_send, rs_recv, device)

    def ar_copy(d):
        return remote(shared.at[fib], shared.at[fib], ar_send, ar_recv, fib_peer(d)[0])

    def ag_copy(d):
        mine = reduced.at[pl.ds(me * 8, 8), :]
        return remote(mine, mine, ag_send, ag_recv, plane_peer(d)[0])

    def rs_all():
        block = scattered.at[pl.ds(0, 7)]
        return remote(block, block, rs_send, rs_recv, plane_peer(1)[0])

    def ar_all():
        block = shared.at[pl.ds(0, 15)]
        return remote(block, block, ar_send, ar_recv, fib_peer(1)[0])

    def ag_all():
        block = reduced.at[pl.ds(0, 56), :]
        return remote(block, block, ag_send, ag_recv, plane_peer(1)[0])

    for d in PLANE:
        rs_copy(d).start()
    scattered[me] = partial[pl.ds(pl.multiple_of(me * 8, 8), 8), :]
    rs_all().wait_recv()
    shared[fib] = jnp.sum(scattered[...], axis=0)
    for d in FIBERS:
        ar_copy(d).start()
    ar_all().wait_recv()
    reduced[pl.ds(pl.multiple_of(me * 8, 8), 8), :] = jnp.sum(shared[...], axis=0)
    for d in PLANE:
        ag_copy(d).start()
    ag_all().wait_recv()

    updated[...] = reduced[...]

    def cholesky_qr(repeat):
        rows = updated[...]
        crossed = lax.dot_general(rows, rows, (((1,), (1,)), ((), ())), precision=HIGHEST, preferred_element_type=F32)
        updated[...] = jnp.dot(eliminate(crossed), rows, precision=HIGHEST, preferred_element_type=F32)

    each(0, 2, cholesky_qr)
    one_stack[...] = halves(updated[...])

    def core(step):
        both = dot(one_stack[...], fibers_high[step])
        out = both[:64] + both[64:] + dot(one_stack[:64, :], fibers_low[step])
        across = jnp.concatenate([out[:, :128], out[:, 128:]], axis=0).T
        for half in range(2):
            for peer in range(8):
                start = half * 64 + peer * 8
                core_out[peer, pl.ds(pl.multiple_of(step * 16 + half * 8, 8), 8), :] = across[start : start + 8, :]

    each(0, 8, core, unroll=2)

    def core_copy(d):
        device, peer = plane_peer(d)
        return remote(core_out.at[peer], core_in.at[me], core_send, core_recv, device)

    def core_all():
        block = core_in.at[pl.ds(0, 7)]
        return remote(block, block, core_send, core_recv, plane_peer(1)[0])

    for d in PLANE:
        core_copy(d).start()
    core_in[me] = core_out[me]
    core_all().wait_recv()
    collected[...] = core_in[...]

    core_all().wait_send()
    rs_all().wait_send()
    ar_all().wait_send()
    ag_all().wait_send()
    two_arrived().wait_send()
    three_copy().wait_send()
    f_all().wait_send()


def body(tensor, factor_one, factor_two, factor_three, factor_four):
    vmem = pl.BlockSpec(memory_space=pltpu.VMEM)
    hbm = pl.BlockSpec(memory_space=pl.ANY)
    dma = pltpu.SemaphoreType.DMA
    updated, core = pl.pallas_call(
        kernel,
        out_shape=(jax.ShapeDtypeStruct((64, 512), F32), jax.ShapeDtypeStruct((8, 128, 128), F32)),
        in_specs=[hbm, vmem, vmem, vmem, vmem],
        out_specs=(vmem, vmem),
        scratch_shapes=[
            pltpu.VMEM((128, 256), BF16),
            pltpu.VMEM((128, 512), BF16),
            pltpu.VMEM((64, 256), F32),
            pltpu.VMEM((32, 128), F32),
            pltpu.VMEM((3, 4096, 128), F32),
            pltpu.VMEM((CHUNKS, 2048, 128), F32),
            pltpu.VMEM((CHUNKS, 2, 1024, 128), F32),
            pltpu.VMEM((4, 256, 128), F32),
            pltpu.VMEM((CHUNKS, 2, 16, 4, 8, 128), F32),
            pltpu.VMEM((512, 2, 8, 128), F32),
            pltpu.VMEM((4, 32, 128), F32),
            pltpu.VMEM((2, 64, 256), F32),
            pltpu.VMEM((64, 256), BF16),
            pltpu.VMEM((4, 128, 256), BF16),
            pltpu.VMEM((4, 128, 256), BF16),
            pltpu.VMEM((8, 512, 256), BF16),
            pltpu.VMEM((8, 512, 256), BF16),
            pltpu.VMEM((64, 512), F32),
            pltpu.VMEM((8, 8, 512), F32),
            pltpu.VMEM((16, 8, 512), F32),
            pltpu.VMEM((64, 512), F32),
            pltpu.VMEM((8, 128, 128), F32),
            pltpu.VMEM((8, 128, 128), F32),
            dma((3,)), dma((CHUNKS, 2)), dma((CHUNKS, 2)), dma((CHUNKS, 2)), dma((CHUNKS, 2)), dma(()), dma(()),
            dma(()), dma(()), dma(()), dma(()), dma(()), dma(()), dma(()), dma(()), dma(()), dma(()), dma(()), dma(()),
        ],
        compiler_params=pltpu.CompilerParams(collective_id=0, has_side_effects=True, vmem_limit_bytes=56 * 2**20),
        name="hooi",
    )(tensor.reshape(8, 4096, 128), factor_four, factor_three, factor_two, factor_one)
    core = core.reshape(8, 2, 2, 2, 2, 8, 2, 64).transpose(7, 5, 4, 2, 0, 1, 3, 6).reshape(64, 8, 4, 64)
    return (updated.T, core)


def solution(mesh):
    in_specs = (P("fib", "row", "slab", None), P(), P("row", None), P("slab", None), P())
    out_specs = (P(), P(None, ("row", "slab"), "fib", None))
    return jax.shard_map(body, mesh=mesh, in_specs=in_specs, out_specs=out_specs, check_vma=False)
```

```python
import jax
import jax.numpy as jnp
from jax import lax
from jax.experimental import pallas as pl
from jax.experimental.pallas import tpu as pltpu
from jax.sharding import PartitionSpec as P

HIGHEST = lax.Precision.HIGHEST
MESH = pl.DeviceIdType.MESH
F32 = jnp.float32
BF16 = jnp.bfloat16
CHUNKS = 8
LAG = 2
PLANE = tuple(range(1, 8))
FIBERS = tuple(sorted(range(1, 16), key=lambda d: -(min(d // 4, 4 - d // 4) + min(d % 4, 4 - d % 4))))


def split(x):
    high = x.astype(BF16)
    return high, (x - high.astype(F32)).astype(BF16)


def dot(a, b):
    return jnp.dot(a, b, preferred_element_type=F32)


def dot_nt(a, b):
    return lax.dot_general(a, b, (((1,), (1,)), ((), ())), preferred_element_type=F32)


def place():
    return lax.axis_index("fib"), lax.axis_index("row"), lax.axis_index("slab")


def plane_peer(d):
    fib, row, slab = place()
    row, slab = lax.rem(row + d // 2, 4), lax.rem(slab + d % 2, 2)
    return (fib, row, slab), row * 2 + slab


def fib_peer(d):
    fib, row, slab = place()
    fib = lax.rem(fib // 4 + d // 4, 4) * 4 + lax.rem(fib % 4 + d % 4, 4)
    return (fib, row, slab), fib


def each(lower, upper, step, unroll=1):
    def run(index, carry):
        step(index)
        return carry

    lax.fori_loop(lower, upper, run, 0, unroll=unroll)


def remote(src, dst, send, recv, device):
    return pltpu.make_async_remote_copy(
        src_ref=src, dst_ref=dst, send_sem=send, recv_sem=recv, device_id=device, device_id_type=MESH
    )


def greet():
    barrier = pltpu.get_barrier_semaphore()
    for d in PLANE:
        pl.semaphore_signal(barrier, inc=1, device_id=plane_peer(d)[0], device_id_type=MESH)
    for d in FIBERS:
        pl.semaphore_signal(barrier, inc=1, device_id=fib_peer(d)[0], device_id_type=MESH)


def stack(x):
    high, low = split(x)
    return jnp.concatenate([jnp.concatenate([high, high], 1), jnp.concatenate([low, low], 1)], 0)


def left_half(shape):
    return lax.broadcasted_iota(jnp.int32, shape, 1) < 64


def halves(x):
    return jnp.concatenate(split(x), axis=0)


def eliminate(crossed, group=4):
    lane = lax.broadcasted_iota(jnp.int32, (8, 64), 1)
    row = lax.broadcasted_iota(jnp.int32, (8, 64), 0)
    below = lax.broadcasted_iota(jnp.int32, (8, 128), 0)
    blocks = [
        jnp.concatenate([crossed[8 * b : 8 * b + 8], jnp.where(lane == row + 8 * b, 1.0, 0.0)], axis=1) for b in range(8)
    ]

    def spread(x):
        return jnp.broadcast_to(x, (8, 128))

    for first in range(0, 64, group):
        b, k = first // 8, first % 8
        here = blocks[b]
        corner = [[spread(here[k + m : k + m + 1, first + n : first + n + 1]) for n in range(m + 1)] for m in range(group)]
        below_diagonal = [[None] * group for m in range(group)]
        scale = [None] * group
        for m in range(group):
            square = corner[m][m]
            for n in range(m):
                square = square - below_diagonal[m][n] * below_diagonal[m][n]
            scale[m] = lax.rsqrt(square)
            for other in range(m + 1, group):
                entry = corner[other][m]
                for n in range(m):
                    entry = entry - below_diagonal[other][n] * below_diagonal[m][n]
                below_diagonal[other][m] = entry * scale[m]

        def forward(parts):
            done = []
            for m in range(group):
                part = parts[m]
                for n in range(m):
                    part = part - done[n] * below_diagonal[m][n]
                done.append(part * scale[m])
            return done

        pivots = forward([spread(here[k + m : k + m + 1, :]) for m in range(group)])
        for at in range(b, 8):
            if at == b and k + group == 8:
                update = here
            else:
                columns = forward([spread(blocks[at][:, first + m : first + m + 1]) for m in range(group)])
                update = blocks[at]
                for m in range(group):
                    update = update - columns[m] * pivots[m]
            if at == b:
                update = jnp.where(below < k, here, update)
                for m in range(group):
                    update = jnp.where(below == k + m, pivots[m], update)
            blocks[at] = update
    return jnp.concatenate(blocks, axis=0)[:, 64:]


def kernel(
    tensor, four_hbm, three_hbm, two_hbm, one_hbm, updated, collected,
    four, three, two, one, dealt, four_stack, one_stack, three_own_block, two_own_block,
    staged, outgoing, incoming, halfway, contracted, fibers, two_all, three_all, three_stack, wide_high, wide_low,
    fibers_high, fibers_low, partial, scattered, shared, state, core_out, core_in,
    load_sem, factor_sem, own_sem, z_send, z_recv, fib_own_sem, f_send, f_recv,
    two_send, two_recv, three_send, three_recv, rs_send, rs_recv, ar_send, ar_recv, ag_send, ag_recv, core_send, core_recv,
):
    fib, row, slab = place()
    me = row * 2 + slab

    def load(chunk):
        return pltpu.make_async_copy(tensor.at[chunk], staged.at[chunk % 3], load_sem.at[chunk % 3])

    def mode_four(chunk):
        slot = chunk % 3

        def two_steps(pair):
            first = staged[slot, pl.ds(2 * pair, 128, stride=32), :]
            second = staged[slot, pl.ds(2 * pair + 1, 128, stride=32), :]
            high, low = split(jnp.concatenate([first, second], axis=0))
            out = dot_nt(four_stack[...], jnp.concatenate([high, low], axis=1))
            out = out[:64] + out[64:]
            outgoing[chunk, pl.ds(2 * pair, 64, stride=32), :] = out[:, :128]
            outgoing[chunk, pl.ds(2 * pair + 1, 64, stride=32), :] = out[:, 128:]

        each(0, 16, two_steps, unroll=2)

    def fetch(n):
        source, target = ((four_hbm, four), (three_hbm, three), (two_hbm, two), (one_hbm, one))[n]
        return pltpu.make_async_copy(source, target, factor_sem.at[n])

    fetch(0).start()
    load(0).start()
    load(1).start()
    for n in range(1, 4):
        fetch(n).start()
    greet()
    fetch(0).wait()
    across = four[...]
    dealt[pl.ds(0, 32, stride=2), :] = across[:32]
    dealt[pl.ds(1, 32, stride=2), :] = across[32:]
    four_stack[...] = stack(dealt[...])
    load(0).wait()
    load(2).start()
    mode_four(0)
    pl.semaphore_wait(pltpu.get_barrier_semaphore(), len(PLANE) + len(FIBERS))

    def z_copy(chunk, half, d):
        device, peer = plane_peer(d)
        return remote(
            outgoing.at[chunk, pl.ds(peer * 256 + half * 128, 128), :],
            incoming.at[chunk, half, pl.ds(me * 128, 128), :],
            z_send.at[chunk, half], z_recv.at[chunk, half], device,
        )

    def z_all(chunk, half):
        block = incoming.at[chunk, half, pl.ds(0, 7 * 128), :]
        return remote(block, block, z_send.at[chunk, half], z_recv.at[chunk, half], plane_peer(1)[0])

    def z_own(chunk, half):
        return pltpu.make_async_copy(
            outgoing.at[chunk, pl.ds(me * 256 + half * 128, 128), :],
            incoming.at[chunk, half, pl.ds(me * 128, 128), :],
            own_sem.at[chunk, half],
        )

    def send_chunk(chunk):
        for half in range(2):
            for d in PLANE:
                z_copy(chunk, half, d).start()
            z_own(chunk, half).start()

    def sent_chunk(chunk):
        for half in range(2):
            z_all(chunk, half).wait_send()

    def f_rows(chunk, half, device):
        return fibers.at[pl.ds((device * CHUNKS + chunk) * 4, 4), half]

    def f_copy(chunk, half, d):
        device, peer = fib_peer(d)
        return remote(contracted.at[chunk, half, peer], f_rows(chunk, half, fib), f_send, f_recv, device)

    def f_all():
        block = fibers.at[pl.ds(0, 15 * CHUNKS * 4)]
        return remote(block, block, f_send, f_recv, fib_peer(1)[0])

    def f_own(chunk, half):
        return pltpu.make_async_copy(contracted.at[chunk, half, fib], f_rows(chunk, half, fib), fib_own_sem.at[chunk, half])

    def two_copy(step):
        return remote(two_own_block, two_all.at[row], two_send, two_recv, (fib, lax.rem(row + step, 4), slab))

    def two_arrived():
        block = two_all.at[pl.ds(0, 3)]
        return remote(block, block, two_send, two_recv, (fib, lax.rem(row + 1, 4), slab))

    def three_copy():
        return remote(three_own_block, three_all.at[slab], three_send, three_recv, (fib, row, 1 - slab))

    def exchange_factors():
        fetch(1).wait()
        fetch(2).wait()
        two_own_block[...] = jnp.concatenate([two[...], two[...]], axis=1)
        across = three[...].T
        nothing = jnp.zeros_like(across)
        mine = jnp.where(slab == 0, 1.0, 0.0)
        block = jnp.concatenate([across * mine, across * (1.0 - mine)], axis=1)
        three_own_block[...] = jnp.concatenate([block] * 4, axis=1)
        for step in range(1, 4):
            two_copy(step).start()
        three_copy().start()
        two_all[row] = two_own_block[...]
        three_all[slab] = three_own_block[...]

    def widen():
        two_arrived().wait_recv()
        three_copy().wait_recv()
        high, low = split(three_all[0] + three_all[1])
        lanes = lax.broadcasted_iota(jnp.int32, (64, 256), 1)
        three_stack[...] = jnp.where(lanes < 128, high.astype(F32), low.astype(F32)).astype(BF16)
        left = left_half((32, 128))
        nothing = jnp.zeros((32, 128), F32)
        for z in range(4):
            block = two_all[z]
            sides = (jnp.where(left, block, 0.0), jnp.where(left, 0.0, block))
            pieces = []
            for i in range(4):
                tiles = [nothing, nothing]
                tiles[i // 2] = sides[i % 2]
                pieces.append(jnp.concatenate(tiles, axis=1))
            high, low = split(jnp.concatenate(pieces, axis=0))
            wide_high[z] = high
            wide_low[z] = low
        fetch(3).wait()
        one_stack[...] = halves(one[...])

    def modes_three_two(chunk, half):
        def rank(r):
            parts = []
            for z in range(4):
                pieces = [incoming[chunk, half, pl.ds((2 * z + c) * 128 + r * 32, 32), :] for c in range(2)]
                high, low = split(jnp.concatenate(pieces, axis=0))
                parts.append(jnp.concatenate([high, low, high, low], axis=0))
            out = dot(three_stack[...], jnp.concatenate(parts, axis=1))
            for z in range(4):
                halfway[z, pl.ds(r, 64, stride=4), :] = out[:, z * 128 : (z + 1) * 128]

        each(0, 4, rank, unroll=2)

        def rows(block):
            at = pl.ds(pl.multiple_of(block * 128, 128), 128)
            total = jnp.zeros((128, 256), F32)
            for z in range(4):
                high, low = split(halfway[z, at, :])
                both = dot(jnp.concatenate([high, low], axis=0), wide_high[z])
                total = total + both[:128] + both[128:] + dot(high, wide_low[z])
            left = left_half((8, 128))
            for f in range(8):
                for t in range(2):
                    lower = total[f * 16 : f * 16 + 8, t * 128 : t * 128 + 128]
                    upper = total[f * 16 + 8 : f * 16 + 16, t * 128 : t * 128 + 128]
                    contracted[chunk, half, block * 8 + f, 2 * t] = jnp.where(left, lower, pltpu.roll(upper, 64, 1))
                    contracted[chunk, half, block * 8 + f, 2 * t + 1] = jnp.where(left, pltpu.roll(lower, 64, 1), upper)

        each(0, 2, rows)

    def advance(turn):
        @pl.when(turn < CHUNKS)
        def _():
            @pl.when(turn >= 2)
            def _():
                sent_chunk(turn - 2)

            send_chunk(turn)

        @pl.when(turn == 0)
        def _():
            exchange_factors()

        @pl.when(turn + 1 < CHUNKS)
        def _():
            load(turn + 1).wait()

            @pl.when(turn + 3 < CHUNKS)
            def _():
                load(turn + 3).start()

            mode_four(turn + 1)

        @pl.when(turn == 0)
        def _():
            widen()

        @pl.when(turn >= LAG)
        def _():
            chunk = turn - LAG

            def one_half(half):
                z_own(chunk, half).wait()
                z_all(chunk, half).wait_recv()
                modes_three_two(chunk, half)
                for d in FIBERS:
                    f_copy(chunk, half, d).start()
                f_own(chunk, half).start()

            each(0, 2, one_half)

    each(0, CHUNKS + LAG, advance)
    each(CHUNKS - 2, CHUNKS, sent_chunk)
    partial[...] = jnp.zeros_like(partial)
    each(0, CHUNKS, lambda chunk: each(0, 2, lambda half: f_own(chunk, half).wait()))
    f_all().wait_recv()
    fiber_rows = fibers.reshape(8192, 128)

    def cross(step):
        block = jnp.concatenate([fiber_rows[pl.ds(2 * step + n, 512, stride=16), :] for n in range(2)], axis=1)
        high, low = split(block)
        fibers_high[step] = high
        fibers_low[step] = low
        both = dot(one_stack[...], high)
        both_parts = halves(both[:64] + both[64:] + dot(one_stack[:64, :], low))
        back = dot_nt(both_parts, high)
        partial[...] += back[:64] + back[64:] + dot_nt(both_parts[:64], low)

    each(0, 8, cross, unroll=2)

    def rs_copy(d):
        device, peer = plane_peer(d)
        return remote(partial.at[pl.ds(peer * 8, 8), :], scattered.at[me], rs_send, rs_recv, device)

    def ar_copy(d):
        return remote(shared.at[fib], shared.at[fib], ar_send, ar_recv, fib_peer(d)[0])

    def ag_copy(d):
        mine = state.at[pl.ds(me * 8, 8), pl.ds(0, 512)]
        return remote(mine, mine, ag_send, ag_recv, plane_peer(d)[0])

    def rs_all():
        block = scattered.at[pl.ds(0, 7)]
        return remote(block, block, rs_send, rs_recv, plane_peer(1)[0])

    def ar_all():
        block = shared.at[pl.ds(0, 15)]
        return remote(block, block, ar_send, ar_recv, fib_peer(1)[0])

    def ag_all():
        block = state.at[pl.ds(0, 56), pl.ds(0, 512)]
        return remote(block, block, ag_send, ag_recv, plane_peer(1)[0])

    for d in PLANE:
        rs_copy(d).start()
    scattered[me] = partial[pl.ds(pl.multiple_of(me * 8, 8), 8), :]
    rs_all().wait_recv()
    shared[fib] = jnp.sum(scattered[...], axis=0)
    for d in FIBERS:
        ar_copy(d).start()
    ar_all().wait_recv()
    state[pl.ds(pl.multiple_of(me * 8, 8), 8), pl.ds(0, 512)] = jnp.sum(shared[...], axis=0)
    for d in PLANE:
        ag_copy(d).start()
    ag_all().wait_recv()

    one_stack[...] = halves(state[:, :512])

    def project(n):
        p_low, middle = n // 4, n % 4
        step = (middle // 2) * 4 + p_low * 2 + middle % 2
        both = dot(one_stack[...], fibers_high[step])
        out = both[:64] + both[64:] + dot(one_stack[:64, :], fibers_low[step])
        across = jnp.concatenate([out[:, :128], out[:, 128:]], axis=0).T
        for high in range(2):
            for peer in range(8):
                start = high * 64 + peer * 8
                at = pl.ds(pl.multiple_of(middle * 16 + high * 8, 8), 8)
                core_out[peer, p_low, at, :] = across[start : start + 8, :]

    each(0, 8, project, unroll=2)

    def core_copy(d):
        device, peer = plane_peer(d)
        return remote(core_out.at[peer], core_in.at[:, me], core_send, core_recv, device)

    def core_all():
        block = core_in.at[:, pl.ds(0, 7)]
        return remote(block, block, core_send, core_recv, plane_peer(1)[0])

    for d in PLANE:
        core_copy(d).start()
    for p_low in range(2):
        core_in[p_low, me] = core_out[me, p_low]

    ag_all().wait_send()
    lanes = lax.broadcasted_iota(jnp.int32, (64, 128), 1)
    state[:, 512:] = jnp.where(lanes == lax.broadcasted_iota(jnp.int32, (64, 128), 0), 1.0, 0.0)

    def cholesky_qr(repeat):
        rows = state[:, :512]
        crossed = lax.dot_general(rows, rows, (((1,), (1,)), ((), ())), precision=HIGHEST, preferred_element_type=F32)
        state[...] = jnp.dot(eliminate(crossed), state[...], precision=HIGHEST, preferred_element_type=F32)

    each(0, 2, cholesky_qr)
    updated[...] = state[:, :512]
    inverse = state[:, 512:]
    weights = halves(jnp.concatenate([inverse, pltpu.roll(inverse, 64, 1)], axis=0))

    core_all().wait_recv()
    core_rows = core_in.reshape(1024, 128)

    def finish(n):
        start = (n % 2) * 512 + (n // 2) * 8
        block = jnp.concatenate([core_rows[pl.ds(start + q, 32, stride=16), :] for q in range(8)], axis=0)
        high, low = split(block)
        both = dot_nt(weights, high)
        out = both[:128] + both[128:] + dot_nt(weights[:128], low)
        for q in range(8):
            tile, off = q // 4, (q % 4) * 32
            lower = out[:64, tile * 128 : tile * 128 + 128]
            upper = out[64:, tile * 128 : tile * 128 + 128]
            if off:
                lower = pltpu.roll(lower, 128 - off, 1)
            if off != 32:
                upper = pltpu.roll(upper, (160 - off) % 128, 1)
            collected[pl.ds(q * 4 + n, 64, stride=32), :] = jnp.where(lanes < 32, lower, upper)

    each(0, 4, finish)

    core_all().wait_send()
    rs_all().wait_send()
    ar_all().wait_send()
    two_arrived().wait_send()
    three_copy().wait_send()
    f_all().wait_send()


def body(tensor, factor_one, factor_two, factor_three, factor_four):
    vmem = pl.BlockSpec(memory_space=pltpu.VMEM)
    hbm = pl.BlockSpec(memory_space=pl.ANY)
    dma = pltpu.SemaphoreType.DMA
    updated, core = pl.pallas_call(
        kernel,
        out_shape=(jax.ShapeDtypeStruct((64, 512), F32), jax.ShapeDtypeStruct((2048, 128), F32)),
        in_specs=[hbm] * 5,
        out_specs=(vmem, vmem),
        scratch_shapes=[
            pltpu.VMEM((64, 128), F32),
            pltpu.VMEM((32, 64), F32),
            pltpu.VMEM((32, 64), F32),
            pltpu.VMEM((64, 512), F32),
            pltpu.VMEM((64, 128), F32),
            pltpu.VMEM((128, 256), BF16),
            pltpu.VMEM((128, 512), BF16),
            pltpu.VMEM((64, 256), F32),
            pltpu.VMEM((32, 128), F32),
            pltpu.VMEM((3, 4096, 128), F32),
            pltpu.VMEM((CHUNKS, 2048, 128), F32),
            pltpu.VMEM((CHUNKS, 2, 1024, 128), F32),
            pltpu.VMEM((4, 256, 128), F32),
            pltpu.VMEM((CHUNKS, 2, 16, 4, 8, 128), F32),
            pltpu.VMEM((512, 2, 8, 128), F32),
            pltpu.VMEM((4, 32, 128), F32),
            pltpu.VMEM((2, 64, 256), F32),
            pltpu.VMEM((64, 256), BF16),
            pltpu.VMEM((4, 128, 256), BF16),
            pltpu.VMEM((4, 128, 256), BF16),
            pltpu.VMEM((8, 512, 256), BF16),
            pltpu.VMEM((8, 512, 256), BF16),
            pltpu.VMEM((64, 512), F32),
            pltpu.VMEM((8, 8, 512), F32),
            pltpu.VMEM((16, 8, 512), F32),
            pltpu.VMEM((64, 640), F32),
            pltpu.VMEM((8, 2, 64, 128), F32),
            pltpu.VMEM((2, 8, 64, 128), F32),
            dma((3,)), dma((4,)), dma((CHUNKS, 2)), dma((CHUNKS, 2)), dma((CHUNKS, 2)), dma((CHUNKS, 2)), dma(()), dma(()),
            dma(()), dma(()), dma(()), dma(()), dma(()), dma(()), dma(()), dma(()), dma(()), dma(()), dma(()), dma(()),
        ],
        compiler_params=pltpu.CompilerParams(collective_id=0, has_side_effects=True, vmem_limit_bytes=56 * 2**20),
        name="hooi",
    )(tensor.reshape(8, 4096, 128), factor_four.T, factor_three, factor_two, factor_one.T)
    return (updated.T, core[:, :64].reshape(64, 8, 4, 64))


def solution(mesh):
    in_specs = (P("fib", "row", "slab", None), P(), P("row", None), P("slab", None), P())
    out_specs = (P(), P(None, ("row", "slab"), "fib", None))
    return jax.shard_map(body, mesh=mesh, in_specs=in_specs, out_specs=out_specs, check_vma=False)
```

```python
import jax
import jax.numpy as jnp
from jax import lax
from jax.experimental import pallas as pl
from jax.experimental.pallas import tpu as pltpu
from jax.sharding import PartitionSpec as P

HIGHEST = lax.Precision.HIGHEST
MESH = pl.DeviceIdType.MESH
F32 = jnp.float32
BF16 = jnp.bfloat16
CHUNKS = 8
LAG = 2
EARLY = 6
PLANE = tuple(range(1, 8))
FIBERS = tuple(sorted(range(1, 16), key=lambda d: -(min(d // 4, 4 - d // 4) + min(d % 4, 4 - d % 4))))


def split(x):
    high = x.astype(BF16)
    return high, (x - high.astype(F32)).astype(BF16)


def dot(a, b):
    return jnp.dot(a, b, preferred_element_type=F32)


def dot_nt(a, b):
    return lax.dot_general(a, b, (((1,), (1,)), ((), ())), preferred_element_type=F32)


def place():
    return lax.axis_index("fib"), lax.axis_index("row"), lax.axis_index("slab")


def plane_peer(d):
    fib, row, slab = place()
    row, slab = lax.rem(row + d // 2, 4), lax.rem(slab + d % 2, 2)
    return (fib, row, slab), row * 2 + slab


def fib_peer(d):
    fib, row, slab = place()
    fib = lax.rem(fib // 4 + d // 4, 4) * 4 + lax.rem(fib % 4 + d % 4, 4)
    return (fib, row, slab), fib


def each(lower, upper, step, unroll=1):
    def run(index, carry):
        step(index)
        return carry

    lax.fori_loop(lower, upper, run, 0, unroll=unroll)


def remote(src, dst, send, recv, device):
    return pltpu.make_async_remote_copy(
        src_ref=src, dst_ref=dst, send_sem=send, recv_sem=recv, device_id=device, device_id_type=MESH
    )


def greet():
    barrier = pltpu.get_barrier_semaphore()
    for d in PLANE:
        pl.semaphore_signal(barrier, inc=1, device_id=plane_peer(d)[0], device_id_type=MESH)
    for d in FIBERS:
        pl.semaphore_signal(barrier, inc=1, device_id=fib_peer(d)[0], device_id_type=MESH)


def stack(x):
    high, low = split(x)
    return jnp.concatenate([jnp.concatenate([high, high], 1), jnp.concatenate([low, low], 1)], 0)


def left_half(shape):
    return lax.broadcasted_iota(jnp.int32, shape, 1) < 64


def halves(x):
    return jnp.concatenate(split(x), axis=0)


def eliminate(crossed, group=4):
    lane = lax.broadcasted_iota(jnp.int32, (8, 64), 1)
    row = lax.broadcasted_iota(jnp.int32, (8, 64), 0)
    below = lax.broadcasted_iota(jnp.int32, (8, 128), 0)
    blocks = [
        jnp.concatenate([crossed[8 * b : 8 * b + 8], jnp.where(lane == row + 8 * b, 1.0, 0.0)], axis=1) for b in range(8)
    ]

    def spread(x):
        return jnp.broadcast_to(x, (8, 128))

    for first in range(0, 64, group):
        b, k = first // 8, first % 8
        here = blocks[b]
        corner = [[spread(here[k + m : k + m + 1, first + n : first + n + 1]) for n in range(m + 1)] for m in range(group)]
        below_diagonal = [[None] * group for m in range(group)]
        scale = [None] * group
        for m in range(group):
            square = corner[m][m]
            for n in range(m):
                square = square - below_diagonal[m][n] * below_diagonal[m][n]
            scale[m] = lax.rsqrt(square)
            for other in range(m + 1, group):
                entry = corner[other][m]
                for n in range(m):
                    entry = entry - below_diagonal[other][n] * below_diagonal[m][n]
                below_diagonal[other][m] = entry * scale[m]

        def forward(parts):
            done = []
            for m in range(group):
                part = parts[m]
                for n in range(m):
                    part = part - done[n] * below_diagonal[m][n]
                done.append(part * scale[m])
            return done

        pivots = forward([spread(here[k + m : k + m + 1, :]) for m in range(group)])
        for at in range(b, 8):
            if at == b and k + group == 8:
                update = here
            else:
                columns = forward([spread(blocks[at][:, first + m : first + m + 1]) for m in range(group)])
                update = blocks[at]
                for m in range(group):
                    update = update - columns[m] * pivots[m]
            if at == b:
                update = jnp.where(below < k, here, update)
                for m in range(group):
                    update = jnp.where(below == k + m, pivots[m], update)
            blocks[at] = update
    return jnp.concatenate(blocks, axis=0)[:, 64:]


def kernel(
    tensor, four_hbm, three_hbm, two_hbm, one_hbm, updated, collected,
    four, three, two, one, dealt, four_stack, one_stack, three_own_block, two_own_block,
    staged, outgoing, incoming, halfway, contracted, fibers, two_all, three_all, three_stack, wide_high, wide_low,
    fibers_high, fibers_low, order, crossed, partial, scattered, shared, state, core_out, core_in,
    load_sem, factor_sem, own_sem, z_send, z_recv, fib_own_sem, f_send, f_recv,
    two_send, two_recv, three_send, three_recv, rs_send, rs_recv, ar_send, ar_recv, ag_send, ag_recv, core_send, core_recv,
):
    fib, row, slab = place()
    me = row * 2 + slab

    def load(chunk):
        return pltpu.make_async_copy(tensor.at[chunk], staged.at[chunk % 3], load_sem.at[chunk % 3])

    def mode_four(chunk):
        slot = chunk % 3

        def two_steps(pair):
            first = staged[slot, pl.ds(2 * pair, 128, stride=32), :]
            second = staged[slot, pl.ds(2 * pair + 1, 128, stride=32), :]
            high, low = split(jnp.concatenate([first, second], axis=0))
            out = dot_nt(four_stack[...], jnp.concatenate([high, low], axis=1))
            out = out[:64] + out[64:]
            outgoing[chunk, pl.ds(2 * pair, 64, stride=32), :] = out[:, :128]
            outgoing[chunk, pl.ds(2 * pair + 1, 64, stride=32), :] = out[:, 128:]

        each(0, 16, two_steps, unroll=2)

    def fetch(n):
        source, target = ((four_hbm, four), (three_hbm, three), (two_hbm, two), (one_hbm, one))[n]
        return pltpu.make_async_copy(source, target, factor_sem.at[n])

    fetch(0).start()
    load(0).start()
    load(1).start()
    for n in range(1, 4):
        fetch(n).start()
    greet()
    fetch(0).wait()
    across = four[...]
    dealt[pl.ds(0, 32, stride=2), :] = across[:32]
    dealt[pl.ds(1, 32, stride=2), :] = across[32:]
    four_stack[...] = stack(dealt[...])
    load(0).wait()
    load(2).start()
    mode_four(0)
    pl.semaphore_wait(pltpu.get_barrier_semaphore(), len(PLANE) + len(FIBERS))

    def z_copy(chunk, half, d):
        device, peer = plane_peer(d)
        return remote(
            outgoing.at[chunk, pl.ds(peer * 256 + half * 128, 128), :],
            incoming.at[chunk, half, pl.ds(me * 128, 128), :],
            z_send.at[chunk, half], z_recv.at[chunk, half], device,
        )

    def z_all(chunk, half):
        block = incoming.at[chunk, half, pl.ds(0, 7 * 128), :]
        return remote(block, block, z_send.at[chunk, half], z_recv.at[chunk, half], plane_peer(1)[0])

    def z_own(chunk, half):
        return pltpu.make_async_copy(
            outgoing.at[chunk, pl.ds(me * 256 + half * 128, 128), :],
            incoming.at[chunk, half, pl.ds(me * 128, 128), :],
            own_sem.at[chunk, half],
        )

    def send_chunk(chunk):
        for half in range(2):
            for d in PLANE:
                z_copy(chunk, half, d).start()
            z_own(chunk, half).start()

    def sent_chunk(chunk):
        for half in range(2):
            z_all(chunk, half).wait_send()

    def f_rows(chunk, half, device):
        return fibers.at[chunk, device, :, half]

    def f_copy(chunk, half, d):
        device, peer = fib_peer(d)
        return remote(contracted.at[chunk, half, peer], f_rows(chunk, half, fib), f_send.at[chunk // EARLY], f_recv.at[chunk // EARLY], device)

    def f_all(late):
        chunks = pl.ds(EARLY, CHUNKS - EARLY) if late else pl.ds(0, EARLY)
        block = fibers.at[chunks, pl.ds(0, 15)]
        return remote(block, block, f_send.at[late], f_recv.at[late], fib_peer(1)[0])

    def f_own(chunk, half):
        return pltpu.make_async_copy(contracted.at[chunk, half, fib], f_rows(chunk, half, fib), fib_own_sem.at[chunk, half])

    def two_copy(step):
        return remote(two_own_block, two_all.at[row], two_send, two_recv, (fib, lax.rem(row + step, 4), slab))

    def two_arrived():
        block = two_all.at[pl.ds(0, 3)]
        return remote(block, block, two_send, two_recv, (fib, lax.rem(row + 1, 4), slab))

    def three_copy():
        return remote(three_own_block, three_all.at[slab], three_send, three_recv, (fib, row, 1 - slab))

    def exchange_factors():
        fetch(1).wait()
        fetch(2).wait()
        two_own_block[...] = jnp.concatenate([two[...], two[...]], axis=1)
        across = three[...].T
        nothing = jnp.zeros_like(across)
        mine = jnp.where(slab == 0, 1.0, 0.0)
        block = jnp.concatenate([across * mine, across * (1.0 - mine)], axis=1)
        three_own_block[...] = jnp.concatenate([block] * 4, axis=1)
        for step in range(1, 4):
            two_copy(step).start()
        three_copy().start()
        two_all[row] = two_own_block[...]
        three_all[slab] = three_own_block[...]

    def widen():
        two_arrived().wait_recv()
        three_copy().wait_recv()
        high, low = split(three_all[0] + three_all[1])
        lanes = lax.broadcasted_iota(jnp.int32, (64, 256), 1)
        three_stack[...] = jnp.where(lanes < 128, high.astype(F32), low.astype(F32)).astype(BF16)
        left = left_half((32, 128))
        nothing = jnp.zeros((32, 128), F32)
        for z in range(4):
            block = two_all[z]
            sides = (jnp.where(left, block, 0.0), jnp.where(left, 0.0, block))
            pieces = []
            for i in range(4):
                tiles = [nothing, nothing]
                tiles[i // 2] = sides[i % 2]
                pieces.append(jnp.concatenate(tiles, axis=1))
            high, low = split(jnp.concatenate(pieces, axis=0))
            wide_high[z] = high
            wide_low[z] = low
        fetch(3).wait()
        natural = lax.broadcasted_iota(jnp.int32, (512, 512), 1)
        there = ((natural >> 2) & 7) * 64 + (natural >> 5) * 4 + (natural & 3)
        same = there == lax.broadcasted_iota(jnp.int32, (512, 512), 0)
        order[...] = jnp.where(same, 1.0, 0.0).astype(BF16)
        one_stack[...] = dot_nt(halves(one[...]), order[...]).astype(BF16)

    def modes_three_two(chunk, half):
        def rank(r):
            parts = []
            for z in range(4):
                pieces = [incoming[chunk, half, pl.ds((2 * z + c) * 128 + r * 32, 32), :] for c in range(2)]
                high, low = split(jnp.concatenate(pieces, axis=0))
                parts.append(jnp.concatenate([high, low, high, low], axis=0))
            out = dot(three_stack[...], jnp.concatenate(parts, axis=1))
            for z in range(4):
                halfway[z, pl.ds(r, 64, stride=4), :] = out[:, z * 128 : (z + 1) * 128]

        each(0, 4, rank, unroll=2)

        def rows(block):
            at = pl.ds(pl.multiple_of(block * 128, 128), 128)
            total = jnp.zeros((128, 256), F32)
            for z in range(4):
                high, low = split(halfway[z, at, :])
                both = dot(jnp.concatenate([high, low], axis=0), wide_high[z])
                total = total + both[:128] + both[128:] + dot(high, wide_low[z])
            left = left_half((8, 128))
            for f in range(8):
                for t in range(2):
                    lower = total[f * 16 : f * 16 + 8, t * 128 : t * 128 + 128]
                    upper = total[f * 16 + 8 : f * 16 + 16, t * 128 : t * 128 + 128]
                    contracted[chunk, half, block * 8 + f, 2 * t] = jnp.where(left, lower, pltpu.roll(upper, 64, 1))
                    contracted[chunk, half, block * 8 + f, 2 * t + 1] = jnp.where(left, pltpu.roll(lower, 64, 1), upper)

        each(0, 2, rows)

    def advance(turn):
        @pl.when(turn < CHUNKS)
        def _():
            @pl.when(turn >= 2)
            def _():
                sent_chunk(turn - 2)

            send_chunk(turn)

        @pl.when(turn == 0)
        def _():
            exchange_factors()

        @pl.when(turn + 1 < CHUNKS)
        def _():
            load(turn + 1).wait()

            @pl.when(turn + 3 < CHUNKS)
            def _():
                load(turn + 3).start()

            mode_four(turn + 1)

        @pl.when(turn == 0)
        def _():
            widen()

        @pl.when(turn >= LAG)
        def _():
            chunk = turn - LAG

            def one_half(half):
                z_own(chunk, half).wait()
                z_all(chunk, half).wait_recv()
                modes_three_two(chunk, half)
                for d in FIBERS:
                    f_copy(chunk, half, d).start()
                f_own(chunk, half).start()

            each(0, 2, one_half)

    each(0, CHUNKS + LAG, advance)
    each(CHUNKS - 2, CHUNKS, sent_chunk)
    partial[...] = jnp.zeros_like(partial)
    each(0, EARLY, lambda chunk: each(0, 2, lambda half: f_own(chunk, half).wait()))
    f_all(0).wait_recv()
    fiber_rows = fibers.reshape(8192, 128)

    def cross(step, first, count):
        block = [fiber_rows[pl.ds(first * 16 + 2 * step + n, count, stride=16), :] for n in range(2)]
        high, low = split(jnp.concatenate(block, axis=1))
        fibers_high[step, pl.ds(first, count), :] = high
        fibers_low[step, pl.ds(first, count), :] = low
        both = dot(one_stack[:, first : first + count], high)
        return both[:64] + both[64:] + dot(one_stack[:64, first : first + count], low)

    def cross_early(step):
        crossed[step] = cross(step, 0, EARLY * 64)

    each(0, 8, cross_early, unroll=2)
    each(EARLY, CHUNKS, lambda chunk: each(0, 2, lambda half: f_own(chunk, half).wait()))
    f_all(1).wait_recv()

    def cross_late(step):
        parts = halves(crossed[step] + cross(step, EARLY * 64, (CHUNKS - EARLY) * 64))
        back = dot_nt(parts, fibers_high[step])
        partial[...] += back[:64] + back[64:] + dot_nt(parts[:64], fibers_low[step])

    each(0, 8, cross_late, unroll=2)

    def rs_copy(d):
        device, peer = plane_peer(d)
        return remote(partial.at[pl.ds(peer * 8, 8), :], scattered.at[me], rs_send, rs_recv, device)

    def ar_copy(d):
        return remote(shared.at[fib], shared.at[fib], ar_send, ar_recv, fib_peer(d)[0])

    def ag_copy(d):
        mine = state.at[pl.ds(me * 8, 8), pl.ds(0, 512)]
        return remote(mine, mine, ag_send, ag_recv, plane_peer(d)[0])

    def rs_all():
        block = scattered.at[pl.ds(0, 7)]
        return remote(block, block, rs_send, rs_recv, plane_peer(1)[0])

    def ar_all():
        block = shared.at[pl.ds(0, 15)]
        return remote(block, block, ar_send, ar_recv, fib_peer(1)[0])

    def ag_all():
        block = state.at[pl.ds(0, 56), pl.ds(0, 512)]
        return remote(block, block, ag_send, ag_recv, plane_peer(1)[0])

    for d in PLANE:
        rs_copy(d).start()
    scattered[me] = partial[pl.ds(pl.multiple_of(me * 8, 8), 8), :]
    rs_all().wait_recv()
    shared[fib] = jnp.sum(scattered[...], axis=0)
    for d in FIBERS:
        ar_copy(d).start()
    ar_all().wait_recv()
    state[pl.ds(pl.multiple_of(me * 8, 8), 8), pl.ds(0, 512)] = jnp.sum(shared[...], axis=0)
    for d in PLANE:
        ag_copy(d).start()
    ag_all().wait_recv()

    one_stack[...] = halves(state[:, :512])

    def project(n):
        p_low, middle = n // 4, n % 4
        step = (middle // 2) * 4 + p_low * 2 + middle % 2
        both = dot(one_stack[...], fibers_high[step])
        out = both[:64] + both[64:] + dot(one_stack[:64, :], fibers_low[step])
        across = jnp.concatenate([out[:, :128], out[:, 128:]], axis=0).T
        for high in range(2):
            for peer in range(8):
                start = high * 64 + peer * 8
                at = pl.ds(pl.multiple_of(middle * 16 + high * 8, 8), 8)
                core_out[peer, p_low, at, :] = across[start : start + 8, :]

    def core_copy(p_low, d):
        device, peer = plane_peer(d)
        return remote(core_out.at[peer, p_low], core_in.at[p_low, me], core_send.at[p_low], core_recv.at[p_low], device)

    def core_all(p_low):
        block = core_in.at[p_low, pl.ds(0, 7)]
        return remote(block, block, core_send.at[p_low], core_recv.at[p_low], plane_peer(1)[0])

    def project_some(p_low):
        each(p_low * 4, p_low * 4 + 4, project, unroll=2)
        for d in PLANE:
            core_copy(p_low, d).start()
        core_in[p_low, me] = core_out[me, p_low]

    for p_low in range(2):
        project_some(p_low)
    ag_all().wait_send()
    lanes = lax.broadcasted_iota(jnp.int32, (64, 128), 1)
    state[:, 512:] = jnp.where(lanes == lax.broadcasted_iota(jnp.int32, (64, 128), 0), 1.0, 0.0)

    def cholesky_qr(repeat):
        rows = state[:, :512]
        crossed = lax.dot_general(rows, rows, (((1,), (1,)), ((), ())), precision=HIGHEST, preferred_element_type=F32)
        state[...] = jnp.dot(eliminate(crossed), state[...], precision=HIGHEST, preferred_element_type=F32)

    each(0, 2, cholesky_qr)
    rows = state[:, :512]
    high = rows.astype(BF16)
    rest = rows - high.astype(F32)
    middle, low = split(rest)
    moved = dot(jnp.concatenate([high, middle, low], axis=0), order[...])
    updated[...] = moved[:64] + (moved[64:128] + moved[128:])
    inverse = state[:, 512:]
    weights = halves(jnp.concatenate([inverse, pltpu.roll(inverse, 64, 1)], axis=0))

    core_all(0).wait_recv()
    core_all(1).wait_recv()
    core_rows = core_in.reshape(1024, 128)

    def finish(n):
        start = (n % 2) * 512 + (n // 2) * 8
        block = jnp.concatenate([core_rows[pl.ds(start + q, 32, stride=16), :] for q in range(8)], axis=0)
        high, low = split(block)
        both = dot_nt(weights, high)
        out = both[:128] + both[128:] + dot_nt(weights[:128], low)
        for q in range(8):
            tile, off = q // 4, (q % 4) * 32
            lower = out[:64, tile * 128 : tile * 128 + 128]
            upper = out[64:, tile * 128 : tile * 128 + 128]
            if off:
                lower = pltpu.roll(lower, 128 - off, 1)
            if off != 32:
                upper = pltpu.roll(upper, (160 - off) % 128, 1)
            collected[pl.ds(q * 4 + n, 64, stride=32), :] = jnp.where(lanes < 32, lower, upper)

    each(0, 4, finish)

    core_all(0).wait_send()
    core_all(1).wait_send()
    rs_all().wait_send()
    ar_all().wait_send()
    two_arrived().wait_send()
    three_copy().wait_send()
    f_all(0).wait_send()
    f_all(1).wait_send()


def body(tensor, factor_one, factor_two, factor_three, factor_four):
    vmem = pl.BlockSpec(memory_space=pltpu.VMEM)
    hbm = pl.BlockSpec(memory_space=pl.ANY)
    dma = pltpu.SemaphoreType.DMA
    updated, core = pl.pallas_call(
        kernel,
        out_shape=(jax.ShapeDtypeStruct((64, 512), F32), jax.ShapeDtypeStruct((2048, 128), F32)),
        in_specs=[hbm] * 5,
        out_specs=(vmem, vmem),
        scratch_shapes=[
            pltpu.VMEM((64, 128), F32),
            pltpu.VMEM((32, 64), F32),
            pltpu.VMEM((32, 64), F32),
            pltpu.VMEM((64, 512), F32),
            pltpu.VMEM((64, 128), F32),
            pltpu.VMEM((128, 256), BF16),
            pltpu.VMEM((128, 512), BF16),
            pltpu.VMEM((64, 256), F32),
            pltpu.VMEM((32, 128), F32),
            pltpu.VMEM((3, 4096, 128), F32),
            pltpu.VMEM((CHUNKS, 2048, 128), F32),
            pltpu.VMEM((CHUNKS, 2, 1024, 128), F32),
            pltpu.VMEM((4, 256, 128), F32),
            pltpu.VMEM((CHUNKS, 2, 16, 4, 8, 128), F32),
            pltpu.VMEM((CHUNKS, 16, 4, 2, 8, 128), F32),
            pltpu.VMEM((4, 32, 128), F32),
            pltpu.VMEM((2, 64, 256), F32),
            pltpu.VMEM((64, 256), BF16),
            pltpu.VMEM((4, 128, 256), BF16),
            pltpu.VMEM((4, 128, 256), BF16),
            pltpu.VMEM((8, 512, 256), BF16),
            pltpu.VMEM((8, 512, 256), BF16),
            pltpu.VMEM((512, 512), BF16),
            pltpu.VMEM((8, 64, 256), F32),
            pltpu.VMEM((64, 512), F32),
            pltpu.VMEM((8, 8, 512), F32),
            pltpu.VMEM((16, 8, 512), F32),
            pltpu.VMEM((64, 640), F32),
            pltpu.VMEM((8, 2, 64, 128), F32),
            pltpu.VMEM((2, 8, 64, 128), F32),
            dma((3,)), dma((4,)), dma((CHUNKS, 2)), dma((CHUNKS, 2)), dma((CHUNKS, 2)), dma((CHUNKS, 2)), dma((2,)), dma((2,)),
            dma(()), dma(()), dma(()), dma(()), dma(()), dma(()), dma(()), dma(()), dma(()), dma(()), dma((2,)), dma((2,)),
        ],
        compiler_params=pltpu.CompilerParams(collective_id=0, has_side_effects=True, vmem_limit_bytes=56 * 2**20),
        name="hooi",
    )(tensor.reshape(8, 4096, 128), factor_four.T, factor_three, factor_two, factor_one.T)
    return (updated.T, core[:, :64].reshape(64, 8, 4, 64))


def solution(mesh):
    in_specs = (P("fib", "row", "slab", None), P(), P("row", None), P("slab", None), P())
    out_specs = (P(), P(None, ("row", "slab"), "fib", None))
    return jax.shard_map(body, mesh=mesh, in_specs=in_specs, out_specs=out_specs, check_vma=False)
```

```python
import jax
import jax.numpy as jnp
from jax import lax
from jax.experimental import pallas as pl
from jax.experimental.pallas import tpu as pltpu
from jax.sharding import PartitionSpec as P

HIGHEST = lax.Precision.HIGHEST
MESH = pl.DeviceIdType.MESH
F32 = jnp.float32
BF16 = jnp.bfloat16
CHUNKS = 8
LAG = 2
EARLY = 7
PLANE = tuple(range(1, 8))
FIBERS = tuple(sorted(range(1, 16), key=lambda d: -(min(d // 4, 4 - d // 4) + min(d % 4, 4 - d % 4))))


def split(x):
    high = x.astype(BF16)
    return high, (x - high.astype(F32)).astype(BF16)


def dot(a, b):
    return jnp.dot(a, b, preferred_element_type=F32)


def dot_nt(a, b):
    return lax.dot_general(a, b, (((1,), (1,)), ((), ())), preferred_element_type=F32)


def place():
    return lax.axis_index("fib"), lax.axis_index("row"), lax.axis_index("slab")


def plane_peer(d):
    fib, row, slab = place()
    row, slab = lax.rem(row + d // 2, 4), lax.rem(slab + d % 2, 2)
    return (fib, row, slab), row * 2 + slab


def fib_peer(d):
    fib, row, slab = place()
    fib = lax.rem(fib // 4 + d // 4, 4) * 4 + lax.rem(fib % 4 + d % 4, 4)
    return (fib, row, slab), fib


def each(lower, upper, step, unroll=1):
    def run(index, carry):
        step(index)
        return carry

    lax.fori_loop(lower, upper, run, 0, unroll=unroll)


def remote(src, dst, send, recv, device):
    return pltpu.make_async_remote_copy(
        src_ref=src, dst_ref=dst, send_sem=send, recv_sem=recv, device_id=device, device_id_type=MESH
    )


def greet():
    barrier = pltpu.get_barrier_semaphore()
    for d in PLANE:
        pl.semaphore_signal(barrier, inc=1, device_id=plane_peer(d)[0], device_id_type=MESH)
    for d in FIBERS:
        pl.semaphore_signal(barrier, inc=1, device_id=fib_peer(d)[0], device_id_type=MESH)


def stack(x):
    high, low = split(x)
    return jnp.concatenate([jnp.concatenate([high, high], 1), jnp.concatenate([low, low], 1)], 0)


def left_half(shape):
    return lax.broadcasted_iota(jnp.int32, shape, 1) < 64


def halves(x):
    return jnp.concatenate(split(x), axis=0)


def eliminate(crossed, group=4):
    lane = lax.broadcasted_iota(jnp.int32, (8, 64), 1)
    row = lax.broadcasted_iota(jnp.int32, (8, 64), 0)
    below = lax.broadcasted_iota(jnp.int32, (8, 128), 0)
    blocks = [
        jnp.concatenate([crossed[8 * b : 8 * b + 8], jnp.where(lane == row + 8 * b, 1.0, 0.0)], axis=1) for b in range(8)
    ]

    def spread(x):
        return jnp.broadcast_to(x, (8, 128))

    for first in range(0, 64, group):
        b, k = first // 8, first % 8
        here = blocks[b]
        corner = [[spread(here[k + m : k + m + 1, first + n : first + n + 1]) for n in range(m + 1)] for m in range(group)]
        below_diagonal = [[None] * group for m in range(group)]
        scale = [None] * group
        for m in range(group):
            square = corner[m][m]
            for n in range(m):
                square = square - below_diagonal[m][n] * below_diagonal[m][n]
            scale[m] = lax.rsqrt(square)
            for other in range(m + 1, group):
                entry = corner[other][m]
                for n in range(m):
                    entry = entry - below_diagonal[other][n] * below_diagonal[m][n]
                below_diagonal[other][m] = entry * scale[m]

        def forward(parts):
            done = []
            for m in range(group):
                part = parts[m]
                for n in range(m):
                    part = part - done[n] * below_diagonal[m][n]
                done.append(part * scale[m])
            return done

        pivots = forward([spread(here[k + m : k + m + 1, :]) for m in range(group)])
        for at in range(b, 8):
            if at == b and k + group == 8:
                update = here
            else:
                columns = forward([spread(blocks[at][:, first + m : first + m + 1]) for m in range(group)])
                update = blocks[at]
                for m in range(group):
                    update = update - columns[m] * pivots[m]
            if at == b:
                update = jnp.where(below < k, here, update)
                for m in range(group):
                    update = jnp.where(below == k + m, pivots[m], update)
            blocks[at] = update
    return jnp.concatenate(blocks, axis=0)[:, 64:]


def kernel(
    tensor, four_hbm, three_hbm, two_hbm, one_hbm, updated, inverse, received,
    four, three, two, one, dealt, four_stack, one_stack, three_own_block, two_own_block,
    staged, outgoing, incoming, halfway, contracted, fibers, two_all, three_all, three_stack, wide_high, wide_low,
    fibers_high, fibers_low, order, crossed, partial, scattered, shared, state, core_out, core_in,
    load_sem, factor_sem, own_sem, z_send, z_recv, fib_own_sem, f_send, f_recv,
    two_send, two_recv, three_send, three_recv, rs_send, rs_recv, ar_send, ar_recv, ag_send, ag_recv, core_send, core_recv, out_sem,
):
    fib, row, slab = place()
    me = row * 2 + slab

    def load(chunk):
        return pltpu.make_async_copy(tensor.at[chunk], staged.at[chunk % 3], load_sem.at[chunk % 3])

    def mode_four(chunk):
        slot = chunk % 3

        def two_steps(pair):
            first = staged[slot, pl.ds(2 * pair, 128, stride=32), :]
            second = staged[slot, pl.ds(2 * pair + 1, 128, stride=32), :]
            high, low = split(jnp.concatenate([first, second], axis=0))
            out = dot_nt(four_stack[...], jnp.concatenate([high, low], axis=1))
            out = out[:64] + out[64:]
            outgoing[chunk, pl.ds(2 * pair, 64, stride=32), :] = out[:, :128]
            outgoing[chunk, pl.ds(2 * pair + 1, 64, stride=32), :] = out[:, 128:]

        each(0, 16, two_steps, unroll=2)

    def fetch(n):
        source, target = ((four_hbm, four), (three_hbm, three), (two_hbm, two), (one_hbm, one))[n]
        return pltpu.make_async_copy(source, target, factor_sem.at[n])

    fetch(0).start()
    load(0).start()
    load(1).start()
    for n in range(1, 4):
        fetch(n).start()
    greet()
    fetch(0).wait()
    across = four[...]
    dealt[pl.ds(0, 32, stride=2), :] = across[:32]
    dealt[pl.ds(1, 32, stride=2), :] = across[32:]
    four_stack[...] = stack(dealt[...])
    load(0).wait()
    load(2).start()
    mode_four(0)
    pl.semaphore_wait(pltpu.get_barrier_semaphore(), len(PLANE) + len(FIBERS))

    def z_copy(chunk, half, d):
        device, peer = plane_peer(d)
        return remote(
            outgoing.at[chunk, pl.ds(peer * 256 + half * 128, 128), :],
            incoming.at[chunk, half, pl.ds(me * 128, 128), :],
            z_send.at[chunk, half], z_recv.at[chunk, half], device,
        )

    def z_all(chunk, half):
        block = incoming.at[chunk, half, pl.ds(0, 7 * 128), :]
        return remote(block, block, z_send.at[chunk, half], z_recv.at[chunk, half], plane_peer(1)[0])

    def z_own(chunk, half):
        return pltpu.make_async_copy(
            outgoing.at[chunk, pl.ds(me * 256 + half * 128, 128), :],
            incoming.at[chunk, half, pl.ds(me * 128, 128), :],
            own_sem.at[chunk, half],
        )

    def send_chunk(chunk):
        for half in range(2):
            for d in PLANE:
                z_copy(chunk, half, d).start()
            z_own(chunk, half).start()

    def sent_chunk(chunk):
        for half in range(2):
            z_all(chunk, half).wait_send()

    def f_rows(chunk, half, device):
        return fibers.at[chunk, device, :, half]

    def f_copy(chunk, half, d):
        device, peer = fib_peer(d)
        return remote(contracted.at[chunk, half, peer], f_rows(chunk, half, fib), f_send.at[chunk // EARLY], f_recv.at[chunk // EARLY], device)

    def f_all(late):
        chunks = pl.ds(EARLY, CHUNKS - EARLY) if late else pl.ds(0, EARLY)
        block = fibers.at[chunks, pl.ds(0, 15)]
        return remote(block, block, f_send.at[late], f_recv.at[late], fib_peer(1)[0])

    def f_own(chunk, half):
        return pltpu.make_async_copy(contracted.at[chunk, half, fib], f_rows(chunk, half, fib), fib_own_sem.at[chunk, half])

    def two_copy(step):
        return remote(two_own_block, two_all.at[row], two_send, two_recv, (fib, lax.rem(row + step, 4), slab))

    def two_arrived():
        block = two_all.at[pl.ds(0, 3)]
        return remote(block, block, two_send, two_recv, (fib, lax.rem(row + 1, 4), slab))

    def three_copy():
        return remote(three_own_block, three_all.at[slab], three_send, three_recv, (fib, row, 1 - slab))

    def exchange_factors():
        fetch(1).wait()
        fetch(2).wait()
        two_own_block[...] = jnp.concatenate([two[...], two[...]], axis=1)
        across = three[...].T
        nothing = jnp.zeros_like(across)
        mine = jnp.where(slab == 0, 1.0, 0.0)
        block = jnp.concatenate([across * mine, across * (1.0 - mine)], axis=1)
        three_own_block[...] = jnp.concatenate([block] * 4, axis=1)
        for step in range(1, 4):
            two_copy(step).start()
        three_copy().start()
        two_all[row] = two_own_block[...]
        three_all[slab] = three_own_block[...]

    def widen():
        two_arrived().wait_recv()
        three_copy().wait_recv()
        high, low = split(three_all[0] + three_all[1])
        lanes = lax.broadcasted_iota(jnp.int32, (64, 256), 1)
        three_stack[...] = jnp.where(lanes < 128, high.astype(F32), low.astype(F32)).astype(BF16)
        left = left_half((32, 128))
        nothing = jnp.zeros((32, 128), F32)
        for z in range(4):
            block = two_all[z]
            sides = (jnp.where(left, block, 0.0), jnp.where(left, 0.0, block))
            pieces = []
            for i in range(4):
                tiles = [nothing, nothing]
                tiles[i // 2] = sides[i % 2]
                pieces.append(jnp.concatenate(tiles, axis=1))
            high, low = split(jnp.concatenate(pieces, axis=0))
            wide_high[z] = high
            wide_low[z] = low
        fetch(3).wait()
        natural = lax.broadcasted_iota(jnp.int32, (512, 512), 1)
        there = ((natural >> 2) & 7) * 64 + (natural >> 5) * 4 + (natural & 3)
        same = there == lax.broadcasted_iota(jnp.int32, (512, 512), 0)
        order[...] = jnp.where(same, 1.0, 0.0).astype(BF16)
        one_stack[...] = dot_nt(halves(one[...]), order[...]).astype(BF16)

    def modes_three_two(chunk, half):
        def rank(r):
            parts = []
            for z in range(4):
                pieces = [incoming[chunk, half, pl.ds((2 * z + c) * 128 + r * 32, 32), :] for c in range(2)]
                high, low = split(jnp.concatenate(pieces, axis=0))
                parts.append(jnp.concatenate([high, low, high, low], axis=0))
            out = dot(three_stack[...], jnp.concatenate(parts, axis=1))
            for z in range(4):
                halfway[z, pl.ds(r, 64, stride=4), :] = out[:, z * 128 : (z + 1) * 128]

        each(0, 4, rank, unroll=2)

        def rows(block):
            at = pl.ds(pl.multiple_of(block * 128, 128), 128)
            total = jnp.zeros((128, 256), F32)
            for z in range(4):
                high, low = split(halfway[z, at, :])
                both = dot(jnp.concatenate([high, low], axis=0), wide_high[z])
                total = total + both[:128] + both[128:] + dot(high, wide_low[z])
            left = left_half((8, 128))
            for f in range(8):
                for t in range(2):
                    lower = total[f * 16 : f * 16 + 8, t * 128 : t * 128 + 128]
                    upper = total[f * 16 + 8 : f * 16 + 16, t * 128 : t * 128 + 128]
                    contracted[chunk, half, block * 8 + f, 2 * t] = jnp.where(left, lower, pltpu.roll(upper, 64, 1))
                    contracted[chunk, half, block * 8 + f, 2 * t + 1] = jnp.where(left, pltpu.roll(lower, 64, 1), upper)

        each(0, 2, rows)

    def advance(turn):
        @pl.when(turn < CHUNKS)
        def _():
            @pl.when(turn >= 2)
            def _():
                sent_chunk(turn - 2)

            send_chunk(turn)

        @pl.when(turn == 0)
        def _():
            exchange_factors()

        @pl.when(turn + 1 < CHUNKS)
        def _():
            load(turn + 1).wait()

            @pl.when(turn + 3 < CHUNKS)
            def _():
                load(turn + 3).start()

            mode_four(turn + 1)

        @pl.when(turn == 0)
        def _():
            widen()

        @pl.when(turn >= LAG)
        def _():
            chunk = turn - LAG

            def one_half(half):
                z_own(chunk, half).wait()
                z_all(chunk, half).wait_recv()
                modes_three_two(chunk, half)
                for d in FIBERS:
                    f_copy(chunk, half, d).start()
                f_own(chunk, half).start()

            each(0, 2, one_half)

    each(0, CHUNKS + LAG, advance)
    each(CHUNKS - 2, CHUNKS, sent_chunk)
    partial[...] = jnp.zeros_like(partial)
    each(0, EARLY, lambda chunk: each(0, 2, lambda half: f_own(chunk, half).wait()))
    f_all(0).wait_recv()
    fiber_rows = fibers.reshape(8192, 128)

    def cross(step, first, count):
        block = [fiber_rows[pl.ds(first * 16 + 2 * step + n, count, stride=16), :] for n in range(2)]
        high, low = split(jnp.concatenate(block, axis=1))
        fibers_high[step, pl.ds(first, count), :] = high
        fibers_low[step, pl.ds(first, count), :] = low
        both = dot(one_stack[:, first : first + count], high)
        return both[:64] + both[64:] + dot(one_stack[:64, first : first + count], low)

    def cross_early(step):
        crossed[step] = cross(step, 0, EARLY * 64)

    each(0, 8, cross_early, unroll=2)
    each(EARLY, CHUNKS, lambda chunk: each(0, 2, lambda half: f_own(chunk, half).wait()))
    f_all(1).wait_recv()

    def cross_late(step):
        parts = halves(crossed[step] + cross(step, EARLY * 64, (CHUNKS - EARLY) * 64))
        back = dot_nt(parts, fibers_high[step])
        partial[...] += back[:64] + back[64:] + dot_nt(parts[:64], fibers_low[step])

    each(0, 8, cross_late, unroll=2)

    def rs_copy(d):
        device, peer = plane_peer(d)
        return remote(partial.at[pl.ds(peer * 8, 8), :], scattered.at[me], rs_send, rs_recv, device)

    def ar_copy(d):
        return remote(shared.at[fib], shared.at[fib], ar_send, ar_recv, fib_peer(d)[0])

    def ag_copy(d):
        mine = state.at[pl.ds(me * 8, 8), pl.ds(0, 512)]
        return remote(mine, mine, ag_send, ag_recv, plane_peer(d)[0])

    def rs_all():
        block = scattered.at[pl.ds(0, 7)]
        return remote(block, block, rs_send, rs_recv, plane_peer(1)[0])

    def ar_all():
        block = shared.at[pl.ds(0, 15)]
        return remote(block, block, ar_send, ar_recv, fib_peer(1)[0])

    def ag_all():
        block = state.at[pl.ds(0, 56), pl.ds(0, 512)]
        return remote(block, block, ag_send, ag_recv, plane_peer(1)[0])

    for d in PLANE:
        rs_copy(d).start()
    scattered[me] = partial[pl.ds(pl.multiple_of(me * 8, 8), 8), :]
    rs_all().wait_recv()
    shared[fib] = jnp.sum(scattered[...], axis=0)
    for d in FIBERS:
        ar_copy(d).start()
    ar_all().wait_recv()
    state[pl.ds(pl.multiple_of(me * 8, 8), 8), pl.ds(0, 512)] = jnp.sum(shared[...], axis=0)
    for d in PLANE:
        ag_copy(d).start()
    ag_all().wait_recv()

    one_stack[...] = halves(state[:, :512])

    def project(n):
        p_low, middle = n // 4, n % 4
        step = (middle // 2) * 4 + p_low * 2 + middle % 2
        both = dot(one_stack[...], fibers_high[step])
        out = both[:64] + both[64:] + dot(one_stack[:64, :], fibers_low[step])
        across = jnp.concatenate([out[:, :128], out[:, 128:]], axis=0).T
        for high in range(2):
            for peer in range(8):
                start = high * 64 + peer * 8
                at = pl.ds(pl.multiple_of(middle * 16 + high * 8, 8), 8)
                core_out[peer, p_low, at, :] = across[start : start + 8, :]

    def core_copy(p_low, d):
        device, peer = plane_peer(d)
        return remote(core_out.at[peer, p_low], core_in.at[p_low, me], core_send.at[p_low], core_recv.at[p_low], device)

    def core_all(p_low):
        block = core_in.at[p_low, pl.ds(0, 7)]
        return remote(block, block, core_send.at[p_low], core_recv.at[p_low], plane_peer(1)[0])

    def project_some(p_low):
        each(p_low * 4, p_low * 4 + 4, project, unroll=2)
        for d in PLANE:
            core_copy(p_low, d).start()
        core_in[p_low, me] = core_out[me, p_low]

    for p_low in range(2):
        project_some(p_low)
    ag_all().wait_send()
    lanes = lax.broadcasted_iota(jnp.int32, (64, 128), 1)
    state[:, 512:] = jnp.where(lanes == lax.broadcasted_iota(jnp.int32, (64, 128), 0), 1.0, 0.0)

    def cholesky_qr(repeat):
        rows = state[:, :512]
        crossed = lax.dot_general(rows, rows, (((1,), (1,)), ((), ())), precision=HIGHEST, preferred_element_type=F32)
        state[...] = jnp.dot(eliminate(crossed), state[...], precision=HIGHEST, preferred_element_type=F32)

    each(0, 2, cholesky_qr)
    rows = state[:, :512]
    high = rows.astype(BF16)
    rest = rows - high.astype(F32)
    middle, low = split(rest)
    moved = dot(jnp.concatenate([high, middle, low], axis=0), order[...])
    updated[...] = moved[:64] + (moved[64:128] + moved[128:])
    inverse[...] = state[:, 512:]
    for p_low in range(2):
        core_all(p_low).wait_recv()
    out_copy = pltpu.make_async_copy(core_in, received, out_sem)
    out_copy.start()

    core_all(0).wait_send()
    core_all(1).wait_send()
    rs_all().wait_send()
    ar_all().wait_send()
    two_arrived().wait_send()
    three_copy().wait_send()
    f_all(0).wait_send()
    f_all(1).wait_send()
    out_copy.wait()


def finish_kernel(received, inverse, rows, updated, core, high, low):
    step = pl.program_id(0)

    @pl.when(step == 0)
    def _():
        updated[...] = rows[...]
        flat = received.reshape(1024, 128)
        for n in range(32):
            p, q = n // 8, n % 8
            part = flat[pl.ds((p % 2) * 512 + (p // 2) * 8 + q, 32, stride=16), :]
            high[pl.ds(n * 32, 32), :], low[pl.ds(n * 32, 32), :] = split(part)

    own = inverse[pl.ds(pl.multiple_of(step * 16, 16), 16), :]
    weights = halves(jnp.concatenate([own, pltpu.roll(own, 64, 1)], axis=0))
    both = dot_nt(weights, high[...])
    out = both[:32] + both[32:] + dot_nt(weights[:32], low[...])
    lanes = lax.broadcasted_iota(jnp.int32, (16, 128), 1)
    for n in range(32):
        p, q = n // 8, n % 8
        tile, off = n // 4, (n % 4) * 32
        lower = out[:16, tile * 128 : tile * 128 + 128]
        upper = out[16:, tile * 128 : tile * 128 + 128]
        if off:
            lower = pltpu.roll(lower, 128 - off, 1)
        if off != 32:
            upper = pltpu.roll(upper, (160 - off) % 128, 1)
        core[pl.ds(q * 4 + p, 16, stride=32), :] = jnp.where(lanes < 32, lower, upper)


def body(tensor, factor_one, factor_two, factor_three, factor_four):
    vmem = pl.BlockSpec(memory_space=pltpu.VMEM)
    hbm = pl.BlockSpec(memory_space=pl.ANY)
    dma = pltpu.SemaphoreType.DMA
    rows, inverse, received = pl.pallas_call(
        kernel,
        out_shape=(
            jax.ShapeDtypeStruct((64, 512), F32),
            jax.ShapeDtypeStruct((64, 128), F32),
            jax.ShapeDtypeStruct((2, 8, 64, 128), F32),
        ),
        in_specs=[hbm] * 5,
        out_specs=(vmem, vmem, hbm),
        scratch_shapes=[
            pltpu.VMEM((64, 128), F32),
            pltpu.VMEM((32, 64), F32),
            pltpu.VMEM((32, 64), F32),
            pltpu.VMEM((64, 512), F32),
            pltpu.VMEM((64, 128), F32),
            pltpu.VMEM((128, 256), BF16),
            pltpu.VMEM((128, 512), BF16),
            pltpu.VMEM((64, 256), F32),
            pltpu.VMEM((32, 128), F32),
            pltpu.VMEM((3, 4096, 128), F32),
            pltpu.VMEM((CHUNKS, 2048, 128), F32),
            pltpu.VMEM((CHUNKS, 2, 1024, 128), F32),
            pltpu.VMEM((4, 256, 128), F32),
            pltpu.VMEM((CHUNKS, 2, 16, 4, 8, 128), F32),
            pltpu.VMEM((CHUNKS, 16, 4, 2, 8, 128), F32),
            pltpu.VMEM((4, 32, 128), F32),
            pltpu.VMEM((2, 64, 256), F32),
            pltpu.VMEM((64, 256), BF16),
            pltpu.VMEM((4, 128, 256), BF16),
            pltpu.VMEM((4, 128, 256), BF16),
            pltpu.VMEM((8, 512, 256), BF16),
            pltpu.VMEM((8, 512, 256), BF16),
            pltpu.VMEM((512, 512), BF16),
            pltpu.VMEM((8, 64, 256), F32),
            pltpu.VMEM((64, 512), F32),
            pltpu.VMEM((8, 8, 512), F32),
            pltpu.VMEM((16, 8, 512), F32),
            pltpu.VMEM((64, 640), F32),
            pltpu.VMEM((8, 2, 64, 128), F32),
            pltpu.VMEM((2, 8, 64, 128), F32),
            dma((3,)), dma((4,)), dma((CHUNKS, 2)), dma((CHUNKS, 2)), dma((CHUNKS, 2)), dma((CHUNKS, 2)), dma((2,)), dma((2,)),
            dma(()), dma(()), dma(()), dma(()), dma(()), dma(()), dma(()), dma(()), dma(()), dma(()), dma((2,)), dma((2,)), dma(()),
        ],
        compiler_params=pltpu.CompilerParams(collective_id=0, has_side_effects=True, vmem_limit_bytes=56 * 2**20),
        name="hooi",
    )(tensor.reshape(8, 4096, 128), factor_four.T, factor_three, factor_two, factor_one.T)
    whole = lambda *shape: pl.BlockSpec(shape, lambda step: (0,) * len(shape))
    updated, core = pl.pallas_call(
        finish_kernel,
        grid=(4,),
        out_shape=(jax.ShapeDtypeStruct((64, 512), F32), jax.ShapeDtypeStruct((2048, 128), F32)),
        in_specs=[whole(2, 8, 64, 128), whole(64, 128), whole(64, 512)],
        out_specs=(whole(64, 512), pl.BlockSpec((512, 128), lambda step: (step, 0))),
        scratch_shapes=[pltpu.VMEM((1024, 128), BF16), pltpu.VMEM((1024, 128), BF16)],
        compiler_params=pltpu.CompilerParams(vmem_limit_bytes=62 * 2**20),
        name="finish",
    )(received, inverse, rows)
    return (updated.T, core[:, :64].reshape(64, 8, 4, 64))


def solution(mesh):
    in_specs = (P("fib", "row", "slab", None), P(), P("row", None), P("slab", None), P())
    out_specs = (P(), P(None, ("row", "slab"), "fib", None))
    return jax.shard_map(body, mesh=mesh, in_specs=in_specs, out_specs=out_specs, check_vma=False)
```

```python
import jax
import jax.numpy as jnp
from jax import lax
from jax.experimental import pallas as pl
from jax.experimental.pallas import tpu as pltpu
from jax.sharding import PartitionSpec as P

HIGHEST = lax.Precision.HIGHEST
MESH = pl.DeviceIdType.MESH
F32 = jnp.float32
BF16 = jnp.bfloat16
CHUNKS = 8
LAG = 2
EARLY = CHUNKS - 1
PLANE = tuple(range(1, 8))
FIBERS = tuple(sorted(range(1, 16), key=lambda d: -(min(d // 4, 4 - d // 4) + min(d % 4, 4 - d % 4))))


def split(x):
    high = x.astype(BF16)
    return high, (x - high.astype(F32)).astype(BF16)


def dot(a, b):
    return jnp.dot(a, b, preferred_element_type=F32)


def dot_nt(a, b):
    return lax.dot_general(a, b, (((1,), (1,)), ((), ())), preferred_element_type=F32)


def place():
    return lax.axis_index("fib"), lax.axis_index("row"), lax.axis_index("slab")


def plane_peer(d):
    fib, row, slab = place()
    row, slab = lax.rem(row + d // 2, 4), lax.rem(slab + d % 2, 2)
    return (fib, row, slab), row * 2 + slab


def fib_peer(d):
    fib, row, slab = place()
    fib = lax.rem(fib // 4 + d // 4, 4) * 4 + lax.rem(fib % 4 + d % 4, 4)
    return (fib, row, slab), fib


def each(lower, upper, step, unroll=1):
    def run(index, carry):
        step(index)
        return carry

    lax.fori_loop(lower, upper, run, 0, unroll=unroll)


def remote(src, dst, send, recv, device):
    return pltpu.make_async_remote_copy(
        src_ref=src, dst_ref=dst, send_sem=send, recv_sem=recv, device_id=device, device_id_type=MESH
    )


def greet():
    barrier = pltpu.get_barrier_semaphore()
    for d in PLANE:
        pl.semaphore_signal(barrier, inc=1, device_id=plane_peer(d)[0], device_id_type=MESH)
    for d in FIBERS:
        pl.semaphore_signal(barrier, inc=1, device_id=fib_peer(d)[0], device_id_type=MESH)


def stack(x):
    high, low = split(x)
    return jnp.concatenate([jnp.concatenate([high, high], 1), jnp.concatenate([low, low], 1)], 0)


def left_half(shape):
    return lax.broadcasted_iota(jnp.int32, shape, 1) < 64


def halves(x):
    return jnp.concatenate(split(x), axis=0)


def eliminate(crossed, group=8):
    lane = lax.broadcasted_iota(jnp.int32, (8, 64), 1)
    row = lax.broadcasted_iota(jnp.int32, (8, 64), 0)
    below = lax.broadcasted_iota(jnp.int32, (8, 128), 0)
    blocks = [
        jnp.concatenate([crossed[8 * b : 8 * b + 8], jnp.where(lane == row + 8 * b, 1.0, 0.0)], axis=1) for b in range(8)
    ]

    def spread(x):
        return jnp.broadcast_to(x, (8, 128))

    for first in range(0, 64, group):
        b, k = first // 8, first % 8
        here = blocks[b]
        corner = [[spread(here[k + m : k + m + 1, first + n : first + n + 1]) for n in range(m + 1)] for m in range(group)]
        below_diagonal = [[None] * group for m in range(group)]
        scale = [None] * group
        for m in range(group):
            square = corner[m][m]
            for n in range(m):
                square = square - below_diagonal[m][n] * below_diagonal[m][n]
            scale[m] = lax.rsqrt(square)
            for other in range(m + 1, group):
                entry = corner[other][m]
                for n in range(m):
                    entry = entry - below_diagonal[other][n] * below_diagonal[m][n]
                below_diagonal[other][m] = entry * scale[m]

        def forward(parts):
            done = []
            for m in range(group):
                part = parts[m]
                for n in range(m):
                    part = part - done[n] * below_diagonal[m][n]
                done.append(part * scale[m])
            return done

        pivots = forward([spread(here[k + m : k + m + 1, :]) for m in range(group)])
        for at in range(b, 8):
            if at == b and k + group == 8:
                update = here
            else:
                columns = forward([spread(blocks[at][:, first + m : first + m + 1]) for m in range(group)])
                update = blocks[at]
                for m in range(group):
                    update = update - columns[m] * pivots[m]
            if at == b:
                update = jnp.where(below < k, here, update)
                for m in range(group):
                    update = jnp.where(below == k + m, pivots[m], update)
            blocks[at] = update
    return jnp.concatenate(blocks, axis=0)[:, 64:]


def kernel(
    tensor, four_hbm, three_hbm, two_hbm, one_hbm, updated, inverse, received,
    four, three, two, one, dealt, four_stack, one_stack, three_own_block, two_own_block,
    staged, outgoing, incoming, halfway, contracted, fibers, two_all, three_all, three_stack, wide_high, wide_low,
    fibers_high, fibers_low, order, crossed, partial, scattered, shared, state, core_out, core_in,
    load_sem, factor_sem, own_sem, z_send, z_recv, fib_own_sem, f_send, f_recv,
    two_send, two_recv, three_send, three_recv, rs_send, rs_recv, ar_send, ar_recv, ag_send, ag_recv, core_send, core_recv, out_sem,
):
    fib, row, slab = place()
    me = row * 2 + slab

    def load(chunk):
        return pltpu.make_async_copy(tensor.at[chunk], staged.at[chunk % 3], load_sem.at[chunk % 3])

    def mode_four(chunk):
        slot = chunk % 3

        def two_steps(pair):
            first = staged[slot, pl.ds(2 * pair, 128, stride=32), :]
            second = staged[slot, pl.ds(2 * pair + 1, 128, stride=32), :]
            high, low = split(jnp.concatenate([first, second], axis=0))
            out = dot_nt(four_stack[...], jnp.concatenate([high, low], axis=1))
            out = out[:64] + out[64:]
            outgoing[chunk, pl.ds(2 * pair, 64, stride=32), :] = out[:, :128]
            outgoing[chunk, pl.ds(2 * pair + 1, 64, stride=32), :] = out[:, 128:]

        each(0, 16, two_steps, unroll=2)

    def fetch(n):
        source, target = ((four_hbm, four), (three_hbm, three), (two_hbm, two), (one_hbm, one))[n]
        return pltpu.make_async_copy(source, target, factor_sem.at[n])

    fetch(0).start()
    load(0).start()
    load(1).start()
    for n in range(1, 4):
        fetch(n).start()
    greet()
    fetch(0).wait()
    across = four[...]
    dealt[pl.ds(0, 32, stride=2), :] = across[:32]
    dealt[pl.ds(1, 32, stride=2), :] = across[32:]
    four_stack[...] = stack(dealt[...])
    load(0).wait()
    load(2).start()
    mode_four(0)
    pl.semaphore_wait(pltpu.get_barrier_semaphore(), len(PLANE) + len(FIBERS))

    def z_copy(chunk, half, d):
        device, peer = plane_peer(d)
        return remote(
            outgoing.at[chunk, pl.ds(peer * 256 + half * 128, 128), :],
            incoming.at[chunk, half, pl.ds(me * 128, 128), :],
            z_send.at[chunk, half], z_recv.at[chunk, half], device,
        )

    def z_all(chunk, half):
        block = incoming.at[chunk, half, pl.ds(0, 7 * 128), :]
        return remote(block, block, z_send.at[chunk, half], z_recv.at[chunk, half], plane_peer(1)[0])

    def z_own(chunk, half):
        return pltpu.make_async_copy(
            outgoing.at[chunk, pl.ds(me * 256 + half * 128, 128), :],
            incoming.at[chunk, half, pl.ds(me * 128, 128), :],
            own_sem.at[chunk, half],
        )

    def send_chunk(chunk):
        for half in range(2):
            for d in PLANE:
                z_copy(chunk, half, d).start()
            z_own(chunk, half).start()

    def sent_chunk(chunk):
        for half in range(2):
            z_all(chunk, half).wait_send()

    def f_rows(chunk, half, device):
        return fibers.at[chunk, device, :, half]

    def f_copy(chunk, half, d):
        device, peer = fib_peer(d)
        stage = (chunk // EARLY) * (1 + half)
        return remote(contracted.at[chunk, half, peer], f_rows(chunk, half, fib), f_send.at[stage], f_recv.at[stage], device)

    def f_all(stage):
        block = fibers.at[pl.ds(0, EARLY), pl.ds(0, 15)] if stage == 0 else fibers.at[EARLY, pl.ds(0, 15), :, stage - 1]
        return remote(block, block, f_send.at[stage], f_recv.at[stage], fib_peer(1)[0])

    def f_own(chunk, half):
        return pltpu.make_async_copy(contracted.at[chunk, half, fib], f_rows(chunk, half, fib), fib_own_sem.at[chunk, half])

    def two_copy(step):
        return remote(two_own_block, two_all.at[row], two_send, two_recv, (fib, lax.rem(row + step, 4), slab))

    def two_arrived():
        block = two_all.at[pl.ds(0, 3)]
        return remote(block, block, two_send, two_recv, (fib, lax.rem(row + 1, 4), slab))

    def three_copy():
        return remote(three_own_block, three_all.at[slab], three_send, three_recv, (fib, row, 1 - slab))

    def exchange_factors():
        fetch(1).wait()
        fetch(2).wait()
        two_own_block[...] = jnp.concatenate([two[...], two[...]], axis=1)
        across = three[...].T
        nothing = jnp.zeros_like(across)
        mine = jnp.where(slab == 0, 1.0, 0.0)
        block = jnp.concatenate([across * mine, across * (1.0 - mine)], axis=1)
        three_own_block[...] = jnp.concatenate([block] * 4, axis=1)
        for step in range(1, 4):
            two_copy(step).start()
        three_copy().start()
        two_all[row] = two_own_block[...]
        three_all[slab] = three_own_block[...]

    def widen():
        two_arrived().wait_recv()
        three_copy().wait_recv()
        high, low = split(three_all[0] + three_all[1])
        lanes = lax.broadcasted_iota(jnp.int32, (64, 256), 1)
        three_stack[...] = jnp.where(lanes < 128, high.astype(F32), low.astype(F32)).astype(BF16)
        left = left_half((32, 128))
        nothing = jnp.zeros((32, 128), F32)
        for z in range(4):
            block = two_all[z]
            sides = (jnp.where(left, block, 0.0), jnp.where(left, 0.0, block))
            pieces = []
            for i in range(4):
                tiles = [nothing, nothing]
                tiles[i // 2] = sides[i % 2]
                pieces.append(jnp.concatenate(tiles, axis=1))
            high, low = split(jnp.concatenate(pieces, axis=0))
            wide_high[z] = high
            wide_low[z] = low
        fetch(3).wait()
        natural = lax.broadcasted_iota(jnp.int32, (512, 512), 1)
        there = ((natural >> 2) & 7) * 64 + (natural >> 5) * 4 + (natural & 3)
        same = there == lax.broadcasted_iota(jnp.int32, (512, 512), 0)
        order[...] = jnp.where(same, 1.0, 0.0).astype(BF16)
        one_stack[...] = dot_nt(halves(one[...]), order[...]).astype(BF16)

    def modes_three_two(chunk, half):
        def rank(r):
            parts = []
            for z in range(4):
                pieces = [incoming[chunk, half, pl.ds((2 * z + c) * 128 + r * 32, 32), :] for c in range(2)]
                high, low = split(jnp.concatenate(pieces, axis=0))
                parts.append(jnp.concatenate([high, low, high, low], axis=0))
            out = dot(three_stack[...], jnp.concatenate(parts, axis=1))
            for z in range(4):
                halfway[z, pl.ds(r, 64, stride=4), :] = out[:, z * 128 : (z + 1) * 128]

        each(0, 4, rank, unroll=4)

        def rows(block):
            at = pl.ds(pl.multiple_of(block * 128, 128), 128)
            total = jnp.zeros((128, 256), F32)
            for z in range(4):
                high, low = split(halfway[z, at, :])
                both = dot(jnp.concatenate([high, low], axis=0), wide_high[z])
                total = total + both[:128] + both[128:] + dot(high, wide_low[z])
            left = left_half((8, 128))
            for f in range(8):
                for t in range(2):
                    lower = total[f * 16 : f * 16 + 8, t * 128 : t * 128 + 128]
                    upper = total[f * 16 + 8 : f * 16 + 16, t * 128 : t * 128 + 128]
                    contracted[chunk, half, block * 8 + f, 2 * t] = jnp.where(left, lower, pltpu.roll(upper, 64, 1))
                    contracted[chunk, half, block * 8 + f, 2 * t + 1] = jnp.where(left, pltpu.roll(lower, 64, 1), upper)

        each(0, 2, rows, unroll=2)

    def advance(turn):
        @pl.when(turn < CHUNKS)
        def _():
            @pl.when(turn >= 2)
            def _():
                sent_chunk(turn - 2)

            send_chunk(turn)

        @pl.when(turn == 0)
        def _():
            exchange_factors()

        @pl.when(turn + 1 < CHUNKS)
        def _():
            load(turn + 1).wait()

            @pl.when(turn + 3 < CHUNKS)
            def _():
                load(turn + 3).start()

            mode_four(turn + 1)

        @pl.when(turn == 0)
        def _():
            widen()

        @pl.when(turn >= LAG)
        def _():
            chunk = turn - LAG

            def one_half(half):
                z_own(chunk, half).wait()
                z_all(chunk, half).wait_recv()
                modes_three_two(chunk, half)
                for d in FIBERS:
                    f_copy(chunk, half, d).start()
                f_own(chunk, half).start()

            each(0, 2, one_half)

    each(0, CHUNKS + LAG, advance)
    each(CHUNKS - 2, CHUNKS, sent_chunk)
    partial[...] = jnp.zeros_like(partial)
    each(0, EARLY, lambda chunk: each(0, 2, lambda half: f_own(chunk, half).wait()))
    f_all(0).wait_recv()
    fiber_rows = fibers.reshape(8192, 128)

    def cross(step, first, count):
        block = [fiber_rows[pl.ds(first * 16 + 2 * step + n, count, stride=16), :] for n in range(2)]
        high, low = split(jnp.concatenate(block, axis=1))
        fibers_high[step, pl.ds(first, count), :] = high
        fibers_low[step, pl.ds(first, count), :] = low
        both = dot(one_stack[:, first : first + count], high)
        return both[:64] + both[64:] + dot(one_stack[:64, first : first + count], low)

    def cross_early(step):
        crossed[step] = cross(step, 0, EARLY * 64)

    each(0, 8, cross_early, unroll=2)

    def cross_late(step):
        parts = halves(crossed[step] + cross(step, EARLY * 64, (CHUNKS - EARLY) * 64))
        back = dot_nt(parts, fibers_high[step])
        partial[...] += back[:64] + back[64:] + dot_nt(parts[:64], fibers_low[step])

    for half in range(2):
        f_own(EARLY, half).wait()
        f_all(1 + half).wait_recv()
        each(half * 4, half * 4 + 4, cross_late, unroll=4)

    def rs_copy(d):
        device, peer = plane_peer(d)
        return remote(partial.at[pl.ds(peer * 8, 8), :], scattered.at[me], rs_send, rs_recv, device)

    def ar_copy(d):
        return remote(shared.at[fib], shared.at[fib], ar_send, ar_recv, fib_peer(d)[0])

    def ag_copy(d):
        mine = state.at[pl.ds(me * 8, 8), pl.ds(0, 512)]
        return remote(mine, mine, ag_send, ag_recv, plane_peer(d)[0])

    def rs_all():
        block = scattered.at[pl.ds(0, 7)]
        return remote(block, block, rs_send, rs_recv, plane_peer(1)[0])

    def ar_all():
        block = shared.at[pl.ds(0, 15)]
        return remote(block, block, ar_send, ar_recv, fib_peer(1)[0])

    def ag_all():
        block = state.at[pl.ds(0, 56), pl.ds(0, 512)]
        return remote(block, block, ag_send, ag_recv, plane_peer(1)[0])

    for d in PLANE:
        rs_copy(d).start()
    scattered[me] = partial[pl.ds(pl.multiple_of(me * 8, 8), 8), :]
    rs_all().wait_recv()
    shared[fib] = jnp.sum(scattered[...], axis=0)
    for d in FIBERS:
        ar_copy(d).start()
    ar_all().wait_recv()
    state[pl.ds(pl.multiple_of(me * 8, 8), 8), pl.ds(0, 512)] = jnp.sum(shared[...], axis=0)
    for d in PLANE:
        ag_copy(d).start()
    ag_all().wait_recv()

    one_stack[...] = halves(state[:, :512])

    def project(n):
        p_low, middle = n // 4, n % 4
        step = (middle // 2) * 4 + p_low * 2 + middle % 2
        both = dot(one_stack[...], fibers_high[step])
        out = both[:64] + both[64:] + dot(one_stack[:64, :], fibers_low[step])
        across = jnp.concatenate([out[:, :128], out[:, 128:]], axis=0).T
        for high in range(2):
            for peer in range(8):
                start = high * 64 + peer * 8
                at = pl.ds(pl.multiple_of(middle * 16 + high * 8, 8), 8)
                core_out[peer, p_low, at, :] = across[start : start + 8, :]

    def core_copy(p_low, d):
        device, peer = plane_peer(d)
        return remote(core_out.at[peer, p_low], core_in.at[p_low, me], core_send.at[p_low], core_recv.at[p_low], device)

    def core_all(p_low):
        block = core_in.at[p_low, pl.ds(0, 7)]
        return remote(block, block, core_send.at[p_low], core_recv.at[p_low], plane_peer(1)[0])

    def project_some(p_low):
        each(p_low * 4, p_low * 4 + 4, project, unroll=4)
        for d in PLANE:
            core_copy(p_low, d).start()
        core_in[p_low, me] = core_out[me, p_low]

    for p_low in range(2):
        project_some(p_low)
    ag_all().wait_send()
    lanes = lax.broadcasted_iota(jnp.int32, (64, 128), 1)
    state[:, 512:] = jnp.where(lanes == lax.broadcasted_iota(jnp.int32, (64, 128), 0), 1.0, 0.0)

    def cholesky_qr(repeat):
        rows = state[:, :512]
        crossed = lax.dot_general(rows, rows, (((1,), (1,)), ((), ())), precision=HIGHEST, preferred_element_type=F32)
        state[...] = jnp.dot(eliminate(crossed), state[...], precision=HIGHEST, preferred_element_type=F32)

    each(0, 2, cholesky_qr)
    rows = state[:, :512]
    high = rows.astype(BF16)
    rest = rows - high.astype(F32)
    middle, low = split(rest)
    moved = dot(jnp.concatenate([high, middle, low], axis=0), order[...])
    updated[...] = moved[:64] + (moved[64:128] + moved[128:])
    inverse[...] = state[:, 512:]
    for p_low in range(2):
        core_all(p_low).wait_recv()
    out_copy = pltpu.make_async_copy(core_in, received, out_sem)
    out_copy.start()

    core_all(0).wait_send()
    core_all(1).wait_send()
    rs_all().wait_send()
    ar_all().wait_send()
    two_arrived().wait_send()
    three_copy().wait_send()
    f_all(0).wait_send()
    f_all(1).wait_send()
    f_all(2).wait_send()
    out_copy.wait()


def finish_kernel(received, inverse, rows, updated, core, high, low):
    step = pl.program_id(0)

    @pl.when(step == 0)
    def _():
        updated[...] = rows[...]
        flat = received.reshape(1024, 128)
        for n in range(32):
            p, q = n // 8, n % 8
            part = flat[pl.ds((p % 2) * 512 + (p // 2) * 8 + q, 32, stride=16), :]
            high[pl.ds(n * 32, 32), :], low[pl.ds(n * 32, 32), :] = split(part)

    own = inverse[pl.ds(pl.multiple_of(step * 32, 32), 32), :]
    weights = halves(jnp.concatenate([own, pltpu.roll(own, 64, 1)], axis=0))
    both = dot_nt(weights, high[...])
    out = both[:64] + both[64:] + dot_nt(weights[:64], low[...])
    lanes = lax.broadcasted_iota(jnp.int32, (32, 128), 1)
    for n in range(32):
        p, q = n // 8, n % 8
        tile, off = n // 4, (n % 4) * 32
        lower = out[:32, tile * 128 : tile * 128 + 128]
        upper = out[32:, tile * 128 : tile * 128 + 128]
        if off:
            lower = pltpu.roll(lower, 128 - off, 1)
        if off != 32:
            upper = pltpu.roll(upper, (160 - off) % 128, 1)
        core[pl.ds(q * 4 + p, 32, stride=32), :] = jnp.where(lanes < 32, lower, upper)


def body(tensor, factor_one, factor_two, factor_three, factor_four):
    vmem = pl.BlockSpec(memory_space=pltpu.VMEM)
    hbm = pl.BlockSpec(memory_space=pl.ANY)
    dma = pltpu.SemaphoreType.DMA
    rows, inverse, received = pl.pallas_call(
        kernel,
        out_shape=(
            jax.ShapeDtypeStruct((64, 512), F32),
            jax.ShapeDtypeStruct((64, 128), F32),
            jax.ShapeDtypeStruct((2, 8, 64, 128), F32),
        ),
        in_specs=[hbm] * 5,
        out_specs=(vmem, vmem, hbm),
        scratch_shapes=[
            pltpu.VMEM((64, 128), F32),
            pltpu.VMEM((32, 64), F32),
            pltpu.VMEM((32, 64), F32),
            pltpu.VMEM((64, 512), F32),
            pltpu.VMEM((64, 128), F32),
            pltpu.VMEM((128, 256), BF16),
            pltpu.VMEM((128, 512), BF16),
            pltpu.VMEM((64, 256), F32),
            pltpu.VMEM((32, 128), F32),
            pltpu.VMEM((3, 4096, 128), F32),
            pltpu.VMEM((CHUNKS, 2048, 128), F32),
            pltpu.VMEM((CHUNKS, 2, 1024, 128), F32),
            pltpu.VMEM((4, 256, 128), F32),
            pltpu.VMEM((CHUNKS, 2, 16, 4, 8, 128), F32),
            pltpu.VMEM((CHUNKS, 16, 4, 2, 8, 128), F32),
            pltpu.VMEM((4, 32, 128), F32),
            pltpu.VMEM((2, 64, 256), F32),
            pltpu.VMEM((64, 256), BF16),
            pltpu.VMEM((4, 128, 256), BF16),
            pltpu.VMEM((4, 128, 256), BF16),
            pltpu.VMEM((8, 512, 256), BF16),
            pltpu.VMEM((8, 512, 256), BF16),
            pltpu.VMEM((512, 512), BF16),
            pltpu.VMEM((8, 64, 256), F32),
            pltpu.VMEM((64, 512), F32),
            pltpu.VMEM((8, 8, 512), F32),
            pltpu.VMEM((16, 8, 512), F32),
            pltpu.VMEM((64, 640), F32),
            pltpu.VMEM((8, 2, 64, 128), F32),
            pltpu.VMEM((2, 8, 64, 128), F32),
            dma((3,)), dma((4,)), dma((CHUNKS, 2)), dma((CHUNKS, 2)), dma((CHUNKS, 2)), dma((CHUNKS, 2)), dma((3,)), dma((3,)),
            dma(()), dma(()), dma(()), dma(()), dma(()), dma(()), dma(()), dma(()), dma(()), dma(()), dma((2,)), dma((2,)), dma(()),
        ],
        compiler_params=pltpu.CompilerParams(collective_id=0, has_side_effects=True, vmem_limit_bytes=56 * 2**20),
        name="hooi",
    )(tensor.reshape(8, 4096, 128), factor_four.T, factor_three, factor_two, factor_one.T)
    whole = lambda *shape: pl.BlockSpec(shape, lambda step: (0,) * len(shape))
    updated, core = pl.pallas_call(
        finish_kernel,
        grid=(2,),
        out_shape=(jax.ShapeDtypeStruct((64, 512), F32), jax.ShapeDtypeStruct((2048, 128), F32)),
        in_specs=[whole(2, 8, 64, 128), whole(64, 128), whole(64, 512)],
        out_specs=(whole(64, 512), pl.BlockSpec((1024, 128), lambda step: (step, 0))),
        scratch_shapes=[pltpu.VMEM((1024, 128), BF16), pltpu.VMEM((1024, 128), BF16)],
        compiler_params=pltpu.CompilerParams(vmem_limit_bytes=62 * 2**20),
        name="finish",
    )(received, inverse, rows)
    return (updated.T, core[:, :64].reshape(64, 8, 4, 64))


def solution(mesh):
    in_specs = (P("fib", "row", "slab", None), P(), P("row", None), P("slab", None), P())
    out_specs = (P(), P(None, ("row", "slab"), "fib", None))
    return jax.shard_map(body, mesh=mesh, in_specs=in_specs, out_specs=out_specs, check_vma=False)
```

```python
import jax
import jax.numpy as jnp
from jax import lax
from jax.experimental import pallas as pl
from jax.experimental.pallas import tpu as pltpu
from jax.sharding import PartitionSpec as P

HIGHEST = lax.Precision.HIGHEST
MESH = pl.DeviceIdType.MESH
F32 = jnp.float32
BF16 = jnp.bfloat16
CHUNKS = 8
LAG = 2
EARLY = CHUNKS - 1
PLANE = (4, 2, 6, 5, 3, 7, 1)
FIBERS = tuple(sorted(range(1, 16), key=lambda d: -(min(d // 4, 4 - d // 4) + min(d % 4, 4 - d % 4))))


def split(x):
    high = x.astype(BF16)
    return high, (x - high.astype(F32)).astype(BF16)


def dot(a, b):
    return jnp.dot(a, b, preferred_element_type=F32)


def dot_nt(a, b):
    return lax.dot_general(a, b, (((1,), (1,)), ((), ())), preferred_element_type=F32)


def place():
    return lax.axis_index("fib"), lax.axis_index("row"), lax.axis_index("slab")


def plane_peer(d):
    fib, row, slab = place()
    row, slab = lax.rem(row + d // 2, 4), lax.rem(slab + d % 2, 2)
    return (fib, row, slab), row * 2 + slab


def fib_peer(d):
    fib, row, slab = place()
    fib = lax.rem(fib // 4 + d // 4, 4) * 4 + lax.rem(fib % 4 + d % 4, 4)
    return (fib, row, slab), fib


def each(lower, upper, step, unroll=1):
    def run(index, carry):
        step(index)
        return carry

    lax.fori_loop(lower, upper, run, 0, unroll=unroll)


def remote(src, dst, send, recv, device):
    return pltpu.make_async_remote_copy(
        src_ref=src, dst_ref=dst, send_sem=send, recv_sem=recv, device_id=device, device_id_type=MESH
    )


def greet():
    barrier = pltpu.get_barrier_semaphore()
    for d in PLANE:
        pl.semaphore_signal(barrier, inc=1, device_id=plane_peer(d)[0], device_id_type=MESH)
    for d in FIBERS:
        pl.semaphore_signal(barrier, inc=1, device_id=fib_peer(d)[0], device_id_type=MESH)


def stack(x):
    high, low = split(x)
    return jnp.concatenate([jnp.concatenate([high, high], 1), jnp.concatenate([low, low], 1)], 0)


def left_half(shape):
    return lax.broadcasted_iota(jnp.int32, shape, 1) < 64


def halves(x):
    return jnp.concatenate(split(x), axis=0)


def eliminate(crossed, group=8):
    lane = lax.broadcasted_iota(jnp.int32, (8, 64), 1)
    row = lax.broadcasted_iota(jnp.int32, (8, 64), 0)
    below = lax.broadcasted_iota(jnp.int32, (8, 128), 0)
    blocks = [
        jnp.concatenate([crossed[8 * b : 8 * b + 8], jnp.where(lane == row + 8 * b, 1.0, 0.0)], axis=1) for b in range(8)
    ]

    def spread(x):
        return jnp.broadcast_to(x, (8, 128))

    for first in range(0, 64, group):
        b, k = first // 8, first % 8
        here = blocks[b]
        corner = [[spread(here[k + m : k + m + 1, first + n : first + n + 1]) for n in range(m + 1)] for m in range(group)]
        below_diagonal = [[None] * group for m in range(group)]
        scale = [None] * group
        for m in range(group):
            square = corner[m][m]
            for n in range(m):
                square = square - below_diagonal[m][n] * below_diagonal[m][n]
            scale[m] = lax.rsqrt(square)
            for other in range(m + 1, group):
                entry = corner[other][m]
                for n in range(m):
                    entry = entry - below_diagonal[other][n] * below_diagonal[m][n]
                below_diagonal[other][m] = entry * scale[m]

        def forward(parts):
            done = []
            for m in range(group):
                part = parts[m]
                for n in range(m):
                    part = part - done[n] * below_diagonal[m][n]
                done.append(part * scale[m])
            return done

        pivots = forward([spread(here[k + m : k + m + 1, :]) for m in range(group)])
        for at in range(b, 8):
            if at == b and k + group == 8:
                update = here
            else:
                columns = forward([spread(blocks[at][:, first + m : first + m + 1]) for m in range(group)])
                update = blocks[at]
                for m in range(group):
                    update = update - columns[m] * pivots[m]
            if at == b:
                update = jnp.where(below < k, here, update)
                for m in range(group):
                    update = jnp.where(below == k + m, pivots[m], update)
            blocks[at] = update
    return jnp.concatenate(blocks, axis=0)[:, 64:]


def kernel(
    tensor, four_hbm, three_hbm, two_hbm, one_hbm, updated, inverse, received,
    four, three, two, one, dealt, four_stack, one_stack, three_own_block, two_own_block,
    staged, outgoing, incoming, halfway, contracted, fibers, two_all, three_all, three_stack, wide_high, wide_low,
    fibers_high, fibers_low, order, crossed, partial, scattered, shared, state, core_out, core_in,
    load_sem, factor_sem, own_sem, z_send, z_recv, fib_own_sem, f_send, f_recv,
    two_send, two_recv, three_send, three_recv, rs_send, rs_recv, ar_send, ar_recv, ag_send, ag_recv, core_send, core_recv, out_sem,
):
    fib, row, slab = place()
    me = row * 2 + slab

    def load(chunk):
        return pltpu.make_async_copy(tensor.at[chunk], staged.at[chunk % 3], load_sem.at[chunk % 3])

    def mode_four(chunk):
        slot = chunk % 3

        def two_steps(pair):
            first = staged[slot, pl.ds(2 * pair, 128, stride=32), :]
            second = staged[slot, pl.ds(2 * pair + 1, 128, stride=32), :]
            high, low = split(jnp.concatenate([first, second], axis=0))
            out = dot_nt(four_stack[...], jnp.concatenate([high, low], axis=1))
            out = out[:64] + out[64:]
            outgoing[chunk, pl.ds(2 * pair, 64, stride=32), :] = out[:, :128]
            outgoing[chunk, pl.ds(2 * pair + 1, 64, stride=32), :] = out[:, 128:]

        each(0, 16, two_steps, unroll=2)

    def fetch(n):
        source, target = ((four_hbm, four), (three_hbm, three), (two_hbm, two), (one_hbm, one))[n]
        return pltpu.make_async_copy(source, target, factor_sem.at[n])

    fetch(0).start()
    load(0).start()
    load(1).start()
    for n in range(1, 4):
        fetch(n).start()
    greet()
    fetch(0).wait()
    across = four[...]
    dealt[pl.ds(0, 32, stride=2), :] = across[:32]
    dealt[pl.ds(1, 32, stride=2), :] = across[32:]
    four_stack[...] = stack(dealt[...])
    load(0).wait()
    load(2).start()
    mode_four(0)
    pl.semaphore_wait(pltpu.get_barrier_semaphore(), len(PLANE) + len(FIBERS))

    def z_copy(chunk, half, d):
        device, peer = plane_peer(d)
        return remote(
            outgoing.at[chunk, pl.ds(peer * 256 + half * 128, 128), :],
            incoming.at[chunk, half, pl.ds(me * 128, 128), :],
            z_send.at[chunk, half], z_recv.at[chunk, half], device,
        )

    def z_all(chunk, half):
        block = incoming.at[chunk, half, pl.ds(0, 7 * 128), :]
        return remote(block, block, z_send.at[chunk, half], z_recv.at[chunk, half], plane_peer(1)[0])

    def z_own(chunk, half):
        return pltpu.make_async_copy(
            outgoing.at[chunk, pl.ds(me * 256 + half * 128, 128), :],
            incoming.at[chunk, half, pl.ds(me * 128, 128), :],
            own_sem.at[chunk, half],
        )

    def send_chunk(chunk):
        for half in range(2):
            for d in PLANE:
                z_copy(chunk, half, d).start()
            z_own(chunk, half).start()

    def sent_chunk(chunk):
        for half in range(2):
            z_all(chunk, half).wait_send()

    def f_rows(chunk, half, device):
        return fibers.at[chunk, device, :, half]

    def f_copy(chunk, half, d):
        device, peer = fib_peer(d)
        stage = (chunk // EARLY) * (1 + half)
        return remote(contracted.at[chunk, half, peer], f_rows(chunk, half, fib), f_send.at[stage], f_recv.at[stage], device)

    def f_all(stage):
        block = fibers.at[pl.ds(0, EARLY), pl.ds(0, 15)] if stage == 0 else fibers.at[EARLY, pl.ds(0, 15), :, stage - 1]
        return remote(block, block, f_send.at[stage], f_recv.at[stage], fib_peer(1)[0])

    def f_own(chunk, half):
        return pltpu.make_async_copy(contracted.at[chunk, half, fib], f_rows(chunk, half, fib), fib_own_sem.at[chunk, half])

    def two_copy(step):
        return remote(two_own_block, two_all.at[row], two_send, two_recv, (fib, lax.rem(row + step, 4), slab))

    def two_arrived():
        block = two_all.at[pl.ds(0, 3)]
        return remote(block, block, two_send, two_recv, (fib, lax.rem(row + 1, 4), slab))

    def three_copy():
        return remote(three_own_block, three_all.at[slab], three_send, three_recv, (fib, row, 1 - slab))

    def exchange_factors():
        fetch(1).wait()
        fetch(2).wait()
        two_own_block[...] = jnp.concatenate([two[...], two[...]], axis=1)
        across = three[...].T
        nothing = jnp.zeros_like(across)
        mine = jnp.where(slab == 0, 1.0, 0.0)
        block = jnp.concatenate([across * mine, across * (1.0 - mine)], axis=1)
        three_own_block[...] = jnp.concatenate([block] * 4, axis=1)
        for step in range(1, 4):
            two_copy(step).start()
        three_copy().start()
        two_all[row] = two_own_block[...]
        three_all[slab] = three_own_block[...]

    def widen():
        two_arrived().wait_recv()
        three_copy().wait_recv()
        high, low = split(three_all[0] + three_all[1])
        lanes = lax.broadcasted_iota(jnp.int32, (64, 256), 1)
        three_stack[...] = jnp.where(lanes < 128, high.astype(F32), low.astype(F32)).astype(BF16)
        left = left_half((32, 128))
        nothing = jnp.zeros((32, 128), F32)
        for z in range(4):
            block = two_all[z]
            sides = (jnp.where(left, block, 0.0), jnp.where(left, 0.0, block))
            pieces = []
            for i in range(4):
                tiles = [nothing, nothing]
                tiles[i // 2] = sides[i % 2]
                pieces.append(jnp.concatenate(tiles, axis=1))
            high, low = split(jnp.concatenate(pieces, axis=0))
            wide_high[z] = high
            wide_low[z] = low
        fetch(3).wait()
        natural = lax.broadcasted_iota(jnp.int32, (512, 512), 1)
        there = ((natural >> 2) & 7) * 64 + (natural >> 5) * 4 + (natural & 3)
        same = there == lax.broadcasted_iota(jnp.int32, (512, 512), 0)
        order[...] = jnp.where(same, 1.0, 0.0).astype(BF16)
        one_stack[...] = dot_nt(halves(one[...]), order[...]).astype(BF16)

    def modes_three_two(chunk, half):
        def rank(r):
            parts = []
            for z in range(4):
                pieces = [incoming[chunk, half, pl.ds((2 * z + c) * 128 + r * 32, 32), :] for c in range(2)]
                high, low = split(jnp.concatenate(pieces, axis=0))
                parts.append(jnp.concatenate([high, low, high, low], axis=0))
            out = dot(three_stack[...], jnp.concatenate(parts, axis=1))
            for z in range(4):
                halfway[z, pl.ds(r, 64, stride=4), :] = out[:, z * 128 : (z + 1) * 128]

        each(0, 4, rank, unroll=4)

        def rows(block):
            at = pl.ds(pl.multiple_of(block * 128, 128), 128)
            total = jnp.zeros((128, 256), F32)
            for z in range(4):
                high, low = split(halfway[z, at, :])
                both = dot(jnp.concatenate([high, low], axis=0), wide_high[z])
                total = total + both[:128] + both[128:] + dot(high, wide_low[z])
            left = left_half((8, 128))
            for f in range(8):
                for t in range(2):
                    lower = total[f * 16 : f * 16 + 8, t * 128 : t * 128 + 128]
                    upper = total[f * 16 + 8 : f * 16 + 16, t * 128 : t * 128 + 128]
                    contracted[chunk, half, block * 8 + f, 2 * t] = jnp.where(left, lower, pltpu.roll(upper, 64, 1))
                    contracted[chunk, half, block * 8 + f, 2 * t + 1] = jnp.where(left, pltpu.roll(lower, 64, 1), upper)

        each(0, 2, rows, unroll=2)

    def advance(turn):
        @pl.when(turn < CHUNKS)
        def _():
            @pl.when(turn >= 2)
            def _():
                sent_chunk(turn - 2)

            send_chunk(turn)

        @pl.when(turn == 0)
        def _():
            exchange_factors()

        @pl.when(turn + 1 < CHUNKS)
        def _():
            load(turn + 1).wait()

            @pl.when(turn + 3 < CHUNKS)
            def _():
                load(turn + 3).start()

            mode_four(turn + 1)

        @pl.when(turn == 0)
        def _():
            widen()

        @pl.when(turn >= LAG)
        def _():
            chunk = turn - LAG

            def one_half(half):
                z_own(chunk, half).wait()
                z_all(chunk, half).wait_recv()
                modes_three_two(chunk, half)
                for d in FIBERS:
                    f_copy(chunk, half, d).start()
                f_own(chunk, half).start()

            each(0, 2, one_half)

    each(0, CHUNKS + LAG, advance)
    each(CHUNKS - 2, CHUNKS, sent_chunk)
    partial[...] = jnp.zeros_like(partial)
    each(0, EARLY, lambda chunk: each(0, 2, lambda half: f_own(chunk, half).wait()))
    f_all(0).wait_recv()
    fiber_rows = fibers.reshape(8192, 128)

    def cross(step, first, count):
        block = [fiber_rows[pl.ds(first * 16 + 2 * step + n, count, stride=16), :] for n in range(2)]
        high, low = split(jnp.concatenate(block, axis=1))
        fibers_high[step, pl.ds(first, count), :] = high
        fibers_low[step, pl.ds(first, count), :] = low
        both = dot(one_stack[:, first : first + count], high)
        return both[:64] + both[64:] + dot(one_stack[:64, first : first + count], low)

    def cross_early(step):
        crossed[step] = cross(step, 0, EARLY * 64)

    each(0, 8, cross_early, unroll=2)

    def cross_late(step):
        parts = halves(crossed[step] + cross(step, EARLY * 64, (CHUNKS - EARLY) * 64))
        back = dot_nt(parts, fibers_high[step])
        partial[...] += back[:64] + back[64:] + dot_nt(parts[:64], fibers_low[step])

    for half in range(2):
        f_own(EARLY, half).wait()
        f_all(1 + half).wait_recv()
        each(half * 4, half * 4 + 4, cross_late, unroll=4)

    def rs_copy(d):
        device, peer = plane_peer(d)
        return remote(partial.at[pl.ds(peer * 8, 8), :], scattered.at[me], rs_send, rs_recv, device)

    def ar_copy(d):
        return remote(shared.at[fib], shared.at[fib], ar_send, ar_recv, fib_peer(d)[0])

    def ag_copy(d):
        mine = state.at[pl.ds(me * 8, 8), pl.ds(0, 512)]
        return remote(mine, mine, ag_send, ag_recv, plane_peer(d)[0])

    def rs_all():
        block = scattered.at[pl.ds(0, 7)]
        return remote(block, block, rs_send, rs_recv, plane_peer(1)[0])

    def ar_all():
        block = shared.at[pl.ds(0, 15)]
        return remote(block, block, ar_send, ar_recv, fib_peer(1)[0])

    def ag_all():
        block = state.at[pl.ds(0, 56), pl.ds(0, 512)]
        return remote(block, block, ag_send, ag_recv, plane_peer(1)[0])

    for d in PLANE:
        rs_copy(d).start()
    scattered[me] = partial[pl.ds(pl.multiple_of(me * 8, 8), 8), :]
    rs_all().wait_recv()
    shared[fib] = jnp.sum(scattered[...], axis=0)
    for d in FIBERS:
        ar_copy(d).start()
    ar_all().wait_recv()
    state[pl.ds(pl.multiple_of(me * 8, 8), 8), pl.ds(0, 512)] = jnp.sum(shared[...], axis=0)
    for d in PLANE:
        ag_copy(d).start()
    ag_all().wait_recv()

    one_stack[...] = halves(state[:, :512])

    def project(n):
        p_low, middle = n // 4, n % 4
        step = (middle // 2) * 4 + p_low * 2 + middle % 2
        both = dot(one_stack[...], fibers_high[step])
        out = both[:64] + both[64:] + dot(one_stack[:64, :], fibers_low[step])
        across = jnp.concatenate([out[:, :128], out[:, 128:]], axis=0).T
        for high in range(2):
            for peer in range(8):
                start = high * 64 + peer * 8
                at = pl.ds(pl.multiple_of(middle * 16 + high * 8, 8), 8)
                core_out[peer, p_low, at, :] = across[start : start + 8, :]

    def core_copy(p_low, pair, d):
        device, peer = plane_peer(d)
        rows = pl.ds(pair * 32, 32)
        return remote(core_out.at[peer, p_low, rows, :], core_in.at[p_low, me, rows, :], core_send.at[p_low], core_recv.at[p_low], device)

    def core_all(p_low):
        block = core_in.at[p_low, pl.ds(0, 7)]
        return remote(block, block, core_send.at[p_low], core_recv.at[p_low], plane_peer(1)[0])

    for p_low in range(2):
        for pair in range(2):
            first = p_low * 4 + pair * 2
            each(first, first + 2, project, unroll=2)
            for d in PLANE:
                core_copy(p_low, pair, d).start()
        core_in[p_low, me] = core_out[me, p_low]
    ag_all().wait_send()
    lanes = lax.broadcasted_iota(jnp.int32, (64, 128), 1)
    state[:, 512:] = jnp.where(lanes == lax.broadcasted_iota(jnp.int32, (64, 128), 0), 1.0, 0.0)

    def cholesky_qr(repeat):
        rows = state[:, :512]
        crossed = lax.dot_general(rows, rows, (((1,), (1,)), ((), ())), precision=HIGHEST, preferred_element_type=F32)
        state[...] = jnp.dot(eliminate(crossed), state[...], precision=HIGHEST, preferred_element_type=F32)

    each(0, 2, cholesky_qr)
    rows = state[:, :512]
    high = rows.astype(BF16)
    rest = rows - high.astype(F32)
    middle, low = split(rest)
    moved = dot(jnp.concatenate([high, middle, low], axis=0), order[...])
    updated[...] = moved[:64] + (moved[64:128] + moved[128:])
    inverse[...] = state[:, 512:]

    def out_copy(p_low):
        return pltpu.make_async_copy(core_in.at[p_low], received.at[p_low], out_sem.at[p_low])

    for p_low in range(2):
        core_all(p_low).wait_recv()
        out_copy(p_low).start()

    core_all(0).wait_send()
    core_all(1).wait_send()
    rs_all().wait_send()
    ar_all().wait_send()
    two_arrived().wait_send()
    three_copy().wait_send()
    f_all(0).wait_send()
    f_all(1).wait_send()
    f_all(2).wait_send()
    out_copy(0).wait()
    out_copy(1).wait()


def finish_kernel(received, inverse, rows, updated, core, high, low):
    step = pl.program_id(0)

    @pl.when(step == 0)
    def _():
        updated[...] = rows[...]
        flat = received.reshape(1024, 128)
        for n in range(32):
            p, q = n // 8, n % 8
            part = flat[pl.ds((p % 2) * 512 + (p // 2) * 8 + q, 32, stride=16), :]
            high[pl.ds(n * 32, 32), :], low[pl.ds(n * 32, 32), :] = split(part)

    own = inverse[pl.ds(pl.multiple_of(step * 32, 32), 32), :]
    weights = halves(jnp.concatenate([own, pltpu.roll(own, 64, 1)], axis=0))
    both = dot_nt(weights, high[...])
    out = both[:64] + both[64:] + dot_nt(weights[:64], low[...])
    lanes = lax.broadcasted_iota(jnp.int32, (32, 128), 1)
    for n in range(32):
        p, q = n // 8, n % 8
        tile, off = n // 4, (n % 4) * 32
        lower = out[:32, tile * 128 : tile * 128 + 128]
        upper = out[32:, tile * 128 : tile * 128 + 128]
        if off:
            lower = pltpu.roll(lower, 128 - off, 1)
        if off != 32:
            upper = pltpu.roll(upper, (160 - off) % 128, 1)
        core[pl.ds(q * 4 + p, 32, stride=32), :] = jnp.where(lanes < 32, lower, upper)


def body(tensor, factor_one, factor_two, factor_three, factor_four):
    vmem = pl.BlockSpec(memory_space=pltpu.VMEM)
    hbm = pl.BlockSpec(memory_space=pl.ANY)
    dma = pltpu.SemaphoreType.DMA
    rows, inverse, received = pl.pallas_call(
        kernel,
        out_shape=(
            jax.ShapeDtypeStruct((64, 512), F32),
            jax.ShapeDtypeStruct((64, 128), F32),
            jax.ShapeDtypeStruct((2, 8, 64, 128), F32),
        ),
        in_specs=[hbm] * 5,
        out_specs=(vmem, vmem, hbm),
        scratch_shapes=[
            pltpu.VMEM((64, 128), F32),
            pltpu.VMEM((32, 64), F32),
            pltpu.VMEM((32, 64), F32),
            pltpu.VMEM((64, 512), F32),
            pltpu.VMEM((64, 128), F32),
            pltpu.VMEM((128, 256), BF16),
            pltpu.VMEM((128, 512), BF16),
            pltpu.VMEM((64, 256), F32),
            pltpu.VMEM((32, 128), F32),
            pltpu.VMEM((3, 4096, 128), F32),
            pltpu.VMEM((CHUNKS, 2048, 128), F32),
            pltpu.VMEM((CHUNKS, 2, 1024, 128), F32),
            pltpu.VMEM((4, 256, 128), F32),
            pltpu.VMEM((CHUNKS, 2, 16, 4, 8, 128), F32),
            pltpu.VMEM((CHUNKS, 16, 4, 2, 8, 128), F32),
            pltpu.VMEM((4, 32, 128), F32),
            pltpu.VMEM((2, 64, 256), F32),
            pltpu.VMEM((64, 256), BF16),
            pltpu.VMEM((4, 128, 256), BF16),
            pltpu.VMEM((4, 128, 256), BF16),
            pltpu.VMEM((8, 512, 256), BF16),
            pltpu.VMEM((8, 512, 256), BF16),
            pltpu.VMEM((512, 512), BF16),
            pltpu.VMEM((8, 64, 256), F32),
            pltpu.VMEM((64, 512), F32),
            pltpu.VMEM((8, 8, 512), F32),
            pltpu.VMEM((16, 8, 512), F32),
            pltpu.VMEM((64, 640), F32),
            pltpu.VMEM((8, 2, 64, 128), F32),
            pltpu.VMEM((2, 8, 64, 128), F32),
            dma((3,)), dma((4,)), dma((CHUNKS, 2)), dma((CHUNKS, 2)), dma((CHUNKS, 2)), dma((CHUNKS, 2)), dma((3,)), dma((3,)),
            dma(()), dma(()), dma(()), dma(()), dma(()), dma(()), dma(()), dma(()), dma(()), dma(()), dma((2,)), dma((2,)), dma((2,)),
        ],
        compiler_params=pltpu.CompilerParams(collective_id=0, has_side_effects=True, vmem_limit_bytes=56 * 2**20),
        name="hooi",
    )(tensor.reshape(8, 4096, 128), factor_four.T, factor_three, factor_two, factor_one.T)
    whole = lambda *shape: pl.BlockSpec(shape, lambda step: (0,) * len(shape))
    updated, core = pl.pallas_call(
        finish_kernel,
        grid=(2,),
        out_shape=(jax.ShapeDtypeStruct((64, 512), F32), jax.ShapeDtypeStruct((2048, 128), F32)),
        in_specs=[whole(2, 8, 64, 128), whole(64, 128), whole(64, 512)],
        out_specs=(whole(64, 512), pl.BlockSpec((1024, 128), lambda step: (step, 0))),
        scratch_shapes=[pltpu.VMEM((1024, 128), BF16), pltpu.VMEM((1024, 128), BF16)],
        compiler_params=pltpu.CompilerParams(vmem_limit_bytes=62 * 2**20),
        name="finish",
    )(received, inverse, rows)
    return (updated.T, core[:, :64].reshape(64, 8, 4, 64))


def solution(mesh):
    in_specs = (P("fib", "row", "slab", None), P(), P("row", None), P("slab", None), P())
    out_specs = (P(), P(None, ("row", "slab"), "fib", None))
    return jax.shard_map(body, mesh=mesh, in_specs=in_specs, out_specs=out_specs, check_vma=False)
```

```python
import jax
import jax.numpy as jnp
from jax import lax
from jax.experimental import pallas as pl
from jax.experimental.pallas import tpu as pltpu
from jax.sharding import PartitionSpec as P

HIGHEST = lax.Precision.HIGHEST
MESH = pl.DeviceIdType.MESH
F32 = jnp.float32
BF16 = jnp.bfloat16
CHUNKS = 8
LAG = 2
EARLY = CHUNKS - 1
PLANE = (4, 2, 6, 5, 3, 7, 1)
FIBERS = tuple(sorted(range(1, 16), key=lambda d: -(min(d // 4, 4 - d // 4) + min(d % 4, 4 - d % 4))))


def split(x):
    high = x.astype(BF16)
    return high, (x - high.astype(F32)).astype(BF16)


def dot(a, b):
    return jnp.dot(a, b, preferred_element_type=F32)


def dot_nt(a, b):
    return lax.dot_general(a, b, (((1,), (1,)), ((), ())), preferred_element_type=F32)


def place():
    return lax.axis_index("fib"), lax.axis_index("row"), lax.axis_index("slab")


def plane_peer(d):
    fib, row, slab = place()
    row, slab = lax.rem(row + d // 2, 4), lax.rem(slab + d % 2, 2)
    return (fib, row, slab), row * 2 + slab


def fib_peer(d):
    fib, row, slab = place()
    fib = lax.rem(fib // 4 + d // 4, 4) * 4 + lax.rem(fib % 4 + d % 4, 4)
    return (fib, row, slab), fib


def each(lower, upper, step, unroll=1):
    def run(index, carry):
        step(index)
        return carry

    lax.fori_loop(lower, upper, run, 0, unroll=unroll)


def remote(src, dst, send, recv, device):
    return pltpu.make_async_remote_copy(
        src_ref=src, dst_ref=dst, send_sem=send, recv_sem=recv, device_id=device, device_id_type=MESH
    )


def greet():
    barrier = pltpu.get_barrier_semaphore()
    for d in PLANE:
        pl.semaphore_signal(barrier, inc=1, device_id=plane_peer(d)[0], device_id_type=MESH)
    for d in FIBERS:
        pl.semaphore_signal(barrier, inc=1, device_id=fib_peer(d)[0], device_id_type=MESH)


def stack(x):
    high, low = split(x)
    return jnp.concatenate([jnp.concatenate([high, high], 1), jnp.concatenate([low, low], 1)], 0)


def left_half(shape):
    return lax.broadcasted_iota(jnp.int32, shape, 1) < 64


def halves(x):
    return jnp.concatenate(split(x), axis=0)


def eliminate(crossed, group=8):
    lane = lax.broadcasted_iota(jnp.int32, (8, 64), 1)
    row = lax.broadcasted_iota(jnp.int32, (8, 64), 0)
    below = lax.broadcasted_iota(jnp.int32, (8, 128), 0)
    blocks = [
        jnp.concatenate([crossed[8 * b : 8 * b + 8], jnp.where(lane == row + 8 * b, 1.0, 0.0)], axis=1) for b in range(8)
    ]

    def spread(x):
        return jnp.broadcast_to(x, (8, 128))

    for first in range(0, 64, group):
        b, k = first // 8, first % 8
        here = blocks[b]
        corner = [[spread(here[k + m : k + m + 1, first + n : first + n + 1]) for n in range(m + 1)] for m in range(group)]
        below_diagonal = [[None] * group for m in range(group)]
        scale = [None] * group
        for m in range(group):
            square = corner[m][m]
            for n in range(m):
                square = square - below_diagonal[m][n] * below_diagonal[m][n]
            scale[m] = lax.rsqrt(square)
            for other in range(m + 1, group):
                entry = corner[other][m]
                for n in range(m):
                    entry = entry - below_diagonal[other][n] * below_diagonal[m][n]
                below_diagonal[other][m] = entry * scale[m]

        def forward(parts):
            done = []
            for m in range(group):
                part = parts[m]
                for n in range(m):
                    part = part - done[n] * below_diagonal[m][n]
                done.append(part * scale[m])
            return done

        pivots = forward([spread(here[k + m : k + m + 1, :]) for m in range(group)])
        for at in range(b, 8):
            if at == b and k + group == 8:
                update = here
            else:
                columns = forward([spread(blocks[at][:, first + m : first + m + 1]) for m in range(group)])
                update = blocks[at]
                for m in range(group):
                    update = update - columns[m] * pivots[m]
            if at == b:
                update = jnp.where(below < k, here, update)
                for m in range(group):
                    update = jnp.where(below == k + m, pivots[m], update)
            blocks[at] = update
    return jnp.concatenate(blocks, axis=0)[:, 64:]


def kernel(
    tensor, four_hbm, three_hbm, two_hbm, one_hbm, updated, inverse, received,
    four, three, two, one, dealt, four_stack, one_stack, three_own_block, two_own_block,
    staged, outgoing, incoming, halfway, contracted, fibers, two_all, three_all, three_stack, wide_high, wide_low,
    fibers_high, fibers_low, order, crossed, partial, scattered, shared, state, core_out, core_in,
    load_sem, factor_sem, own_sem, z_send, z_recv, fib_own_sem, f_send, f_recv,
    two_send, two_recv, three_send, three_recv, rs_send, rs_recv, ar_send, ar_recv, ag_send, ag_recv, core_send, core_recv, out_sem,
):
    fib, row, slab = place()
    me = row * 2 + slab

    def load(chunk):
        return pltpu.make_async_copy(tensor.at[chunk], staged.at[chunk % 3], load_sem.at[chunk % 3])

    def mode_four(chunk):
        slot = chunk % 3

        def two_steps(pair):
            first = staged[slot, pl.ds(2 * pair, 128, stride=32), :]
            second = staged[slot, pl.ds(2 * pair + 1, 128, stride=32), :]
            high, low = split(jnp.concatenate([first, second], axis=0))
            out = dot_nt(four_stack[...], jnp.concatenate([high, low], axis=1))
            out = out[:64] + out[64:]
            outgoing[chunk, pl.ds(2 * pair, 64, stride=32), :] = out[:, :128]
            outgoing[chunk, pl.ds(2 * pair + 1, 64, stride=32), :] = out[:, 128:]

        each(0, 16, two_steps, unroll=4)

    def fetch(n):
        source, target = ((four_hbm, four), (three_hbm, three), (two_hbm, two), (one_hbm, one))[n]
        return pltpu.make_async_copy(source, target, factor_sem.at[n])

    fetch(0).start()
    load(0).start()
    load(1).start()
    for n in range(1, 4):
        fetch(n).start()
    greet()
    fetch(0).wait()
    across = four[...]
    dealt[pl.ds(0, 32, stride=2), :] = across[:32]
    dealt[pl.ds(1, 32, stride=2), :] = across[32:]
    four_stack[...] = stack(dealt[...])
    load(0).wait()
    load(2).start()
    mode_four(0)
    pl.semaphore_wait(pltpu.get_barrier_semaphore(), len(PLANE) + len(FIBERS))

    def z_copy(chunk, half, d):
        device, peer = plane_peer(d)
        return remote(
            outgoing.at[chunk, pl.ds(peer * 256 + half * 128, 128), :],
            incoming.at[chunk, half, pl.ds(me * 128, 128), :],
            z_send.at[chunk, half], z_recv.at[chunk, half], device,
        )

    def z_all(chunk, half):
        block = incoming.at[chunk, half, pl.ds(0, 7 * 128), :]
        return remote(block, block, z_send.at[chunk, half], z_recv.at[chunk, half], plane_peer(1)[0])

    def z_own(chunk, half):
        return pltpu.make_async_copy(
            outgoing.at[chunk, pl.ds(me * 256 + half * 128, 128), :],
            incoming.at[chunk, half, pl.ds(me * 128, 128), :],
            own_sem.at[chunk, half],
        )

    def send_chunk(chunk):
        for half in range(2):
            for d in PLANE:
                z_copy(chunk, half, d).start()
            z_own(chunk, half).start()

    def sent_chunk(chunk):
        for half in range(2):
            z_all(chunk, half).wait_send()

    def f_rows(chunk, half, device):
        return fibers.at[chunk, device, :, half]

    def f_copy(chunk, half, d):
        device, peer = fib_peer(d)
        stage = (chunk // EARLY) * (1 + half)
        return remote(contracted.at[chunk, half, peer], f_rows(chunk, half, fib), f_send.at[stage], f_recv.at[stage], device)

    def f_all(stage):
        block = fibers.at[pl.ds(0, EARLY), pl.ds(0, 15)] if stage == 0 else fibers.at[EARLY, pl.ds(0, 15), :, stage - 1]
        return remote(block, block, f_send.at[stage], f_recv.at[stage], fib_peer(1)[0])

    def f_own(chunk, half):
        return pltpu.make_async_copy(contracted.at[chunk, half, fib], f_rows(chunk, half, fib), fib_own_sem.at[chunk, half])

    def two_copy(step):
        return remote(two_own_block, two_all.at[row], two_send, two_recv, (fib, lax.rem(row + step, 4), slab))

    def two_arrived():
        block = two_all.at[pl.ds(0, 3)]
        return remote(block, block, two_send, two_recv, (fib, lax.rem(row + 1, 4), slab))

    def three_copy():
        return remote(three_own_block, three_all.at[slab], three_send, three_recv, (fib, row, 1 - slab))

    def exchange_factors():
        fetch(1).wait()
        fetch(2).wait()
        two_own_block[...] = jnp.concatenate([two[...], two[...]], axis=1)
        across = three[...].T
        nothing = jnp.zeros_like(across)
        mine = jnp.where(slab == 0, 1.0, 0.0)
        block = jnp.concatenate([across * mine, across * (1.0 - mine)], axis=1)
        three_own_block[...] = jnp.concatenate([block] * 4, axis=1)
        for step in range(1, 4):
            two_copy(step).start()
        three_copy().start()
        two_all[row] = two_own_block[...]
        three_all[slab] = three_own_block[...]

    def widen():
        two_arrived().wait_recv()
        three_copy().wait_recv()
        high, low = split(three_all[0] + three_all[1])
        lanes = lax.broadcasted_iota(jnp.int32, (64, 256), 1)
        three_stack[...] = jnp.where(lanes < 128, high.astype(F32), low.astype(F32)).astype(BF16)
        left = left_half((32, 128))
        nothing = jnp.zeros((32, 128), F32)
        for z in range(4):
            block = two_all[z]
            sides = (jnp.where(left, block, 0.0), jnp.where(left, 0.0, block))
            pieces = []
            for i in range(4):
                tiles = [nothing, nothing]
                tiles[i // 2] = sides[i % 2]
                pieces.append(jnp.concatenate(tiles, axis=1))
            high, low = split(jnp.concatenate(pieces, axis=0))
            wide_high[z] = high
            wide_low[z] = low
        fetch(3).wait()
        natural = lax.broadcasted_iota(jnp.int32, (512, 512), 1)
        there = ((natural >> 2) & 7) * 64 + (natural >> 5) * 4 + (natural & 3)
        same = there == lax.broadcasted_iota(jnp.int32, (512, 512), 0)
        order[...] = jnp.where(same, 1.0, 0.0).astype(BF16)
        one_stack[...] = dot_nt(halves(one[...]), order[...]).astype(BF16)

    def modes_three_two(chunk, half):
        def rank(r):
            parts = []
            for z in range(4):
                pieces = [incoming[chunk, half, pl.ds((2 * z + c) * 128 + r * 32, 32), :] for c in range(2)]
                high, low = split(jnp.concatenate(pieces, axis=0))
                parts.append(jnp.concatenate([high, low, high, low], axis=0))
            out = dot(three_stack[...], jnp.concatenate(parts, axis=1))
            for z in range(4):
                halfway[z, pl.ds(r, 64, stride=4), :] = out[:, z * 128 : (z + 1) * 128]

        each(0, 4, rank, unroll=4)

        def rows(block):
            at = pl.ds(pl.multiple_of(block * 128, 128), 128)
            total = jnp.zeros((128, 256), F32)
            for z in range(4):
                high, low = split(halfway[z, at, :])
                both = dot(jnp.concatenate([high, low], axis=0), wide_high[z])
                total = total + both[:128] + both[128:] + dot(high, wide_low[z])
            left = left_half((8, 128))
            for f in range(8):
                for t in range(2):
                    lower = total[f * 16 : f * 16 + 8, t * 128 : t * 128 + 128]
                    upper = total[f * 16 + 8 : f * 16 + 16, t * 128 : t * 128 + 128]
                    contracted[chunk, half, block * 8 + f, 2 * t] = jnp.where(left, lower, pltpu.roll(upper, 64, 1))
                    contracted[chunk, half, block * 8 + f, 2 * t + 1] = jnp.where(left, pltpu.roll(lower, 64, 1), upper)

        each(0, 2, rows, unroll=2)

    def advance(turn):
        @pl.when(turn < CHUNKS)
        def _():
            @pl.when(turn >= 2)
            def _():
                sent_chunk(turn - 2)

            send_chunk(turn)

        @pl.when(turn == 0)
        def _():
            exchange_factors()

        @pl.when(turn + 1 < CHUNKS)
        def _():
            load(turn + 1).wait()

            @pl.when(turn + 3 < CHUNKS)
            def _():
                load(turn + 3).start()

            mode_four(turn + 1)

        @pl.when(turn == 0)
        def _():
            widen()

        @pl.when(turn >= LAG)
        def _():
            chunk = turn - LAG

            def one_half(half):
                z_own(chunk, half).wait()
                z_all(chunk, half).wait_recv()
                modes_three_two(chunk, half)
                for d in FIBERS:
                    f_copy(chunk, half, d).start()
                f_own(chunk, half).start()

            each(0, 2, one_half)

    each(0, CHUNKS + LAG, advance)
    each(CHUNKS - 2, CHUNKS, sent_chunk)
    partial[...] = jnp.zeros_like(partial)
    each(0, EARLY, lambda chunk: each(0, 2, lambda half: f_own(chunk, half).wait()))
    f_all(0).wait_recv()
    fiber_rows = fibers.reshape(8192, 128)

    def cross(step, first, count):
        block = [fiber_rows[pl.ds(first * 16 + 2 * step + n, count, stride=16), :] for n in range(2)]
        high, low = split(jnp.concatenate(block, axis=1))
        fibers_high[step, pl.ds(first, count), :] = high
        fibers_low[step, pl.ds(first, count), :] = low
        both = dot(one_stack[:, first : first + count], high)
        return both[:64] + both[64:] + dot(one_stack[:64, first : first + count], low)

    def cross_early(step):
        crossed[step] = cross(step, 0, EARLY * 64)

    each(0, 8, cross_early, unroll=2)

    def cross_late(step):
        parts = halves(crossed[step] + cross(step, EARLY * 64, (CHUNKS - EARLY) * 64))
        back = dot_nt(parts, fibers_high[step])
        partial[...] += back[:64] + back[64:] + dot_nt(parts[:64], fibers_low[step])

    for half in range(2):
        f_own(EARLY, half).wait()
        f_all(1 + half).wait_recv()
        each(half * 4, half * 4 + 4, cross_late, unroll=4)

    def rs_copy(d):
        device, peer = plane_peer(d)
        return remote(partial.at[pl.ds(peer * 8, 8), :], scattered.at[me], rs_send, rs_recv, device)

    def ar_copy(d):
        return remote(shared.at[fib], shared.at[fib], ar_send, ar_recv, fib_peer(d)[0])

    def ag_copy(d):
        mine = state.at[pl.ds(me * 8, 8), pl.ds(0, 512)]
        return remote(mine, mine, ag_send, ag_recv, plane_peer(d)[0])

    def rs_all():
        block = scattered.at[pl.ds(0, 7)]
        return remote(block, block, rs_send, rs_recv, plane_peer(1)[0])

    def ar_all():
        block = shared.at[pl.ds(0, 15)]
        return remote(block, block, ar_send, ar_recv, fib_peer(1)[0])

    def ag_all():
        block = state.at[pl.ds(0, 56), pl.ds(0, 512)]
        return remote(block, block, ag_send, ag_recv, plane_peer(1)[0])

    for d in PLANE:
        rs_copy(d).start()
    scattered[me] = partial[pl.ds(pl.multiple_of(me * 8, 8), 8), :]
    rs_all().wait_recv()
    shared[fib] = jnp.sum(scattered[...], axis=0)
    for d in FIBERS:
        ar_copy(d).start()
    ar_all().wait_recv()
    state[pl.ds(pl.multiple_of(me * 8, 8), 8), pl.ds(0, 512)] = jnp.sum(shared[...], axis=0)
    for d in PLANE:
        ag_copy(d).start()
    ag_all().wait_recv()

    one_stack[...] = halves(state[:, :512])

    def project(n):
        p_low, middle = n // 4, n % 4
        step = (middle // 2) * 4 + p_low * 2 + middle % 2
        both = dot(one_stack[...], fibers_high[step])
        out = both[:64] + both[64:] + dot(one_stack[:64, :], fibers_low[step])
        across = jnp.concatenate([out[:, :128], out[:, 128:]], axis=0).T
        for high in range(2):
            for peer in range(8):
                start = high * 64 + peer * 8
                at = pl.ds(pl.multiple_of(middle * 16 + high * 8, 8), 8)
                core_out[peer, p_low, at, :] = across[start : start + 8, :]

    def core_copy(p_low, pair, d):
        device, peer = plane_peer(d)
        rows = pl.ds(pair * 32, 32)
        return remote(core_out.at[peer, p_low, rows, :], core_in.at[p_low, me, rows, :], core_send.at[p_low], core_recv.at[p_low], device)

    def core_all(p_low):
        block = core_in.at[p_low, pl.ds(0, 7)]
        return remote(block, block, core_send.at[p_low], core_recv.at[p_low], plane_peer(1)[0])

    for p_low in range(2):
        for pair in range(2):
            first = p_low * 4 + pair * 2
            each(first, first + 2, project, unroll=2)
            for d in PLANE:
                core_copy(p_low, pair, d).start()
        core_in[p_low, me] = core_out[me, p_low]
    ag_all().wait_send()
    lanes = lax.broadcasted_iota(jnp.int32, (64, 128), 1)
    state[:, 512:] = jnp.where(lanes == lax.broadcasted_iota(jnp.int32, (64, 128), 0), 1.0, 0.0)

    def cholesky_qr(repeat):
        rows = state[:, :512]
        crossed = lax.dot_general(rows, rows, (((1,), (1,)), ((), ())), precision=HIGHEST, preferred_element_type=F32)
        state[...] = jnp.dot(eliminate(crossed), state[...], precision=HIGHEST, preferred_element_type=F32)

    each(0, 2, cholesky_qr)
    rows = state[:, :512]
    high = rows.astype(BF16)
    rest = rows - high.astype(F32)
    middle, low = split(rest)
    moved = dot(jnp.concatenate([high, middle, low], axis=0), order[...])
    updated[...] = moved[:64] + (moved[64:128] + moved[128:])
    inverse[...] = state[:, 512:]

    def out_copy(p_low):
        return pltpu.make_async_copy(core_in.at[p_low], received.at[p_low], out_sem.at[p_low])

    for p_low in range(2):
        core_all(p_low).wait_recv()
        out_copy(p_low).start()

    core_all(0).wait_send()
    core_all(1).wait_send()
    rs_all().wait_send()
    ar_all().wait_send()
    two_arrived().wait_send()
    three_copy().wait_send()
    f_all(0).wait_send()
    f_all(1).wait_send()
    f_all(2).wait_send()
    out_copy(0).wait()
    out_copy(1).wait()


def finish_kernel(received, inverse, rows, updated, core, high, low):
    step = pl.program_id(0)

    @pl.when(step == 0)
    def _():
        updated[...] = rows[...]
        flat = received.reshape(1024, 128)
        for n in range(32):
            p, q = n // 8, n % 8
            part = flat[pl.ds((p % 2) * 512 + (p // 2) * 8 + q, 32, stride=16), :]
            high[pl.ds(n * 32, 32), :], low[pl.ds(n * 32, 32), :] = split(part)

    own = inverse[pl.ds(pl.multiple_of(step * 32, 32), 32), :]
    weights = halves(jnp.concatenate([own, pltpu.roll(own, 64, 1)], axis=0))
    both = dot_nt(weights, high[...])
    out = both[:64] + both[64:] + dot_nt(weights[:64], low[...])
    lanes = lax.broadcasted_iota(jnp.int32, (32, 128), 1)
    for n in range(32):
        p, q = n // 8, n % 8
        tile, off = n // 4, (n % 4) * 32
        lower = out[:32, tile * 128 : tile * 128 + 128]
        upper = out[32:, tile * 128 : tile * 128 + 128]
        if off:
            lower = pltpu.roll(lower, 128 - off, 1)
        if off != 32:
            upper = pltpu.roll(upper, (160 - off) % 128, 1)
        core[pl.ds(q * 4 + p, 32, stride=32), :] = jnp.where(lanes < 32, lower, upper)


def body(tensor, factor_one, factor_two, factor_three, factor_four):
    vmem = pl.BlockSpec(memory_space=pltpu.VMEM)
    hbm = pl.BlockSpec(memory_space=pl.ANY)
    dma = pltpu.SemaphoreType.DMA
    rows, inverse, received = pl.pallas_call(
        kernel,
        out_shape=(
            jax.ShapeDtypeStruct((64, 512), F32),
            jax.ShapeDtypeStruct((64, 128), F32),
            jax.ShapeDtypeStruct((2, 8, 64, 128), F32),
        ),
        in_specs=[hbm] * 5,
        out_specs=(vmem, vmem, hbm),
        scratch_shapes=[
            pltpu.VMEM((64, 128), F32),
            pltpu.VMEM((32, 64), F32),
            pltpu.VMEM((32, 64), F32),
            pltpu.VMEM((64, 512), F32),
            pltpu.VMEM((64, 128), F32),
            pltpu.VMEM((128, 256), BF16),
            pltpu.VMEM((128, 512), BF16),
            pltpu.VMEM((64, 256), F32),
            pltpu.VMEM((32, 128), F32),
            pltpu.VMEM((3, 4096, 128), F32),
            pltpu.VMEM((CHUNKS, 2048, 128), F32),
            pltpu.VMEM((CHUNKS, 2, 1024, 128), F32),
            pltpu.VMEM((4, 256, 128), F32),
            pltpu.VMEM((CHUNKS, 2, 16, 4, 8, 128), F32),
            pltpu.VMEM((CHUNKS, 16, 4, 2, 8, 128), F32),
            pltpu.VMEM((4, 32, 128), F32),
            pltpu.VMEM((2, 64, 256), F32),
            pltpu.VMEM((64, 256), BF16),
            pltpu.VMEM((4, 128, 256), BF16),
            pltpu.VMEM((4, 128, 256), BF16),
            pltpu.VMEM((8, 512, 256), BF16),
            pltpu.VMEM((8, 512, 256), BF16),
            pltpu.VMEM((512, 512), BF16),
            pltpu.VMEM((8, 64, 256), F32),
            pltpu.VMEM((64, 512), F32),
            pltpu.VMEM((8, 8, 512), F32),
            pltpu.VMEM((16, 8, 512), F32),
            pltpu.VMEM((64, 640), F32),
            pltpu.VMEM((8, 2, 64, 128), F32),
            pltpu.VMEM((2, 8, 64, 128), F32),
            dma((3,)), dma((4,)), dma((CHUNKS, 2)), dma((CHUNKS, 2)), dma((CHUNKS, 2)), dma((CHUNKS, 2)), dma((3,)), dma((3,)),
            dma(()), dma(()), dma(()), dma(()), dma(()), dma(()), dma(()), dma(()), dma(()), dma(()), dma((2,)), dma((2,)), dma((2,)),
        ],
        compiler_params=pltpu.CompilerParams(collective_id=0, has_side_effects=True, vmem_limit_bytes=56 * 2**20),
        name="hooi",
    )(tensor.reshape(8, 4096, 128), factor_four.T, factor_three, factor_two, factor_one.T)
    whole = lambda *shape: pl.BlockSpec(shape, lambda step: (0,) * len(shape))
    updated, core = pl.pallas_call(
        finish_kernel,
        grid=(2,),
        out_shape=(jax.ShapeDtypeStruct((64, 512), F32), jax.ShapeDtypeStruct((2048, 128), F32)),
        in_specs=[whole(2, 8, 64, 128), whole(64, 128), whole(64, 512)],
        out_specs=(whole(64, 512), pl.BlockSpec((1024, 128), lambda step: (step, 0))),
        scratch_shapes=[pltpu.VMEM((1024, 128), BF16), pltpu.VMEM((1024, 128), BF16)],
        compiler_params=pltpu.CompilerParams(vmem_limit_bytes=62 * 2**20),
        name="finish",
    )(received, inverse, rows)
    return (updated.T, core[:, :64].reshape(64, 8, 4, 64))


def solution(mesh):
    in_specs = (P("fib", "row", "slab", None), P(), P("row", None), P("slab", None), P())
    out_specs = (P(), P(None, ("row", "slab"), "fib", None))
    return jax.shard_map(body, mesh=mesh, in_specs=in_specs, out_specs=out_specs, check_vma=False)
```
